32 devices in a mesh: pa: 4 (over x, core), pb: 8 (over z, y).
Axes of the slice: x: 2, y: 2, z: 4, core: 2. Of those that a mesh axis runs over, the one named last changes fastest.
Arguments:
- queries: bfloat16 [1024, 768], replicated, may hold values from -500 to 500, as said below
- passages: bfloat16 [16384, 768], P(('pa', 'pb')), may hold values from -32 to 32
- noise: bfloat16 [1024, 16384], P(None, ('pa', 'pb')), may hold values from 0.0099487305 to 0.98828125
- mix_weight: bfloat16 [768, 1024], replicated, may hold values from -0.046875 to 0.046875
- answer_queries: bfloat16 [1024, 1024], P('pb'), may hold values from -150 to 150, as said below
- key_weight: bfloat16 [1024, 1024], replicated, may hold values from -1 to 1
- value_weight: bfloat16 [1024, 1024], replicated, may hold values from -0.1875 to 0.1875
- token_states: bfloat16 [256, 256, 1024], P(('pa', 'pb')), may hold values from -6 to 6, as said below
- block_owner: int32 [256], replicated, may hold values from 0 to 255, as said below
- listed: int32 [8, 64], P('pb', 'pa'), may hold values from 0 to 255, as said below
Outputs:
- attended: bfloat16 [1024, 1024], P('pb', 'pa')
The draws below stay inside these ranges and needn't reach their ends.
Inputs may be any that keep to these rules, and one draw needn't show every extreme that they name: A permutation: block b lies in slot block_owner[b]; slots run through the devices in pa+pb order, 8 to a device, and the holding device's shelf is slot // 8. Entries p * 16 to (p + 1) * 16 - 1 of row g name blocks whose slots lie on devices with pa index p; they come in groups of exactly 2 from 8 different devices. No block appears twice in a row; a block may appear in several rows, and some devices hold blocks listed by many rows. `queries`: embedding values. `answer_queries`: query values. `token_states`: state values.
All inputs are finite; a program needn't handle non-finite values.
Results may differ from the reference program's by a relative error of at most 0.012.
The reference program's roundings to bfloat16 on the way (of `weights`, `blended_half`, `conditioned`, `key_rows`, `value_rows` and `probs`) count: a program that leaves them out, or rounds other values in their place, can miss the bound.
Values may be sent and summed in bfloat16 or wider, within the bound.
No kernel may reach another device: no remote copies, remote signals or barrier semaphores. Data moves between devices by JAX's collectives and lax.ppermute only.
A program may use at most 192 MiB of HBM per device.

```python
import jax
import jax.numpy as jnp
from jax import lax

DQ = 768
DM = 1024
HEADS = 16
HEAD_DIM = 64
ROWS = 128
SEQ = 256
BLK_DEV = 8
LIST_DEV = 16
CAP = 2
PDEV = 512
NP = 16384
NQ = 1024
KL = 64
NB = 256
N_PA = 4
N_PB = 8


def folded(key, number):
    return jax.random.fold_in(key, number)


def passage_base(key, members):
    anchor = folded(key, 11)
    values = jax.vmap(lambda member: jax.random.normal(folded(anchor, member), (DQ,), jnp.float32))(members)
    return jnp.clip(values, -5.0, 5.0)


def passage_rows(key, members):
    values = passage_base(key, members)
    return values


def draw_passages(key, part):
    values = passage_rows(key, jnp.arange(NP, dtype=jnp.int32))
    return values.astype(jnp.bfloat16)


def draw_queries(key, part):
    values = jnp.clip(jax.random.normal(folded(key, 21), (NQ, DQ), jnp.float32), -5.0, 5.0)
    return values.astype(jnp.bfloat16)


def block_states(key, members):
    anchor = folded(key, 31)
    values = jax.vmap(lambda member: jax.random.normal(folded(anchor, member), (SEQ, DM), jnp.float32))(members)
    values = jnp.clip(values, -5.0, 5.0)
    return values


def key_matrix(key):
    values = jnp.clip(jax.random.normal(folded(key, 41), (DM, DM), jnp.float32), -5.0, 5.0)
    return values * DM ** (-0.5)


def layout(key):
    owner_of = jax.random.permutation(folded(key, 51), NB).astype(jnp.int32)
    block_at = jnp.argsort(owner_of).astype(jnp.int32)
    owner_count = LIST_DEV // CAP
    devices = jnp.arange(N_PB, dtype=jnp.int32)
    popular = jax.random.randint(folded(key, 52), (N_PA, 2), 0, N_PB)
    popular_mask = (devices[None, :] == popular[:, 0:1]) | (devices[None, :] == popular[:, 1:2])
    chance = jax.random.randint(folded(key, 53), (N_PB, N_PA, N_PB), 0, 4) < 3
    jitter = jax.random.randint(folded(key, 54), (N_PB, N_PA, N_PB), 0, 1024)
    ranking = (jitter + 2048 * (popular_mask[None] & chance).astype(jnp.int32)) * N_PB + devices
    _, owners = lax.top_k(ranking, owner_count)
    slot_rank = jax.random.randint(folded(key, 55), (N_PB, N_PA, owner_count, BLK_DEV), 0, 1024) * BLK_DEV
    slot_rank = slot_rank + jnp.arange(BLK_DEV, dtype=jnp.int32)
    local_slots = jnp.argsort(slot_rank, -1)[..., :CAP].astype(jnp.int32)
    row_index = jnp.arange(N_PA, dtype=jnp.int32)[None, :, None, None]
    slot_ids = (row_index * N_PB + owners[..., None]) * BLK_DEV + local_slots
    blocks = block_at[slot_ids].reshape(N_PB, N_PA, LIST_DEV)
    shuffle = jax.random.randint(folded(key, 56), (N_PB, N_PA, LIST_DEV), 0, 1024) * LIST_DEV
    shuffle = jnp.argsort(shuffle + jnp.arange(LIST_DEV, dtype=jnp.int32), -1)
    blocks = jnp.take_along_axis(blocks, shuffle, -1)
    return (owner_of, blocks.reshape(N_PB, N_PA * LIST_DEV).astype(jnp.int32))


def draw_block_owner(key, part):
    owner_of, listing = layout(key)
    return owner_of


def draw_listed(key, part):
    owner_of, listing = layout(key)
    return listing


def draw_token_states(key, part):
    return block_states(key, jnp.arange(NB, dtype=jnp.int32)).astype(jnp.bfloat16)


def draw_key_weight(key, part):
    return key_matrix(key).astype(jnp.bfloat16)


def draw_answer_queries(key, part):
    values = 0.2 * jnp.clip(jax.random.normal(folded(key, 61), (NQ, DM), jnp.float32), -5.0, 5.0)
    return values.astype(jnp.bfloat16)


def block_scale(own_key, shape, cuts, low, largest):
    def one(axis_at, blocks):
        draws = jax.random.uniform(jax.random.fold_in(jax.random.fold_in(own_key, 6), axis_at), (blocks,), jnp.float32, low / len(cuts), largest / len(cuts))
        return jnp.repeat(jnp.exp(draws), shape[axis_at] // blocks).reshape((-1,) + (1,) * (len(shape) - axis_at - 1))

    level = one(*cuts[0])
    for cut in cuts[1:]:
        level = level * one(*cut)
    return level


def scatter_about(stream_key, dims, spread, reach, kind=jnp.bfloat16):
    return jnp.clip(spread * jax.random.normal(stream_key, dims, jnp.float32), -reach, reach).astype(kind)


def setup_inputs(seed: int = 0) -> dict:
    seeds = jax.random.split(jax.random.key(seed), 11)
    return {
        "queries": draw_queries(jax.random.fold_in(seeds[10], 71), 0),
        "passages": draw_passages(jax.random.fold_in(seeds[10], 71), 0),
        "noise": jnp.clip(0.0099487305 + 0.9783325 * jax.random.uniform(seeds[2], (NQ, NP), jnp.float32) ** block_scale(seeds[2], (NQ, NP), ((1, 32),), -0.2, 0.2), 0.0099487305, 0.98828125).astype(jnp.bfloat16),
        "mix_weight": scatter_about(seeds[3], (DQ, DM), (25 * DQ) ** -0.5, 0.046875),
        "answer_queries": draw_answer_queries(jax.random.fold_in(seeds[10], 71), 0),
        "key_weight": draw_key_weight(jax.random.fold_in(seeds[10], 71), 0),
        "value_weight": scatter_about(seeds[6], (DM, DM), DM ** -0.5, 0.1875),
        "token_states": draw_token_states(jax.random.fold_in(seeds[10], 71), 0),
        "block_owner": draw_block_owner(jax.random.fold_in(seeds[10], 71), 0),
        "listed": draw_listed(jax.random.fold_in(seeds[10], 71), 0),
    }


TEMPER = 0.5
FLOOR = -1.0e30


def softened(queries, passage_block, noise_block):
    logits = jnp.dot(queries, passage_block.T, preferred_element_type=jnp.float32)
    gumbel = -jnp.log(-jnp.log(noise_block.astype(jnp.float32)))
    return (logits * (DQ ** -0.5) + gumbel) / TEMPER


def reference(queries, passages, noise, mix_weight, answer_queries, key_weight, value_weight, token_states, block_owner, listed):
    stepping = jnp.arange(NP // PDEV, dtype=jnp.int32)

    def blocks_at(number):
        anchor = number * PDEV
        return (lax.dynamic_slice_in_dim(passages, anchor, PDEV, 0),
                lax.dynamic_slice_in_dim(noise, anchor, PDEV, 1))

    def first_pass(running, number):
        highest, denominator = running
        passage_block, noise_block = blocks_at(number)
        scores = softened(queries, passage_block, noise_block)
        raised = jnp.maximum(highest, jnp.max(scores, 1))
        denominator = denominator * jnp.exp(highest - raised) + jnp.sum(jnp.exp(scores - raised[:, None]), 1)
        return (raised, denominator), None

    start_high = jnp.full((NQ,), FLOOR, jnp.float32)
    (highest, denominator), _ = lax.scan(first_pass, (start_high, jnp.zeros((NQ,), jnp.float32)), stepping)

    def second_pass(blended, number):
        passage_block, noise_block = blocks_at(number)
        scores = softened(queries, passage_block, noise_block)
        weights = (jnp.exp(scores - highest[:, None]) / denominator[:, None]).astype(jnp.bfloat16)
        return blended + jnp.dot(weights, passage_block, preferred_element_type=jnp.float32), None

    blended, _ = lax.scan(second_pass, jnp.zeros((NQ, DQ), jnp.float32), stepping)
    blended_half = blended.astype(jnp.bfloat16)
    conditioned = (answer_queries.astype(jnp.float32)
                   + jnp.dot(blended_half, mix_weight, preferred_element_type=jnp.float32)).astype(jnp.bfloat16)

    def group_out(group):
        block_ids = lax.dynamic_index_in_dim(listed, group, 0, keepdims=False)
        slot_ids = jnp.take(block_owner, block_ids, axis=0)
        holder = slot_ids // BLK_DEV
        states = jnp.take(token_states, slot_ids, axis=0).reshape(KL * SEQ, DM)
        key_rows = lax.optimization_barrier(
            jnp.dot(states, key_weight, preferred_element_type=jnp.float32).astype(jnp.bfloat16))
        key_rows = key_rows.astype(jnp.float32).reshape(KL, SEQ, HEADS, HEAD_DIM)
        value_rows = lax.optimization_barrier(
            jnp.dot(states, value_weight, preferred_element_type=jnp.float32).astype(jnp.bfloat16))
        value_rows = value_rows.astype(jnp.float32).reshape(KL, SEQ, HEADS, HEAD_DIM)
        query_rows = lax.dynamic_slice_in_dim(conditioned, group * ROWS, ROWS, 0)
        query_rows = query_rows.astype(jnp.float32).reshape(ROWS, HEADS, HEAD_DIM)
        block_scores = jnp.einsum("rhd,lthd->rhlt", query_rows, key_rows)
        block_high = jnp.max(block_scores, 3)
        shared = holder[:, None] == holder[None, :]
        shelf_high = jnp.max(jnp.where(shared[None, None], block_high[:, :, None, :], FLOOR), 3)
        exponent = jnp.exp(block_scores - shelf_high[..., None])
        block_total = jnp.sum(exponent, 3)
        probs = lax.optimization_barrier(exponent.astype(jnp.bfloat16)).astype(jnp.float32)
        block_out = jnp.einsum("rhlt,lthd->rhld", probs, value_rows)
        group_high = jnp.max(shelf_high, 2)
        factor = jnp.exp(shelf_high - group_high[..., None])
        upper = jnp.sum(factor[..., None] * block_out, 2)
        lower = jnp.sum(factor * block_total, 2)
        return (upper / lower[..., None]).reshape(ROWS, DM).astype(jnp.bfloat16)

    attended = lax.map(group_out, jnp.arange(N_PB, dtype=jnp.int32))
    return attended.reshape(NQ, DM)
```

```python
import functools

import jax
import jax.numpy as jnp
from jax import lax
from jax.experimental import pallas as pl
from jax.experimental.pallas import tpu as pltpu
from jax.sharding import PartitionSpec as P

HEADS = 16
PAIR = 2
TEMPER = 0.5
FLOOR = -1e30
LANES = 128
STAT_ROWS = 32
VMEM_BYTES = 40 * 1024 * 1024
F32 = jnp.float32
BF16 = jnp.bfloat16
NT = (((1,), (1,)), ((), ()))


def grant():
    return pltpu.CompilerParams(vmem_limit_bytes=VMEM_BYTES)


def thirds(value):
    first = value.astype(BF16).astype(F32)
    rest = value - first
    second = rest.astype(BF16).astype(F32)
    return first, second, rest - second


def pack_row(mixed, shift, total):
    lane = lax.broadcasted_iota(jnp.int32, (mixed.shape[0], LANES), 1)
    tail = jnp.zeros((mixed.shape[0], LANES), F32)
    for at, term in enumerate(thirds(shift) + thirds(total)):
        tail = jnp.where(lane == at, term, tail)
    return jnp.concatenate([mixed, tail], 1).astype(BF16)


def unpack_row(packed):
    width = packed.shape[1] - LANES
    tail = packed[:, width:].astype(F32)
    shift = tail[:, 0:1] + tail[:, 1:2] + tail[:, 2:3]
    total = tail[:, 3:4] + tail[:, 4:5] + tail[:, 5:6]
    return packed[:, :width].astype(F32), shift, total


def merge_rows(parts):
    shift = functools.reduce(jnp.maximum, [part[1] for part in parts])
    mixed, total = 0.0, 0.0
    for part in parts:
        factor = jnp.exp(part[1] - shift)
        mixed = mixed + part[0] * factor
        total = total + part[2] * factor
    return mixed, shift, total


def retrieval_kernel(place, queries, passages, noise, keep, send, rows_scratch, *, spread):
    core = place[0]
    logits = lax.dot_general(queries[...], passages[...], NT, preferred_element_type=F32)
    gumbel = -jnp.log(-jnp.log(noise[...].astype(F32)))
    scores = (logits * queries.shape[1] ** (-0.5) + gumbel) / TEMPER
    shift = jnp.max(scores, 1, keepdims=True)
    weight = jnp.exp(scores - shift)
    total = jnp.sum(weight, 1, keepdims=True)
    mixed = jnp.dot(weight.astype(BF16), passages[...], preferred_element_type=F32)
    rows_scratch[...] = pack_row(mixed, shift, total).astype(F32)
    part = keep.shape[2]
    for column in range(spread):
        mine = pl.multiple_of((column * PAIR + core) * part, part)
        other = pl.multiple_of((column * PAIR + 1 - core) * part, part)
        keep[column, 0] = rows_scratch[pl.ds(mine, part), :].astype(BF16)
        send[column, 0] = rows_scratch[pl.ds(other, part), :].astype(BF16)


def retrieve(place, queries, passages, noise, readers, spread):
    count, width = queries.shape
    group = count // readers
    part = group // (PAIR * spread)
    shape = jax.ShapeDtypeStruct((spread, readers, part, width + LANES), BF16)
    spec = pl.BlockSpec((spread, 1, part, width + LANES), lambda g, place: (0, g, 0, 0))
    return pl.pallas_call(
        functools.partial(retrieval_kernel, spread=spread),
        grid_spec=pltpu.PrefetchScalarGridSpec(
            num_scalar_prefetch=1,
            grid=(readers,),
            in_specs=[
                pl.BlockSpec((group, width), lambda g, place: (g, 0)),
                pl.BlockSpec(passages.shape, lambda g, place: (0, 0)),
                pl.BlockSpec((group, noise.shape[1]), lambda g, place: (g, 0)),
            ],
            out_specs=[spec, spec],
            scratch_shapes=[pltpu.VMEM((group, width + LANES), F32)],
        ),
        out_shape=[shape, shape],
        compiler_params=grant(),
        name="retrieve",
    )(place, queries, passages, noise)


def pair_kernel(place, keep, recv, out, *, spread):
    for offset in range(spread):
        column = lax.bitwise_xor(place[1], offset)
        merged = merge_rows([unpack_row(keep[column, 0]), unpack_row(recv[column, 0])])
        out[offset, 0] = pack_row(*merged)


def merge_pair(place, keep, recv, spread):
    spec = pl.BlockSpec((spread, 1) + keep.shape[2:], lambda g, place: (0, g, 0, 0))
    return pl.pallas_call(
        functools.partial(pair_kernel, spread=spread),
        grid_spec=pltpu.PrefetchScalarGridSpec(
            num_scalar_prefetch=1, grid=(keep.shape[1],), in_specs=[spec, spec], out_specs=spec
        ),
        out_shape=jax.ShapeDtypeStruct(keep.shape, BF16),
        compiler_params=grant(),
        name="merge_pair",
    )(place, keep, recv)


def column_kernel(*refs):
    *parts, out = refs
    out[0] = pack_row(*merge_rows([unpack_row(part[0]) for part in parts]))


def merge_columns(parts):
    spec = pl.BlockSpec((1,) + parts[0].shape[1:], lambda g: (g, 0, 0))
    return pl.pallas_call(
        column_kernel,
        grid=(parts[0].shape[0],),
        in_specs=[spec] * len(parts),
        out_specs=spec,
        out_shape=jax.ShapeDtypeStruct(parts[0].shape, BF16),
        compiler_params=grant(),
        name="merge_columns",
    )(*parts)


def condition_kernel(place, parts, mix_weight, answers, keep, send, rows_scratch, *, spread):
    mixed, _, total = merge_rows([unpack_row(parts[at]) for at in range(parts.shape[0])])
    blended_half = (mixed / total).astype(BF16)
    part = blended_half.shape[0]
    start = pl.multiple_of((place[1] * PAIR + place[0]) * part, part)
    answer = answers[pl.ds(start, part), :].astype(F32)
    rows_scratch[...] = answer + jnp.dot(blended_half, mix_weight[...], preferred_element_type=F32)
    stride = keep.shape[1] // spread
    for column in range(spread):
        mine = pl.multiple_of((column * PAIR + place[0]) * stride, stride)
        other = pl.multiple_of((column * PAIR + 1 - place[0]) * stride, stride)
        keep[:, column * stride : (column + 1) * stride] = rows_scratch[:, pl.ds(mine, stride)].astype(BF16)
        send[:, column * stride : (column + 1) * stride] = rows_scratch[:, pl.ds(other, stride)].astype(BF16)


def condition(place, parts, mix_weight, answers, spread):
    model_width = mix_weight.shape[1]
    shape = jax.ShapeDtypeStruct((parts.shape[1], model_width // PAIR), BF16)
    whole = pl.BlockSpec(memory_space=pltpu.VMEM)
    return pl.pallas_call(
        functools.partial(condition_kernel, spread=spread),
        in_specs=[pl.BlockSpec(memory_space=pltpu.SMEM), whole, whole, whole],
        out_specs=[whole, whole],
        out_shape=[shape, shape],
        scratch_shapes=[pltpu.VMEM((parts.shape[1], model_width), F32)],
        compiler_params=grant(),
        name="condition",
    )(place, parts, mix_weight, answers.astype(F32))


def attend_kernel(place, table, pieces, key_own, key_pair, value_own, value_pair, out, *, offset, rows, inner, head_width):
    z = pl.program_id(0)
    relative = lax.bitwise_xor(z, place[3])
    spread = pieces.shape[0]
    quarters = []
    for column in range(spread):
        for core in range(PAIR):
            quarters.append(
                pieces[lax.bitwise_xor(place[1], column), relative, lax.bitwise_xor(place[0], core)]
            )
    query = jnp.concatenate(quarters, 0)
    width = query.shape[1]
    count = width // head_width
    lane = lax.broadcasted_iota(jnp.int32, query.shape, 1) // head_width
    spaced = jnp.concatenate([jnp.where(lane == head, query, jnp.zeros_like(query)) for head in range(count)], 0)
    entry = relative * inner + offset
    tokens = key_own.shape[1]
    shelves = []
    for shelf, (keys, values) in enumerate(((key_own, value_own), (key_pair, value_pair))):
        scores, slots = [], []
        for at in range(2):
            slot = table[entry * 6 + shelf * 3 + at]
            slots.append(slot)
            scores.append(lax.dot_general(keys[slot], spaced, NT, preferred_element_type=F32))
        high = jnp.maximum(jnp.max(scores[0], 0, keepdims=True), jnp.max(scores[1], 0, keepdims=True))
        total, mixed = 0.0, 0.0
        for slot, score in zip(slots, scores):
            exponent = jnp.exp(score - high)
            total = total + jnp.sum(exponent, 0, keepdims=True)
            start = pl.multiple_of(slot * tokens, tokens)
            mixed = mixed + jnp.dot(
                values[:, pl.ds(start, tokens)], exponent.astype(BF16), preferred_element_type=F32
            )
        there = table[entry * 6 + shelf * 3 + 2] > 0
        shelves.append((jnp.where(there, high, FLOOR), jnp.where(there, total, 0.0), mixed, there))
    high = jnp.maximum(shelves[0][0], shelves[1][0])
    total, mixed = 0.0, 0.0
    for shelf_high, shelf_total, shelf_mixed, there in shelves:
        factor = jnp.where(there, jnp.exp(shelf_high - high), 0.0)
        total = total + shelf_total * factor
        mixed = mixed + shelf_mixed * factor
    for head in range(count):
        out[0, head * head_width : (head + 1) * head_width, :] = mixed[
            head * head_width : (head + 1) * head_width, head * rows : (head + 1) * rows
        ].astype(BF16)
    out[0, width:, :] = pack_stats(high, total, count, rows)


def pack_stats(high, total, count, rows):
    places = lax.broadcasted_iota(jnp.int32, (STAT_ROWS, rows), 0)
    packed = jnp.zeros((STAT_ROWS, rows), F32)
    for head in range(count):
        here = slice(head * rows, (head + 1) * rows)
        for at, term in enumerate(thirds(high[:, here]) + thirds(total[:, here])):
            packed = jnp.where(places == head * 6 + at, term, packed)
    return packed.astype(BF16)


def attend(place, table, pieces, keys, values, offset, column, inner, head_width):
    spread, outer, pair, part, half = pieces.shape
    width = half // spread
    rows = spread * pair * part
    slots, tokens = keys[0].shape[:2]

    def at_column(*lead):
        return lambda z, place, table: lead + (lax.bitwise_xor(place[1], column),)

    key_spec = pl.BlockSpec((slots, tokens, width), at_column(0, 0))
    value_spec = pl.BlockSpec(
        (width, slots * tokens), lambda z, place, table: (lax.bitwise_xor(place[1], column), 0)
    )
    return pl.pallas_call(
        functools.partial(attend_kernel, offset=offset, rows=rows, inner=inner, head_width=head_width),
        grid_spec=pltpu.PrefetchScalarGridSpec(
            num_scalar_prefetch=2,
            grid=(outer,),
            in_specs=[
                pl.BlockSpec((spread, outer, pair, part, width), at_column(0, 0, 0, 0)),
                key_spec,
                key_spec,
                value_spec,
                value_spec,
            ],
            out_specs=pl.BlockSpec((1, width + STAT_ROWS, rows), lambda z, place, table: (z, 0, 0)),
        ),
        out_shape=jax.ShapeDtypeStruct((outer, width + STAT_ROWS, rows), BF16),
        compiler_params=grant(),
        cost_estimate=pl.CostEstimate(
            flops=outer * 4 * 4 * rows * tokens * width * (width // head_width),
            bytes_accessed=4 * slots * tokens * width * 2,
            transcendentals=outer * 4 * rows * tokens * (width // head_width),
        ),
        name="attend",
    )(place, table, pieces, *keys, *values)


def unpack_stats(packed, width, count):
    tail = packed[width:, :].astype(F32)
    highs, totals = [], []
    for head in range(count):
        base = head * 6
        highs.append(tail[base : base + 1] + tail[base + 1 : base + 2] + tail[base + 2 : base + 3])
        totals.append(tail[base + 3 : base + 4] + tail[base + 4 : base + 5] + tail[base + 5 : base + 6])
    return highs, totals


def merge_heads(parts, width, head_width):
    count = width // head_width
    stats = [unpack_stats(part, width, count) for part in parts]
    mixes, highs, totals = [], [], []
    for head in range(count):
        high = functools.reduce(jnp.maximum, [stat[0][head] for stat in stats])
        mixed, total = 0.0, 0.0
        for part, stat in zip(parts, stats):
            factor = jnp.where(stat[1][head] > 0, jnp.exp(stat[0][head] - high), 0.0)
            total = total + stat[1][head] * factor
            mixed = mixed + part[head * head_width : (head + 1) * head_width, :].astype(F32) * factor
        mixes.append(mixed)
        highs.append(high)
        totals.append(total)
    return mixes, highs, totals


def gather_kernel(place, *refs, inner, spread, head_width):
    *parts, out = refs
    width = out.shape[2] - STAT_ROWS
    rows = out.shape[3]
    count = width // head_width
    for offset in range(inner):
        taken = [parts[offset * spread + column][0] for column in range(spread)]
        mixes, highs, totals = merge_heads(taken, width, head_width)
        target = lax.bitwise_xor(place[2], offset)
        for head in range(count):
            out[0, target, head * head_width : (head + 1) * head_width, :] = mixes[head].astype(BF16)
        out[0, target, width:, :] = pack_stats(
            jnp.concatenate(highs, 1), jnp.concatenate(totals, 1), count, rows
        )


def merge_lots(place, parts, inner, spread, head_width):
    outer, height, rows = parts[0].shape
    spec = pl.BlockSpec((1, height, rows), lambda z, place: (z, 0, 0))
    return pl.pallas_call(
        functools.partial(gather_kernel, inner=inner, spread=spread, head_width=head_width),
        grid_spec=pltpu.PrefetchScalarGridSpec(
            num_scalar_prefetch=1,
            grid=(outer,),
            in_specs=[spec] * len(parts),
            out_specs=pl.BlockSpec((1, inner, height, rows), lambda z, place: (z, 0, 0, 0)),
        ),
        out_shape=jax.ShapeDtypeStruct((outer, inner, height, rows), BF16),
        compiler_params=grant(),
        name="merge_lots",
    )(place, *parts)


def finish_kernel(parts, out, *, head_width):
    width = parts.shape[1] - STAT_ROWS
    mixes, _, totals = merge_heads([parts[at] for at in range(parts.shape[0])], width, head_width)
    done = jnp.concatenate([mixed / total for mixed, total in zip(mixes, totals)], 0)
    out[...] = done.T.astype(BF16)


def finish(parts, head_width):
    whole = pl.BlockSpec(memory_space=pltpu.VMEM)
    return pl.pallas_call(
        functools.partial(finish_kernel, head_width=head_width),
        in_specs=[whole],
        out_specs=whole,
        out_shape=jax.ShapeDtypeStruct((parts.shape[2], parts.shape[1] - STAT_ROWS), BF16),
        compiler_params=grant(),
        name="finish",
    )(parts)


def local(
    queries,
    passages,
    noise,
    mix_weight,
    answer_queries,
    key_weight,
    value_weight,
    token_states,
    block_owner,
    listed,
):
    readers = lax.axis_size("pb")
    runners = lax.axis_size("pa")
    group = lax.axis_index("pb")
    runner = lax.axis_index("pa")
    spread = runners // PAIR
    inner = 1
    while (2 * inner) * (2 * inner) <= readers:
        inner *= 2
    outer = readers // inner
    model_width = key_weight.shape[0]
    head_width = model_width // HEADS
    slots, tokens = token_states.shape[:2]
    place = jnp.stack([runner % PAIR, runner // PAIR, group % inner, group // inner]).astype(jnp.int32)

    def swap(value, axis, bits):
        size = lax.axis_size(axis)
        return lax.ppermute(value, axis, [(at, at ^ bits) for at in range(size)])

    entries = listed
    step = 1
    while step < readers:
        entries = jnp.concatenate([entries, swap(entries, "pb", step)], 0)
        step *= 2
    slot_ids = jnp.take(block_owner, entries, axis=0)
    held = slot_ids // slots == runner * readers + group
    inside = slot_ids % slots
    chosen = jnp.stack(
        [
            jnp.min(jnp.where(held, inside, slots - 1), 1),
            jnp.max(jnp.where(held, inside, 0), 1),
            jnp.any(held, 1).astype(jnp.int32),
        ],
        1,
    )
    table = jnp.concatenate([chosen, swap(chosen, "pa", 1)], 1).reshape(-1)

    states = token_states.reshape(slots * tokens, model_width)
    pair_states = swap(states, "pa", 1)

    def core_columns(weight):
        split = weight.reshape(model_width, spread, PAIR, model_width // runners)
        return lax.dynamic_index_in_dim(split, runner % PAIR, 2, keepdims=False).reshape(model_width, -1)

    own_key, own_value = core_columns(key_weight), core_columns(value_weight)
    keys, values = [], []
    for rows in (states, pair_states):
        keys.append(
            jnp.dot(rows, own_key, preferred_element_type=F32).astype(BF16).reshape(slots, tokens, -1)
        )
        values.append(
            lax.dot_general(own_value, rows, (((0,), (1,)), ((), ())), preferred_element_type=F32).astype(BF16)
        )

    keep, send = retrieve(place, queries, passages, noise, readers, spread)
    by_column = merge_pair(place, keep, swap(send, "pa", 1), spread)
    parts = [by_column[0]] + [swap(by_column[at], "pa", at * PAIR) for at in range(1, spread)]
    by_group = merge_columns(parts)
    mine = lax.all_to_all(by_group, "pb", split_axis=0, concat_axis=0, tiled=True)
    kept, sent = condition(place, mine, mix_weight, answer_queries, spread)

    pieces = jnp.stack([kept, swap(sent, "pa", 1)])[None]
    step = inner
    while step < readers:
        pieces = jnp.concatenate([pieces, swap(pieces, "pb", step)], 0)
        step *= 2
    pieces = jnp.stack([pieces] + [swap(pieces, "pa", at * PAIR) for at in range(1, spread)])
    lots = []
    for offset in range(inner):
        query = pieces if offset == 0 else swap(pieces, "pb", offset)
        own = []
        for column in reversed(range(spread)):
            lot = attend(place, table, query, keys, values, offset, column, inner, head_width)
            own.append(lot if column == 0 else swap(lot, "pa", column * PAIR))
        lots += own[::-1]
    merged = merge_lots(place, lots, inner, spread, head_width)
    merged = merged.reshape((readers,) + merged.shape[2:])
    return finish(lax.all_to_all(merged, "pb", split_axis=0, concat_axis=0, tiled=True), head_width)


def solution(mesh):
    return jax.shard_map(
        local,
        mesh=mesh,
        in_specs=(
            P(),
            P(("pa", "pb"), None),
            P(None, ("pa", "pb")),
            P(),
            P("pb", None),
            P(),
            P(),
            P(("pa", "pb"), None, None),
            P(),
            P("pb", "pa"),
        ),
        out_specs=P("pb", "pa"),
        check_vma=False,
    )
```

```python
import functools

import jax
import jax.numpy as jnp
from jax import lax
from jax.experimental import pallas as pl
from jax.experimental.pallas import tpu as pltpu
from jax.sharding import PartitionSpec as P

HEADS = 16
PAIR = 2
TEMPER = 0.5
FLOOR = -1e30
LANES = 128
STAT_ROWS = 32
NOTE_AT = 6
STEP_GROUPS = 2
PROJECT_STEPS = 4
VMEM_BYTES = 40 * 1024 * 1024
WIDE_BYTES = 60 * 1024 * 1024
F32 = jnp.float32
BF16 = jnp.bfloat16
NT = (((1,), (1,)), ((), ()))


def grant():
    return pltpu.CompilerParams(vmem_limit_bytes=VMEM_BYTES)


def thirds(value):
    first = value.astype(BF16).astype(F32)
    rest = value - first
    second = rest.astype(BF16).astype(F32)
    return first, second, rest - second


def pack_tail(shift, total):
    lane = lax.broadcasted_iota(jnp.int32, (shift.shape[0], LANES), 1)
    tail = jnp.zeros((shift.shape[0], LANES), F32)
    for at, term in enumerate(thirds(shift) + thirds(total)):
        tail = jnp.where(lane == at, term, tail)
    return tail


def unpack_tail(tail):
    term = lax.broadcasted_iota(jnp.int32, (LANES, 2 * LANES), 0)
    half = lax.broadcasted_iota(jnp.int32, (LANES, 2 * LANES), 1) // LANES
    pick = jnp.where(term // 3 == half, 1.0, 0.0).astype(BF16)
    both = jnp.dot(tail, pick, preferred_element_type=F32)
    return both[:, :LANES], both[:, LANES:]


def merge_rows(parts):
    width = parts[0].shape[1] - LANES
    stats = [unpack_tail(part[:, width:]) for part in parts]
    shift = functools.reduce(jnp.maximum, [stat[0] for stat in stats])
    factors = [jnp.exp(stat[0] - shift) for stat in stats]
    total = sum(stat[1] * factor for stat, factor in zip(stats, factors))
    tiles = [
        sum(part[:, at : at + LANES].astype(F32) * factor for part, factor in zip(parts, factors))
        for at in range(0, width, LANES)
    ]
    return tiles, shift, total


def flat(value):
    return value.reshape((-1, value.shape[-1]))


def retrieval_kernel(place, queries, passages, noise, keep, send, rows_scratch, *, spread):
    core = place[0]
    groups, part = keep.shape[1:3]
    width = queries.shape[1]
    logits = lax.dot_general(queries[...], passages[...], NT, preferred_element_type=F32)
    gumbel = -jnp.log(-jnp.log(noise[...].astype(F32)))
    scores = (logits * width ** (-0.5) + gumbel) / TEMPER
    shift = jnp.max(scores, 1, keepdims=True)
    weight = jnp.exp(scores - shift)
    total = jnp.sum(weight, 1, keepdims=True)
    rows_scratch[:, :width] = jnp.dot(weight.astype(BF16), passages[...], preferred_element_type=F32)
    rows_scratch[:, width:] = pack_tail(shift, total)
    for at in range(groups):
        for column in range(spread):
            base = (at * spread + column) * PAIR
            mine = pl.multiple_of((base + core) * part, part)
            other = pl.multiple_of((base + 1 - core) * part, part)
            keep[column, at] = rows_scratch[pl.ds(mine, part), :].astype(BF16)
            send[column, at] = rows_scratch[pl.ds(other, part), :].astype(BF16)


def retrieve(place, queries, passages, noise, readers, spread):
    count, width = queries.shape
    group = count // readers
    part = group // (PAIR * spread)
    shape = jax.ShapeDtypeStruct((spread, readers, part, width + LANES), BF16)
    spec = pl.BlockSpec((spread, STEP_GROUPS, part, width + LANES), lambda g, place: (0, g, 0, 0))
    rows = group * STEP_GROUPS
    return pl.pallas_call(
        functools.partial(retrieval_kernel, spread=spread),
        grid_spec=pltpu.PrefetchScalarGridSpec(
            num_scalar_prefetch=1,
            grid=(readers // STEP_GROUPS,),
            in_specs=[
                pl.BlockSpec((rows, width), lambda g, place: (g, 0)),
                pl.BlockSpec(passages.shape, lambda g, place: (0, 0)),
                pl.BlockSpec((rows, noise.shape[1]), lambda g, place: (g, 0)),
            ],
            out_specs=[spec, spec],
            scratch_shapes=[pltpu.VMEM((rows, width + LANES), F32)],
        ),
        out_shape=[shape, shape],
        compiler_params=pltpu.CompilerParams(vmem_limit_bytes=WIDE_BYTES),
        cost_estimate=pl.CostEstimate(
            flops=4 * count * width * passages.shape[0],
            bytes_accessed=2 * (2 * count * width + passages.size + noise.size),
            transcendentals=3 * noise.size,
        ),
        name="retrieve",
    )(place, queries, passages, noise)


def store_rows(out, tiles, shift, total, note=None):
    for at, tile in enumerate(tiles):
        out[..., at * LANES : (at + 1) * LANES] = tile.astype(BF16).reshape(out.shape[:-1] + (LANES,))
    tail = pack_tail(shift, total)
    if note is not None:
        tail = tail + note
    out[..., len(tiles) * LANES :] = tail.astype(BF16).reshape(out.shape[:-1] + (LANES,))


def pair_kernel(place, keep, recv, *outs):
    for offset, out in enumerate(outs):
        column = lax.bitwise_xor(place[1], offset)
        store_rows(out, *merge_rows([flat(keep[column]), flat(recv[column])]))


def merge_pair(place, keep, recv, spread):
    readers = keep.shape[1]
    spec = pl.BlockSpec((spread, readers // 2) + keep.shape[2:], lambda g, place: (0, g, 0, 0))
    out = pl.BlockSpec((readers // 2,) + keep.shape[2:], lambda g, place: (g, 0, 0))
    return pl.pallas_call(
        pair_kernel,
        grid_spec=pltpu.PrefetchScalarGridSpec(
            num_scalar_prefetch=1, grid=(2,), in_specs=[spec, spec], out_specs=[out] * spread
        ),
        out_shape=[jax.ShapeDtypeStruct(keep.shape[1:], BF16)] * spread,
        compiler_params=grant(),
        name="merge_pair",
    )(place, keep, recv)


def column_kernel(note, *refs):
    *parts, out = refs
    store_rows(out, *merge_rows([flat(part[...]) for part in parts]), note[...])


def merge_columns(note, parts):
    readers = parts[0].shape[0]
    spec = pl.BlockSpec((readers // 2,) + parts[0].shape[1:], lambda g: (g, 0, 0))
    return pl.pallas_call(
        column_kernel,
        grid=(2,),
        in_specs=[pl.BlockSpec(note.shape, lambda g: (0, 0))] + [spec] * len(parts),
        out_specs=spec,
        out_shape=jax.ShapeDtypeStruct(parts[0].shape, BF16),
        compiler_params=grant(),
        name="merge_columns",
    )(note, *parts)


def condition_kernel(place, parts, mix_weight, answers, keep, send, rows_scratch, *, spread):
    tiles, _, total = merge_rows([parts[at] for at in range(parts.shape[0])])
    blended_half = jnp.concatenate([(tile / total).astype(BF16) for tile in tiles], 1)
    part = blended_half.shape[0]
    start = pl.multiple_of((place[1] * PAIR + place[0]) * part, part)
    answer = answers[pl.ds(start, part), :].astype(F32)
    rows_scratch[...] = answer + jnp.dot(blended_half, mix_weight[...], preferred_element_type=F32)
    stride = keep.shape[1] // spread
    for column in range(spread):
        mine = pl.multiple_of((column * PAIR + place[0]) * stride, stride)
        other = pl.multiple_of((column * PAIR + 1 - place[0]) * stride, stride)
        keep[:, column * stride : (column + 1) * stride] = rows_scratch[:, pl.ds(mine, stride)].astype(BF16)
        send[:, column * stride : (column + 1) * stride] = rows_scratch[:, pl.ds(other, stride)].astype(BF16)


def condition(place, parts, mix_weight, answers, spread):
    model_width = mix_weight.shape[1]
    shape = jax.ShapeDtypeStruct((parts.shape[1], model_width // PAIR), BF16)
    whole = pl.BlockSpec(memory_space=pltpu.VMEM)
    return pl.pallas_call(
        functools.partial(condition_kernel, spread=spread),
        in_specs=[pl.BlockSpec(memory_space=pltpu.SMEM), whole, whole, whole],
        out_specs=[whole, whole],
        out_shape=[shape, shape],
        scratch_shapes=[pltpu.VMEM((parts.shape[1], model_width), F32)],
        compiler_params=grant(),
        name="condition",
    )(place, parts, mix_weight, answers)


def project_kernel(place, states, *refs):
    spread = len(refs) // 2 - 1
    keys, values = refs[-2:]
    width = keys.shape[1] // spread
    for column in range(spread):
        key = jnp.dot(states[...], refs[column][...], preferred_element_type=F32)
        keys[:, column * width : (column + 1) * width] = key.astype(BF16)
        value = jnp.dot(states[...], refs[spread + column][...], preferred_element_type=F32)
        values[column * width : (column + 1) * width, :] = value.astype(BF16).T


def project(place, states, key_weight, value_weight, spread):
    rows, model_width = states.shape
    width = model_width // (PAIR * spread)
    chunk = rows // PROJECT_STEPS

    def weight_spec(column):
        return pl.BlockSpec((model_width, width), lambda t, place: (0, column * PAIR + place[0]))

    specs = [weight_spec(column) for column in range(spread)]
    return pl.pallas_call(
        project_kernel,
        grid_spec=pltpu.PrefetchScalarGridSpec(
            num_scalar_prefetch=1,
            grid=(PROJECT_STEPS,),
            in_specs=[pl.BlockSpec((chunk, model_width), lambda t, place: (t, 0))] + specs + specs,
            out_specs=[
                pl.BlockSpec((chunk, spread * width), lambda t, place: (t, 0)),
                pl.BlockSpec((spread * width, chunk), lambda t, place: (0, t)),
            ],
        ),
        out_shape=[
            jax.ShapeDtypeStruct((rows, spread * width), BF16),
            jax.ShapeDtypeStruct((spread * width, rows), BF16),
        ],
        compiler_params=grant(),
        cost_estimate=pl.CostEstimate(
            flops=4 * rows * model_width * spread * width,
            bytes_accessed=2 * (2 * model_width * spread * width + 2 * rows * model_width),
            transcendentals=0,
        ),
        name="project",
    )(place, states, *([key_weight] * spread), *([value_weight] * spread))


def attend_kernel(
    place, table, pieces, key_own, key_pair, value_own, value_pair, out, *, offset, column, inner, tokens, head_width
):
    z = pl.program_id(0)
    relative = lax.bitwise_xor(z, place[3])
    spread, rows = pieces.shape[0], out.shape[2]
    width = out.shape[1] - STAT_ROWS
    count = width // head_width
    left = pl.multiple_of(lax.bitwise_xor(place[1], column) * width, width)
    quarters = []
    for lane in range(spread):
        for core in range(PAIR):
            lead = (lax.bitwise_xor(place[1], lane), relative, lax.bitwise_xor(place[0], core))
            quarters.append(pieces[lead + (slice(None), pl.ds(left, width))])
    query = jnp.concatenate(quarters, 0).T
    head_at = lax.broadcasted_iota(jnp.int32, query.shape, 0) // head_width
    spaced = jnp.concatenate([jnp.where(head_at == head, query, jnp.zeros_like(query)) for head in range(count)], 1)
    entry = z * inner + lax.bitwise_xor(place[2], offset)
    shelves = []
    for shelf, (keys, values) in enumerate(((key_own, value_own), (key_pair, value_pair))):
        scores, starts = [], []
        for at in range(2):
            start = pl.multiple_of(table[entry * 6 + shelf * 3 + at] * tokens, tokens)
            starts.append(start)
            key = keys[pl.ds(start, tokens), pl.ds(left, width)]
            scores.append(jnp.dot(key, spaced, preferred_element_type=F32))
        high = jnp.maximum(jnp.max(scores[0], 0, keepdims=True), jnp.max(scores[1], 0, keepdims=True))
        total, mixed = 0.0, 0.0
        for start, score in zip(starts, scores):
            exponent = jnp.exp(score - high)
            total = total + jnp.sum(exponent, 0, keepdims=True)
            value = values[pl.ds(left, width), pl.ds(start, tokens)]
            mixed = mixed + jnp.dot(value, exponent.astype(BF16), preferred_element_type=F32)
        there = table[entry * 6 + shelf * 3 + 2] > 0
        blocks = [
            mixed[head * head_width : (head + 1) * head_width, head * rows : (head + 1) * rows]
            for head in range(count)
        ]
        shelves.append((jnp.where(there, high, FLOOR), jnp.where(there, total, 0.0), blocks, there))
    high = jnp.maximum(shelves[0][0], shelves[1][0])
    factors = [jnp.where(there, jnp.exp(shelf_high - high), 0.0) for shelf_high, _, _, there in shelves]
    total = shelves[0][1] * factors[0] + shelves[1][1] * factors[1]
    for head in range(count):
        here = slice(head * rows, (head + 1) * rows)
        joined = shelves[0][2][head] * factors[0][:, here] + shelves[1][2][head] * factors[1][:, here]
        out[0, head * head_width : (head + 1) * head_width, :] = joined.astype(BF16)
    out[0, width:, :] = pack_stats(high, total, count, rows)


def pack_stats(high, total, count, rows):
    places = lax.broadcasted_iota(jnp.int32, (STAT_ROWS, rows), 0)
    packed = jnp.zeros((STAT_ROWS, rows), F32)
    for head in range(count):
        here = slice(head * rows, (head + 1) * rows)
        for at, term in enumerate(thirds(high[:, here]) + thirds(total[:, here])):
            packed = jnp.where(places == head * 6 + at, term, packed)
    return packed.astype(BF16)


def attend(place, table, pieces, keys, values, offset, column, inner, tokens, head_width):
    spread, outer, pair, part, half = pieces.shape
    width = half // spread
    rows = spread * pair * part
    whole = pl.BlockSpec(memory_space=pltpu.VMEM)
    return pl.pallas_call(
        functools.partial(
            attend_kernel, offset=offset, column=column, inner=inner, tokens=tokens, head_width=head_width
        ),
        grid_spec=pltpu.PrefetchScalarGridSpec(
            num_scalar_prefetch=2,
            grid=(outer,),
            in_specs=[whole] * 5,
            out_specs=pl.BlockSpec((1, width + STAT_ROWS, rows), lambda z, place, table: (z, 0, 0)),
        ),
        out_shape=jax.ShapeDtypeStruct((outer, width + STAT_ROWS, rows), BF16),
        compiler_params=grant(),
        cost_estimate=pl.CostEstimate(
            flops=outer * 4 * 4 * rows * tokens * width * (width // head_width),
            bytes_accessed=outer * 2 * (width + STAT_ROWS) * rows,
            transcendentals=outer * 4 * rows * tokens * (width // head_width),
        ),
        name="attend",
    )(place, table, pieces, *keys, *values)


def unpack_stats(packed, width, count):
    tail = packed[width:, :].astype(F32)
    highs, totals = [], []
    for head in range(count):
        base = head * 6
        highs.append(tail[base : base + 1] + tail[base + 1 : base + 2] + tail[base + 2 : base + 3])
        totals.append(tail[base + 3 : base + 4] + tail[base + 4 : base + 5] + tail[base + 5 : base + 6])
    return highs, totals


def merge_heads(parts, width, head_width):
    count = width // head_width
    stats = [unpack_stats(part, width, count) for part in parts]
    mixes, highs, totals = [], [], []
    for head in range(count):
        high = functools.reduce(jnp.maximum, [stat[0][head] for stat in stats])
        mixed, total = 0.0, 0.0
        for part, stat in zip(parts, stats):
            factor = jnp.where(stat[1][head] > 0, jnp.exp(stat[0][head] - high), 0.0)
            total = total + stat[1][head] * factor
            mixed = mixed + part[head * head_width : (head + 1) * head_width, :].astype(F32) * factor
        mixes.append(mixed)
        highs.append(high)
        totals.append(total)
    return mixes, highs, totals


def gather_kernel(place, *refs, inner, spread, head_width):
    *parts, out = refs
    width = out.shape[2] - STAT_ROWS
    rows = out.shape[3]
    count = width // head_width
    for offset in range(inner):
        taken = [parts[offset * spread + column][0] for column in range(spread)]
        mixes, highs, totals = merge_heads(taken, width, head_width)
        target = lax.bitwise_xor(place[2], offset)
        for head in range(count):
            out[0, target, head * head_width : (head + 1) * head_width, :] = mixes[head].astype(BF16)
        out[0, target, width:, :] = pack_stats(
            jnp.concatenate(highs, 1), jnp.concatenate(totals, 1), count, rows
        )


def merge_lots(place, parts, inner, spread, head_width):
    outer, height, rows = parts[0].shape
    spec = pl.BlockSpec((1, height, rows), lambda z, place: (z, 0, 0))
    return pl.pallas_call(
        functools.partial(gather_kernel, inner=inner, spread=spread, head_width=head_width),
        grid_spec=pltpu.PrefetchScalarGridSpec(
            num_scalar_prefetch=1,
            grid=(outer,),
            in_specs=[spec] * len(parts),
            out_specs=pl.BlockSpec((1, inner, height, rows), lambda z, place: (z, 0, 0, 0)),
        ),
        out_shape=jax.ShapeDtypeStruct((outer, inner, height, rows), BF16),
        compiler_params=grant(),
        name="merge_lots",
    )(place, *parts)


def finish_kernel(parts, out, *, head_width):
    width = parts.shape[1] - STAT_ROWS
    mixes, _, totals = merge_heads([parts[at] for at in range(parts.shape[0])], width, head_width)
    done = jnp.concatenate([mixed / total for mixed, total in zip(mixes, totals)], 0)
    out[...] = done.T.astype(BF16)


def finish(parts, head_width):
    whole = pl.BlockSpec(memory_space=pltpu.VMEM)
    return pl.pallas_call(
        functools.partial(finish_kernel, head_width=head_width),
        in_specs=[whole],
        out_specs=whole,
        out_shape=jax.ShapeDtypeStruct((parts.shape[2], parts.shape[1] - STAT_ROWS), BF16),
        compiler_params=grant(),
        name="finish",
    )(parts)


def local(
    queries,
    passages,
    noise,
    mix_weight,
    answer_queries,
    key_weight,
    value_weight,
    token_states,
    block_owner,
    listed,
):
    readers = lax.axis_size("pb")
    runners = lax.axis_size("pa")
    group = lax.axis_index("pb")
    runner = lax.axis_index("pa")
    spread = runners // PAIR
    inner = 1
    while (2 * inner) * (2 * inner) <= readers:
        inner *= 2
    outer = readers // inner
    model_width = key_weight.shape[0]
    head_width = model_width // HEADS
    slots, tokens = token_states.shape[:2]
    place = jnp.stack([runner % PAIR, runner // PAIR, group % inner, group // inner]).astype(jnp.int32)

    def swap(value, axis, bits):
        size = lax.axis_size(axis)
        return lax.ppermute(value, axis, [(at, at ^ bits) for at in range(size)])

    states = token_states.reshape(slots * tokens, model_width)
    pair_states = swap(states, "pa", 1)

    keep, send = retrieve(place, queries, passages, noise, readers, spread)
    wanted = jnp.take(block_owner, listed[0], axis=0)
    digits = jnp.concatenate([wanted // LANES, wanted % LANES]).astype(F32)
    note = jnp.pad(digits[None], ((0, 0), (NOTE_AT, LANES - NOTE_AT - digits.shape[0])))
    by_column = merge_pair(place, keep, swap(send, "pa", 1), spread)
    own_key, own_value = project(place, states, key_weight, value_weight, spread)
    parts = [by_column[0]] + [swap(by_column[at], "pa", at * PAIR) for at in range(1, spread)]
    by_group = merge_columns(note, parts)
    mine = lax.all_to_all(by_group, "pb", split_axis=0, concat_axis=0, tiled=True)
    pair_key, pair_value = project(place, pair_states, key_weight, value_weight, spread)
    keys, values = (own_key, pair_key), (own_value, pair_value)
    kept, sent = condition(place, mine, mix_weight, answer_queries, spread)

    digits = mine[:, 0, queries.shape[1] + NOTE_AT :][:, : digits.shape[0]].astype(jnp.int32)
    slot_ids = digits[:, : wanted.shape[0]] * LANES + digits[:, wanted.shape[0] :]
    held = slot_ids // slots == runner * readers + group
    inside = slot_ids % slots
    chosen = jnp.stack(
        [
            jnp.min(jnp.where(held, inside, slots - 1), 1),
            jnp.max(jnp.where(held, inside, 0), 1),
            jnp.any(held, 1).astype(jnp.int32),
        ],
        1,
    )
    table = jnp.concatenate([chosen, swap(chosen, "pa", 1)], 1).reshape(-1)

    pieces = jnp.stack([kept, swap(sent, "pa", 1)])[None]
    step = inner
    while step < readers:
        pieces = jnp.concatenate([pieces, swap(pieces, "pb", step)], 0)
        step *= 2
    pieces = jnp.stack([pieces] + [swap(pieces, "pa", at * PAIR) for at in range(1, spread)])
    lots = []
    for offset in range(inner):
        query = pieces if offset == 0 else swap(pieces, "pb", offset)
        own = []
        for column in reversed(range(spread)):
            lot = attend(place, table, query, keys, values, offset, column, inner, tokens, head_width)
            own.append(lot if column == 0 else swap(lot, "pa", column * PAIR))
        lots += own[::-1]
    merged = merge_lots(place, lots, inner, spread, head_width)
    merged = merged.reshape((readers,) + merged.shape[2:])
    return finish(lax.all_to_all(merged, "pb", split_axis=0, concat_axis=0, tiled=True), head_width)


def solution(mesh):
    return jax.shard_map(
        local,
        mesh=mesh,
        in_specs=(
            P(),
            P(("pa", "pb"), None),
            P(None, ("pa", "pb")),
            P(),
            P("pb", None),
            P(),
            P(),
            P(("pa", "pb"), None, None),
            P(),
            P("pb", "pa"),
        ),
        out_specs=P("pb", "pa"),
        check_vma=False,
    )
```

```python
import functools

import jax
import jax.numpy as jnp
from jax import lax
from jax.experimental import pallas as pl
from jax.experimental.pallas import tpu as pltpu
from jax.sharding import PartitionSpec as P

HEADS = 16
PAIR = 2
TEMPER = 0.5
FLOOR = -1e30
LANES = 128
STAT_ROWS = 32
NOTE_AT = 6
STEP_GROUPS = 2
PROJECT_STEPS = 2
ATTEND_GROUPS = 4
HEAD_BUNDLE = 2
VMEM_BYTES = 40 * 1024 * 1024
WIDE_BYTES = 60 * 1024 * 1024
F32 = jnp.float32
BF16 = jnp.bfloat16
NT = (((1,), (1,)), ((), ()))


def grant():
    return pltpu.CompilerParams(vmem_limit_bytes=VMEM_BYTES)


def thirds(value):
    first = value.astype(BF16).astype(F32)
    rest = value - first
    second = rest.astype(BF16).astype(F32)
    return first, second, rest - second


def pack_tail(shift, total):
    lane = lax.broadcasted_iota(jnp.int32, (shift.shape[0], LANES), 1)
    tail = jnp.zeros((shift.shape[0], LANES), F32)
    for at, term in enumerate(thirds(shift) + thirds(total)):
        tail = jnp.where(lane == at, term, tail)
    return tail


def unpack_tail(tail):
    term = lax.broadcasted_iota(jnp.int32, (LANES, 2 * LANES), 0)
    half = lax.broadcasted_iota(jnp.int32, (LANES, 2 * LANES), 1) // LANES
    pick = jnp.where(term // 3 == half, 1.0, 0.0).astype(BF16)
    both = jnp.dot(tail, pick, preferred_element_type=F32)
    return both[:, :LANES], both[:, LANES:]


def merge_rows(parts):
    width = parts[0].shape[1] - LANES
    stats = [unpack_tail(part[:, width:]) for part in parts]
    shift = functools.reduce(jnp.maximum, [stat[0] for stat in stats])
    factors = [jnp.exp(stat[0] - shift) for stat in stats]
    total = sum(stat[1] * factor for stat, factor in zip(stats, factors))
    tiles = [
        sum(part[:, at : at + LANES].astype(F32) * factor for part, factor in zip(parts, factors))
        for at in range(0, width, LANES)
    ]
    return tiles, shift, total


def flat(value):
    return value.reshape((-1, value.shape[-1]))


def retrieval_kernel(place, queries, passages, noise, keep, send, rows_scratch, *, spread):
    core = place[0]
    groups, part = keep.shape[1:3]
    width = queries.shape[1]
    logits = lax.dot_general(queries[...], passages[...], NT, preferred_element_type=F32)
    gumbel = -jnp.log(-jnp.log(noise[...].astype(F32)))
    scores = (logits * width ** (-0.5) + gumbel) / TEMPER
    shift = jnp.max(scores, 1, keepdims=True)
    weight = jnp.exp(scores - shift)
    total = jnp.sum(weight, 1, keepdims=True)
    rows_scratch[:, :width] = jnp.dot(weight.astype(BF16), passages[...], preferred_element_type=F32)
    rows_scratch[:, width:] = pack_tail(shift, total)
    for at in range(groups):
        for column in range(spread):
            base = (at * spread + column) * PAIR
            mine = pl.multiple_of((base + core) * part, part)
            other = pl.multiple_of((base + 1 - core) * part, part)
            keep[column, at] = rows_scratch[pl.ds(mine, part), :].astype(BF16)
            send[column, at] = rows_scratch[pl.ds(other, part), :].astype(BF16)


def retrieve(place, queries, passages, noise, readers, spread):
    count, width = queries.shape
    group = count // readers
    part = group // (PAIR * spread)
    shape = jax.ShapeDtypeStruct((spread, readers, part, width + LANES), BF16)
    spec = pl.BlockSpec((spread, STEP_GROUPS, part, width + LANES), lambda g, place: (0, g, 0, 0))
    rows = group * STEP_GROUPS
    return pl.pallas_call(
        functools.partial(retrieval_kernel, spread=spread),
        grid_spec=pltpu.PrefetchScalarGridSpec(
            num_scalar_prefetch=1,
            grid=(readers // STEP_GROUPS,),
            in_specs=[
                pl.BlockSpec((rows, width), lambda g, place: (g, 0)),
                pl.BlockSpec(passages.shape, lambda g, place: (0, 0)),
                pl.BlockSpec((rows, noise.shape[1]), lambda g, place: (g, 0)),
            ],
            out_specs=[spec, spec],
            scratch_shapes=[pltpu.VMEM((rows, width + LANES), F32)],
        ),
        out_shape=[shape, shape],
        compiler_params=pltpu.CompilerParams(vmem_limit_bytes=WIDE_BYTES),
        cost_estimate=pl.CostEstimate(
            flops=4 * count * width * passages.shape[0],
            bytes_accessed=2 * (2 * count * width + passages.size + noise.size),
            transcendentals=3 * noise.size,
        ),
        name="retrieve",
    )(place, queries, passages, noise)


def store_rows(out, tiles, shift, total, note=None):
    for at, tile in enumerate(tiles):
        out[..., at * LANES : (at + 1) * LANES] = tile.astype(BF16).reshape(out.shape[:-1] + (LANES,))
    tail = pack_tail(shift, total)
    if note is not None:
        tail = tail + note
    out[..., len(tiles) * LANES :] = tail.astype(BF16).reshape(out.shape[:-1] + (LANES,))


def pair_kernel(place, keep, recv, *outs):
    for offset, out in enumerate(outs):
        column = lax.bitwise_xor(place[1], offset)
        store_rows(out, *merge_rows([flat(keep[column]), flat(recv[column])]))


def merge_pair(place, keep, recv, spread):
    readers = keep.shape[1]
    spec = pl.BlockSpec((spread, readers // 2) + keep.shape[2:], lambda g, place: (0, g, 0, 0))
    out = pl.BlockSpec((readers // 2,) + keep.shape[2:], lambda g, place: (g, 0, 0))
    return pl.pallas_call(
        pair_kernel,
        grid_spec=pltpu.PrefetchScalarGridSpec(
            num_scalar_prefetch=1, grid=(2,), in_specs=[spec, spec], out_specs=[out] * spread
        ),
        out_shape=[jax.ShapeDtypeStruct(keep.shape[1:], BF16)] * spread,
        compiler_params=grant(),
        name="merge_pair",
    )(place, keep, recv)


def column_kernel(note, *refs):
    *parts, out = refs
    store_rows(out, *merge_rows([flat(part[...]) for part in parts]), note[...])


def merge_columns(note, parts):
    readers = parts[0].shape[0]
    spec = pl.BlockSpec((readers // 2,) + parts[0].shape[1:], lambda g: (g, 0, 0))
    return pl.pallas_call(
        column_kernel,
        grid=(2,),
        in_specs=[pl.BlockSpec(note.shape, lambda g: (0, 0))] + [spec] * len(parts),
        out_specs=spec,
        out_shape=jax.ShapeDtypeStruct(parts[0].shape, BF16),
        compiler_params=grant(),
        name="merge_columns",
    )(note, *parts)


def condition_kernel(place, parts, mix_weight, answers, keep, send, rows_scratch, *, spread):
    tiles, _, total = merge_rows([parts[at] for at in range(parts.shape[0])])
    blended_half = jnp.concatenate([(tile / total).astype(BF16) for tile in tiles], 1)
    part = blended_half.shape[0]
    start = pl.multiple_of((place[1] * PAIR + place[0]) * part, part)
    answer = answers[pl.ds(start, part), :].astype(F32)
    rows_scratch[...] = answer + jnp.dot(blended_half, mix_weight[...], preferred_element_type=F32)
    stride = keep.shape[1] // spread
    for column in range(spread):
        mine = pl.multiple_of((column * PAIR + place[0]) * stride, stride)
        other = pl.multiple_of((column * PAIR + 1 - place[0]) * stride, stride)
        keep[:, column * stride : (column + 1) * stride] = rows_scratch[:, pl.ds(mine, stride)].astype(BF16)
        send[:, column * stride : (column + 1) * stride] = rows_scratch[:, pl.ds(other, stride)].astype(BF16)


def condition(place, parts, mix_weight, answers, spread):
    model_width = mix_weight.shape[1]
    shape = jax.ShapeDtypeStruct((parts.shape[1], model_width // PAIR), BF16)
    whole = pl.BlockSpec(memory_space=pltpu.VMEM)
    return pl.pallas_call(
        functools.partial(condition_kernel, spread=spread),
        in_specs=[pl.BlockSpec(memory_space=pltpu.SMEM), whole, whole, whole],
        out_specs=[whole, whole],
        out_shape=[shape, shape],
        scratch_shapes=[pltpu.VMEM((parts.shape[1], model_width), F32)],
        compiler_params=grant(),
        name="condition",
    )(place, parts, mix_weight, answers)


def project_kernel(place, states, *refs):
    spread = len(refs) // 2 - 1
    keys, values = refs[-2:]
    width = keys.shape[1] // spread
    for column in range(spread):
        key = jnp.dot(states[...], refs[column][...], preferred_element_type=F32)
        keys[:, column * width : (column + 1) * width] = key.astype(BF16)
        value = jnp.dot(states[...], refs[spread + column][...], preferred_element_type=F32)
        values[column * width : (column + 1) * width, :] = value.astype(BF16).T


def project(place, states, key_weight, value_weight, spread):
    rows, model_width = states.shape
    width = model_width // (PAIR * spread)
    chunk = rows // PROJECT_STEPS

    def weight_spec(column):
        return pl.BlockSpec((model_width, width), lambda t, place: (0, column * PAIR + place[0]))

    specs = [weight_spec(column) for column in range(spread)]
    return pl.pallas_call(
        project_kernel,
        grid_spec=pltpu.PrefetchScalarGridSpec(
            num_scalar_prefetch=1,
            grid=(PROJECT_STEPS,),
            in_specs=[pl.BlockSpec((chunk, model_width), lambda t, place: (t, 0))] + specs + specs,
            out_specs=[
                pl.BlockSpec((chunk, spread * width), lambda t, place: (t, 0)),
                pl.BlockSpec((spread * width, chunk), lambda t, place: (0, t)),
            ],
        ),
        out_shape=[
            jax.ShapeDtypeStruct((rows, spread * width), BF16),
            jax.ShapeDtypeStruct((spread * width, rows), BF16),
        ],
        compiler_params=grant(),
        cost_estimate=pl.CostEstimate(
            flops=4 * rows * model_width * spread * width,
            bytes_accessed=2 * (2 * model_width * spread * width + 2 * rows * model_width),
            transcendentals=0,
        ),
        name="project",
    )(place, states, *([key_weight] * spread), *([value_weight] * spread))


def attend_group(z, place, table, pieces, keys, values, out, row, offset, column, inner, tokens, head_width):
    relative = lax.bitwise_xor(z, place[3])
    spread, rows = pieces.shape[0], out.shape[2]
    width = out.shape[1] - STAT_ROWS
    count = width // head_width
    left = pl.multiple_of(lax.bitwise_xor(place[1], column) * width, width)
    quarters = []
    for lane in range(spread):
        for core in range(PAIR):
            lead = (lax.bitwise_xor(place[1], lane), relative, lax.bitwise_xor(place[0], core))
            quarters.append(pieces[lead + (slice(None), pl.ds(left, width))])
    query = jnp.concatenate(quarters, 0).T
    head_at = lax.broadcasted_iota(jnp.int32, query.shape, 0) // head_width
    spaced = jnp.concatenate([jnp.where(head_at == head, query, jnp.zeros_like(query)) for head in range(count)], 1)
    entry = z * inner + lax.bitwise_xor(place[2], offset)
    bundle = min(HEAD_BUNDLE, count)
    shelves = []
    for shelf in range(PAIR):
        starts = [
            pl.multiple_of(table[entry * 6 + shelf * 3 + at] * tokens, tokens) for at in range(2)
        ]
        scores = [
            jnp.dot(keys[shelf][pl.ds(start, tokens), pl.ds(left, width)], spaced, preferred_element_type=F32)
            for start in starts
        ]
        high = functools.reduce(jnp.maximum, [jnp.max(score, 0, keepdims=True) for score in scores])
        exponents = [jnp.exp(score - high) for score in scores]
        total = sum(jnp.sum(exponent, 0, keepdims=True) for exponent in exponents)
        probs = jnp.concatenate([exponent.astype(BF16) for exponent in exponents], 0)
        there = table[entry * 6 + shelf * 3 + 2] > 0
        blocks = []
        for first in range(0, count, bundle):
            top = pl.multiple_of(left + first * head_width, bundle * head_width)
            value = jnp.concatenate(
                [values[shelf][pl.ds(top, bundle * head_width), pl.ds(start, tokens)] for start in starts], 1
            )
            mixed = jnp.dot(value, probs[:, first * rows : (first + bundle) * rows], preferred_element_type=F32)
            for head in range(bundle):
                blocks.append(
                    mixed[head * head_width : (head + 1) * head_width, head * rows : (head + 1) * rows]
                )
        shelves.append((jnp.where(there, high, FLOOR), jnp.where(there, total, 0.0), blocks, there))
    high = functools.reduce(jnp.maximum, [shelf[0] for shelf in shelves])
    factors = [jnp.where(there, jnp.exp(shelf_high - high), 0.0) for shelf_high, _, _, there in shelves]
    total = sum(shelf[1] * factor for shelf, factor in zip(shelves, factors))
    for head in range(count):
        here = slice(head * rows, (head + 1) * rows)
        joined = sum(shelf[2][head] * factor[:, here] for shelf, factor in zip(shelves, factors))
        out[row, head * head_width : (head + 1) * head_width, :] = joined.astype(BF16)
    out[row, width:, :] = pack_stats(high, total, count, rows)


def attend_kernel(place, table, pieces, key_own, key_pair, value_own, value_pair, out, **fixed):
    step = out.shape[0]
    for row in range(step):
        z = pl.program_id(0) * step + row
        attend_group(z, place, table, pieces, (key_own, key_pair), (value_own, value_pair), out, row, **fixed)


def pack_stats(high, total, count, rows):
    places = lax.broadcasted_iota(jnp.int32, (STAT_ROWS, rows), 0)
    packed = jnp.zeros((STAT_ROWS, rows), F32)
    for head in range(count):
        here = slice(head * rows, (head + 1) * rows)
        for at, term in enumerate(thirds(high[:, here]) + thirds(total[:, here])):
            packed = jnp.where(places == head * 6 + at, term, packed)
    return packed.astype(BF16)


def attend(place, table, pieces, keys, values, offset, column, inner, tokens, head_width):
    spread, outer, pair, part, half = pieces.shape
    width = half // spread
    rows = spread * pair * part
    at_once = min(ATTEND_GROUPS, outer)
    whole = pl.BlockSpec(memory_space=pltpu.VMEM)
    return pl.pallas_call(
        functools.partial(
            attend_kernel, offset=offset, column=column, inner=inner, tokens=tokens, head_width=head_width
        ),
        grid_spec=pltpu.PrefetchScalarGridSpec(
            num_scalar_prefetch=2,
            grid=(outer // at_once,),
            in_specs=[whole] * 5,
            out_specs=pl.BlockSpec((at_once, width + STAT_ROWS, rows), lambda z, place, table: (z, 0, 0)),
        ),
        out_shape=jax.ShapeDtypeStruct((outer, width + STAT_ROWS, rows), BF16),
        compiler_params=grant(),
        cost_estimate=pl.CostEstimate(
            flops=outer * 4 * 4 * rows * tokens * width * (width // head_width),
            bytes_accessed=outer * 2 * (width + STAT_ROWS) * rows,
            transcendentals=outer * 4 * rows * tokens * (width // head_width),
        ),
        name="attend",
    )(place, table, pieces, *keys, *values)


def unpack_stats(packed, width, count):
    tail = packed[width:, :].astype(F32)
    highs, totals = [], []
    for head in range(count):
        base = head * 6
        highs.append(tail[base : base + 1] + tail[base + 1 : base + 2] + tail[base + 2 : base + 3])
        totals.append(tail[base + 3 : base + 4] + tail[base + 4 : base + 5] + tail[base + 5 : base + 6])
    return highs, totals


def merge_heads(parts, width, head_width):
    count = width // head_width
    stats = [unpack_stats(part, width, count) for part in parts]
    mixes, highs, totals = [], [], []
    for head in range(count):
        high = functools.reduce(jnp.maximum, [stat[0][head] for stat in stats])
        mixed, total = 0.0, 0.0
        for part, stat in zip(parts, stats):
            factor = jnp.where(stat[1][head] > 0, jnp.exp(stat[0][head] - high), 0.0)
            total = total + stat[1][head] * factor
            mixed = mixed + part[head * head_width : (head + 1) * head_width, :].astype(F32) * factor
        mixes.append(mixed)
        highs.append(high)
        totals.append(total)
    return mixes, highs, totals


def gather_kernel(place, *refs, inner, spread, head_width):
    *parts, out = refs
    width = out.shape[2] - STAT_ROWS
    rows = out.shape[3]
    count = width // head_width
    for offset in range(inner):
        taken = [parts[offset * spread + column][0] for column in range(spread)]
        mixes, highs, totals = merge_heads(taken, width, head_width)
        target = lax.bitwise_xor(place[2], offset)
        for head in range(count):
            out[0, target, head * head_width : (head + 1) * head_width, :] = mixes[head].astype(BF16)
        out[0, target, width:, :] = pack_stats(
            jnp.concatenate(highs, 1), jnp.concatenate(totals, 1), count, rows
        )


def merge_lots(place, parts, inner, spread, head_width):
    outer, height, rows = parts[0].shape
    spec = pl.BlockSpec((1, height, rows), lambda z, place: (z, 0, 0))
    return pl.pallas_call(
        functools.partial(gather_kernel, inner=inner, spread=spread, head_width=head_width),
        grid_spec=pltpu.PrefetchScalarGridSpec(
            num_scalar_prefetch=1,
            grid=(outer,),
            in_specs=[spec] * len(parts),
            out_specs=pl.BlockSpec((1, inner, height, rows), lambda z, place: (z, 0, 0, 0)),
        ),
        out_shape=jax.ShapeDtypeStruct((outer, inner, height, rows), BF16),
        compiler_params=grant(),
        name="merge_lots",
    )(place, *parts)


def finish_kernel(parts, out, *, head_width):
    width = parts.shape[1] - STAT_ROWS
    mixes, _, totals = merge_heads([parts[at] for at in range(parts.shape[0])], width, head_width)
    done = jnp.concatenate([mixed / total for mixed, total in zip(mixes, totals)], 0)
    out[...] = done.T.astype(BF16)


def finish(parts, head_width):
    whole = pl.BlockSpec(memory_space=pltpu.VMEM)
    return pl.pallas_call(
        functools.partial(finish_kernel, head_width=head_width),
        in_specs=[whole],
        out_specs=whole,
        out_shape=jax.ShapeDtypeStruct((parts.shape[2], parts.shape[1] - STAT_ROWS), BF16),
        compiler_params=grant(),
        name="finish",
    )(parts)


def local(
    queries,
    passages,
    noise,
    mix_weight,
    answer_queries,
    key_weight,
    value_weight,
    token_states,
    block_owner,
    listed,
):
    readers = lax.axis_size("pb")
    runners = lax.axis_size("pa")
    group = lax.axis_index("pb")
    runner = lax.axis_index("pa")
    spread = runners // PAIR
    inner = 1
    while (2 * inner) * (2 * inner) <= readers:
        inner *= 2
    outer = readers // inner
    model_width = key_weight.shape[0]
    head_width = model_width // HEADS
    slots, tokens = token_states.shape[:2]
    place = jnp.stack([runner % PAIR, runner // PAIR, group % inner, group // inner]).astype(jnp.int32)

    def swap(value, axis, bits):
        size = lax.axis_size(axis)
        return lax.ppermute(value, axis, [(at, at ^ bits) for at in range(size)])

    states = token_states.reshape(slots * tokens, model_width)
    pair_states = swap(states, "pa", 1)

    keep, send = retrieve(place, queries, passages, noise, readers, spread)
    wanted = jnp.take(block_owner, listed[0], axis=0)
    digits = jnp.concatenate([wanted // LANES, wanted % LANES]).astype(F32)
    note = jnp.pad(digits[None], ((0, 0), (NOTE_AT, LANES - NOTE_AT - digits.shape[0])))
    by_column = merge_pair(place, keep, swap(send, "pa", 1), spread)
    *by_column, states = lax.optimization_barrier((*by_column, states))
    parts = [by_column[0]] + [swap(by_column[at], "pa", at * PAIR) for at in range(1, spread)]
    own_key, own_value = project(place, states, key_weight, value_weight, spread)
    *parts, own_key, own_value = lax.optimization_barrier((*parts, own_key, own_value))
    by_group = merge_columns(note, parts)
    by_group, pair_states = lax.optimization_barrier((by_group, pair_states))
    mine = lax.all_to_all(by_group, "pb", split_axis=0, concat_axis=0, tiled=True)
    pair_key, pair_value = project(place, pair_states, key_weight, value_weight, spread)
    mine, pair_key, pair_value = lax.optimization_barrier((mine, pair_key, pair_value))
    keys, values = (own_key, pair_key), (own_value, pair_value)
    kept, sent = condition(place, mine, mix_weight, answer_queries, spread)

    digits = mine[:, 0, queries.shape[1] + NOTE_AT :][:, : digits.shape[0]].astype(jnp.int32)
    slot_ids = digits[:, : wanted.shape[0]] * LANES + digits[:, wanted.shape[0] :]
    held = slot_ids // slots == runner * readers + group
    inside = slot_ids % slots
    chosen = jnp.stack(
        [
            jnp.min(jnp.where(held, inside, slots - 1), 1),
            jnp.max(jnp.where(held, inside, 0), 1),
            jnp.any(held, 1).astype(jnp.int32),
        ],
        1,
    )
    table = jnp.concatenate([chosen, swap(chosen, "pa", 1)], 1).reshape(-1)

    pieces = jnp.stack([kept, swap(sent, "pa", 1)])[None]
    step = inner
    while step < readers:
        pieces = jnp.concatenate([pieces, swap(pieces, "pb", step)], 0)
        step *= 2
    pieces = jnp.stack([pieces] + [swap(pieces, "pa", at * PAIR) for at in range(1, spread)])
    lots = []
    for offset in range(inner):
        query = pieces if offset == 0 else swap(pieces, "pb", offset)
        own = []
        for column in reversed(range(spread)):
            lot = attend(place, table, query, keys, values, offset, column, inner, tokens, head_width)
            own.append(lot if column == 0 else swap(lot, "pa", column * PAIR))
        lots += own[::-1]
    merged = merge_lots(place, lots, inner, spread, head_width)
    merged = merged.reshape((readers,) + merged.shape[2:])
    return finish(lax.all_to_all(merged, "pb", split_axis=0, concat_axis=0, tiled=True), head_width)


def solution(mesh):
    return jax.shard_map(
        local,
        mesh=mesh,
        in_specs=(
            P(),
            P(("pa", "pb"), None),
            P(None, ("pa", "pb")),
            P(),
            P("pb", None),
            P(),
            P(),
            P(("pa", "pb"), None, None),
            P(),
            P("pb", "pa"),
        ),
        out_specs=P("pb", "pa"),
        check_vma=False,
    )
```

```python
import functools

import jax
import jax.numpy as jnp
from jax import lax
from jax.experimental import pallas as pl
from jax.experimental.pallas import tpu as pltpu
from jax.sharding import PartitionSpec as P

HEADS = 16
PAIR = 2
TEMPER = 0.5
FLOOR = -1e30
LANES = 128
STAT_ROWS = 32
NOTE_AT = 6
STEP_GROUPS = 2
PROJECT_STEPS = 4
ATTEND_GROUPS = 4
HEAD_BUNDLE = 2
VMEM_BYTES = 16 * 1024 * 1024
WIDE_BYTES = 24 * 1024 * 1024
F32 = jnp.float32
BF16 = jnp.bfloat16
NT = (((1,), (1,)), ((), ()))
SCALARS = pl.BlockSpec(memory_space=pltpu.SMEM)


def grant():
    return pltpu.CompilerParams(vmem_limit_bytes=VMEM_BYTES)


def thirds(value):
    first = value.astype(BF16).astype(F32)
    rest = value - first
    second = rest.astype(BF16).astype(F32)
    return first, second, rest - second


def pack_tail(shift, total):
    lane = lax.broadcasted_iota(jnp.int32, (shift.shape[0], LANES), 1)
    tail = jnp.zeros((shift.shape[0], LANES), F32)
    for at, term in enumerate(thirds(shift) + thirds(total)):
        tail = jnp.where(lane == at, term, tail)
    return tail


def unpack_tail(tail):
    term = lax.broadcasted_iota(jnp.int32, (LANES, 2 * LANES), 0)
    half = lax.broadcasted_iota(jnp.int32, (LANES, 2 * LANES), 1) // LANES
    pick = jnp.where(term // 3 == half, 1.0, 0.0).astype(BF16)
    both = jnp.dot(tail, pick, preferred_element_type=F32)
    return both[:, :LANES], both[:, LANES:]


def merge_rows(parts):
    width = parts[0].shape[1] - LANES
    stats = [unpack_tail(part[:, width:]) for part in parts]
    shift = functools.reduce(jnp.maximum, [stat[0] for stat in stats])
    factors = [jnp.exp(stat[0] - shift) for stat in stats]
    total = sum(stat[1] * factor for stat, factor in zip(stats, factors))
    tiles = [
        sum(part[:, at : at + LANES].astype(F32) * factor for part, factor in zip(parts, factors))
        for at in range(0, width, LANES)
    ]
    return tiles, shift, total


def flat(value):
    return value.reshape((-1, value.shape[-1]))


def retrieval_kernel(place, queries, passages, noise, keep, send, rows_scratch, *, spread):
    core = place[0]
    groups, part = keep.shape[1:3]
    width = queries.shape[1]
    logits = lax.dot_general(queries[...], passages[...], NT, preferred_element_type=F32)
    gumbel = -jnp.log(-jnp.log(noise[...].astype(F32)))
    scores = (logits * width ** (-0.5) + gumbel) * (1 / TEMPER)
    shift = jnp.max(scores, 1, keepdims=True)
    weight = jnp.exp(scores - shift)
    total = jnp.sum(weight, 1, keepdims=True)
    rows_scratch[:, :width] = jnp.dot(weight.astype(BF16), passages[...], preferred_element_type=F32)
    rows_scratch[:, width:] = pack_tail(shift, total)
    for at in range(groups):
        for column in range(spread):
            base = (at * spread + column) * PAIR
            mine = pl.multiple_of((base + core) * part, part)
            other = pl.multiple_of((base + 1 - core) * part, part)
            keep[column, at] = rows_scratch[pl.ds(mine, part), :].astype(BF16)
            send[column, at] = rows_scratch[pl.ds(other, part), :].astype(BF16)


def retrieve(place, queries, passages, noise, readers, spread):
    count, width = queries.shape
    group = count // readers
    part = group // (PAIR * spread)
    shape = jax.ShapeDtypeStruct((spread, readers, part, width + LANES), BF16)
    spec = pl.BlockSpec((spread, STEP_GROUPS, part, width + LANES), lambda g, place: (0, g, 0, 0))
    rows = group * STEP_GROUPS
    return pl.pallas_call(
        functools.partial(retrieval_kernel, spread=spread),
        grid_spec=pltpu.PrefetchScalarGridSpec(
            num_scalar_prefetch=1,
            grid=(readers // STEP_GROUPS,),
            in_specs=[
                pl.BlockSpec((rows, width), lambda g, place: (g, 0)),
                pl.BlockSpec(passages.shape, lambda g, place: (0, 0)),
                pl.BlockSpec((rows, noise.shape[1]), lambda g, place: (g, 0)),
            ],
            out_specs=[spec, spec],
            scratch_shapes=[pltpu.VMEM((rows, width + LANES), F32)],
        ),
        out_shape=[shape, shape],
        compiler_params=pltpu.CompilerParams(vmem_limit_bytes=WIDE_BYTES),
        cost_estimate=pl.CostEstimate(
            flops=4 * count * width * passages.shape[0],
            bytes_accessed=2 * (2 * count * width + passages.size + noise.size),
            transcendentals=3 * noise.size,
        ),
        name="retrieve",
    )(place, queries, passages, noise)


def store_rows(out, tiles, shift, total, note=None):
    for at, tile in enumerate(tiles):
        out[..., at * LANES : (at + 1) * LANES] = tile.astype(BF16).reshape(out.shape[:-1] + (LANES,))
    tail = pack_tail(shift, total)
    if note is not None:
        tail = tail + note
    out[..., len(tiles) * LANES :] = tail.astype(BF16).reshape(out.shape[:-1] + (LANES,))


def hand_on(place, out):
    for at in range(out.shape[0]):
        out[at] = place[at]


def pair_kernel(place, keep, recv, *outs):
    *outs, later = outs
    hand_on(place, later)
    for offset, out in enumerate(outs):
        column = lax.bitwise_xor(place[1], offset)
        store_rows(out, *merge_rows([flat(keep[column]), flat(recv[column])]))


def merge_pair(place, keep, recv, spread):
    readers = keep.shape[1]
    spec = pl.BlockSpec((spread, readers // 2) + keep.shape[2:], lambda g, place: (0, g, 0, 0))
    out = pl.BlockSpec((readers // 2,) + keep.shape[2:], lambda g, place: (g, 0, 0))
    return pl.pallas_call(
        pair_kernel,
        grid_spec=pltpu.PrefetchScalarGridSpec(
            num_scalar_prefetch=1, grid=(2,), in_specs=[spec, spec], out_specs=[out] * spread + [SCALARS]
        ),
        out_shape=[jax.ShapeDtypeStruct(keep.shape[1:], BF16)] * spread
        + [jax.ShapeDtypeStruct(place.shape, place.dtype)],
        compiler_params=grant(),
        name="merge_pair",
    )(place, keep, recv)


def column_kernel(place, note, done, *refs):
    *parts, out, later = refs
    hand_on(place, later)
    store_rows(out, *merge_rows([flat(part[...]) for part in parts]), note[...] + done[0:1, :])


def merge_columns(place, note, done, parts):
    readers = parts[0].shape[0]
    spec = pl.BlockSpec((readers // 2,) + parts[0].shape[1:], lambda g, place: (g, 0, 0))
    return pl.pallas_call(
        column_kernel,
        grid_spec=pltpu.PrefetchScalarGridSpec(
            num_scalar_prefetch=1,
            grid=(2,),
            in_specs=[
                pl.BlockSpec(note.shape, lambda g, place: (0, 0)),
                pl.BlockSpec(done.shape, lambda g, place: (0, 0)),
            ]
            + [spec] * len(parts),
            out_specs=[spec, SCALARS],
        ),
        out_shape=[
            jax.ShapeDtypeStruct(parts[0].shape, BF16),
            jax.ShapeDtypeStruct(place.shape, place.dtype),
        ],
        compiler_params=grant(),
        name="merge_columns",
    )(place, note, done, *parts)


def condition_kernel(place, parts, mix_weight, answers, done, keep, send, rows_scratch, *, spread):
    tiles, _, total = merge_rows([parts[at] for at in range(parts.shape[0])])
    blended_half = jnp.concatenate([(tile / total).astype(BF16) for tile in tiles], 1)
    part = blended_half.shape[0]
    start = pl.multiple_of((place[1] * PAIR + place[0]) * part, part)
    answer = answers[pl.ds(start, part), :].astype(F32)
    rows_scratch[...] = answer + jnp.dot(blended_half, mix_weight[...], preferred_element_type=F32)
    stride = keep.shape[1] // spread
    for column in range(spread):
        mine = pl.multiple_of((column * PAIR + place[0]) * stride, stride)
        other = pl.multiple_of((column * PAIR + 1 - place[0]) * stride, stride)
        keep[:, column * stride : (column + 1) * stride] = rows_scratch[:, pl.ds(mine, stride)].astype(BF16)
        send[:, column * stride : (column + 1) * stride] = rows_scratch[:, pl.ds(other, stride)].astype(BF16)


def condition(place, parts, mix_weight, answers, done, spread):
    model_width = mix_weight.shape[1]
    shape = jax.ShapeDtypeStruct((parts.shape[1], model_width // PAIR), BF16)
    whole = pl.BlockSpec(memory_space=pltpu.VMEM)
    return pl.pallas_call(
        functools.partial(condition_kernel, spread=spread),
        in_specs=[SCALARS, whole, whole, whole, whole],
        out_specs=[whole, whole],
        out_shape=[shape, shape],
        scratch_shapes=[pltpu.VMEM((parts.shape[1], model_width), F32)],
        compiler_params=grant(),
        name="condition",
    )(place, parts, mix_weight, answers, done)


def project_kernel(place, states, *refs):
    spread = (len(refs) - 3) // 2
    keys, values, done = refs[-3:]
    done[...] = jnp.zeros_like(done)
    width = keys.shape[1] // spread
    for column in range(spread):
        key = jnp.dot(states[...], refs[column][...], preferred_element_type=F32)
        keys[:, column * width : (column + 1) * width] = key.astype(BF16)
        value = jnp.dot(states[...], refs[spread + column][...], preferred_element_type=F32)
        values[column * width : (column + 1) * width, :] = value.astype(BF16).T


def project(place, states, key_weight, value_weight, spread):
    rows, model_width = states.shape
    width = model_width // (PAIR * spread)
    chunk = rows // PROJECT_STEPS

    def weight_spec(column):
        return pl.BlockSpec((model_width, width), lambda t, place: (0, column * PAIR + place[0]))

    specs = [weight_spec(column) for column in range(spread)]
    return pl.pallas_call(
        project_kernel,
        grid_spec=pltpu.PrefetchScalarGridSpec(
            num_scalar_prefetch=1,
            grid=(PROJECT_STEPS,),
            in_specs=[pl.BlockSpec((chunk, model_width), lambda t, place: (t, 0))] + specs + specs,
            out_specs=[
                pl.BlockSpec((chunk, spread * width), lambda t, place: (t, 0)),
                pl.BlockSpec((spread * width, chunk), lambda t, place: (0, t)),
                pl.BlockSpec((8, LANES), lambda t, place: (0, 0)),
            ],
        ),
        out_shape=[
            jax.ShapeDtypeStruct((rows, spread * width), BF16),
            jax.ShapeDtypeStruct((spread * width, rows), BF16),
            jax.ShapeDtypeStruct((8, LANES), F32),
        ],
        compiler_params=grant(),
        cost_estimate=pl.CostEstimate(
            flops=4 * rows * model_width * spread * width,
            bytes_accessed=2 * (2 * model_width * spread * width + 2 * rows * model_width),
            transcendentals=0,
        ),
        name="project",
    )(place, states, *([key_weight] * spread), *([value_weight] * spread))


def attend_group(z, place, table, pieces, keys, values, out, row, offset, column, inner, tokens, head_width):
    relative = lax.bitwise_xor(z, place[3])
    spread, rows = pieces.shape[0], out.shape[2]
    width = out.shape[1] - STAT_ROWS
    count = width // head_width
    left = pl.multiple_of(lax.bitwise_xor(place[1], column) * width, width)
    quarters = []
    for lane in range(spread):
        for core in range(PAIR):
            lead = (lax.bitwise_xor(place[1], lane), relative, lax.bitwise_xor(place[0], core))
            quarters.append(pieces[lead + (slice(None), pl.ds(left, width))])
    query = jnp.concatenate(quarters, 0).T
    head_at = lax.broadcasted_iota(jnp.int32, query.shape, 0) // head_width
    spaced = jnp.concatenate([jnp.where(head_at == head, query, jnp.zeros_like(query)) for head in range(count)], 1)
    entry = z * inner + lax.bitwise_xor(place[2], offset)
    bundle = min(HEAD_BUNDLE, count)
    shelves = []
    for shelf in range(PAIR):
        starts = [
            pl.multiple_of(table[entry * 6 + shelf * 3 + at] * tokens, tokens) for at in range(2)
        ]
        scores = [
            jnp.dot(keys[shelf][pl.ds(start, tokens), pl.ds(left, width)], spaced, preferred_element_type=F32)
            for start in starts
        ]
        high = functools.reduce(jnp.maximum, [jnp.max(score, 0, keepdims=True) for score in scores])
        exponents = [jnp.exp(score - high) for score in scores]
        total = sum(jnp.sum(exponent, 0, keepdims=True) for exponent in exponents)
        probs = jnp.concatenate([exponent.astype(BF16) for exponent in exponents], 0)
        there = table[entry * 6 + shelf * 3 + 2] > 0
        blocks = []
        for first in range(0, count, bundle):
            top = pl.multiple_of(left + first * head_width, bundle * head_width)
            value = jnp.concatenate(
                [values[shelf][pl.ds(top, bundle * head_width), pl.ds(start, tokens)] for start in starts], 1
            )
            mixed = jnp.dot(value, probs[:, first * rows : (first + bundle) * rows], preferred_element_type=F32)
            for head in range(bundle):
                blocks.append(
                    mixed[head * head_width : (head + 1) * head_width, head * rows : (head + 1) * rows]
                )
        shelves.append((jnp.where(there, high, FLOOR), jnp.where(there, total, 0.0), blocks, there))
    high = functools.reduce(jnp.maximum, [shelf[0] for shelf in shelves])
    factors = [jnp.where(there, jnp.exp(shelf_high - high), 0.0) for shelf_high, _, _, there in shelves]
    total = sum(shelf[1] * factor for shelf, factor in zip(shelves, factors))
    for head in range(count):
        here = slice(head * rows, (head + 1) * rows)
        joined = sum(shelf[2][head] * factor[:, here] for shelf, factor in zip(shelves, factors))
        out[row, head * head_width : (head + 1) * head_width, :] = joined.astype(BF16)
    out[row, width:, :] = pack_stats(high, total, count, rows)


def attend_kernel(place, table, pieces, key_own, key_pair, value_own, value_pair, out, **fixed):
    step = out.shape[0]
    for row in range(step):
        z = pl.program_id(0) * step + row
        attend_group(z, place, table, pieces, (key_own, key_pair), (value_own, value_pair), out, row, **fixed)


def pack_stats(high, total, count, rows):
    places = lax.broadcasted_iota(jnp.int32, (STAT_ROWS, rows), 0)
    packed = jnp.zeros((STAT_ROWS, rows), F32)
    for head in range(count):
        here = slice(head * rows, (head + 1) * rows)
        for at, term in enumerate(thirds(high[:, here]) + thirds(total[:, here])):
            packed = jnp.where(places == head * 6 + at, term, packed)
    return packed.astype(BF16)


def attend(place, table, pieces, keys, values, offset, column, inner, tokens, head_width):
    spread, outer, pair, part, half = pieces.shape
    width = half // spread
    rows = spread * pair * part
    at_once = min(ATTEND_GROUPS, outer)
    whole = pl.BlockSpec(memory_space=pltpu.VMEM)
    return pl.pallas_call(
        functools.partial(
            attend_kernel, offset=offset, column=column, inner=inner, tokens=tokens, head_width=head_width
        ),
        grid_spec=pltpu.PrefetchScalarGridSpec(
            num_scalar_prefetch=2,
            grid=(outer // at_once,),
            in_specs=[whole] * 5,
            out_specs=pl.BlockSpec((at_once, width + STAT_ROWS, rows), lambda z, place, table: (z, 0, 0)),
        ),
        out_shape=jax.ShapeDtypeStruct((outer, width + STAT_ROWS, rows), BF16),
        compiler_params=grant(),
        cost_estimate=pl.CostEstimate(
            flops=outer * 4 * 4 * rows * tokens * width * (width // head_width),
            bytes_accessed=outer * 2 * (width + STAT_ROWS) * rows,
            transcendentals=outer * 4 * rows * tokens * (width // head_width),
        ),
        name="attend",
    )(place, table, pieces, *keys, *values)


def unpack_stats(packed, width, count):
    tail = packed[width:, :].astype(F32)
    highs, totals = [], []
    for head in range(count):
        base = head * 6
        highs.append(tail[base : base + 1] + tail[base + 1 : base + 2] + tail[base + 2 : base + 3])
        totals.append(tail[base + 3 : base + 4] + tail[base + 4 : base + 5] + tail[base + 5 : base + 6])
    return highs, totals


def merge_heads(parts, width, head_width):
    count = width // head_width
    stats = [unpack_stats(part, width, count) for part in parts]
    mixes, highs, totals = [], [], []
    for head in range(count):
        high = functools.reduce(jnp.maximum, [stat[0][head] for stat in stats])
        mixed, total = 0.0, 0.0
        for part, stat in zip(parts, stats):
            factor = jnp.where(stat[1][head] > 0, jnp.exp(stat[0][head] - high), 0.0)
            total = total + stat[1][head] * factor
            mixed = mixed + part[head * head_width : (head + 1) * head_width, :].astype(F32) * factor
        mixes.append(mixed)
        highs.append(high)
        totals.append(total)
    return mixes, highs, totals


def gather_kernel(place, *refs, inner, spread, head_width):
    *parts, out = refs
    width = out.shape[2] - STAT_ROWS
    rows = out.shape[3]
    count = width // head_width
    for offset in range(inner):
        taken = [parts[offset * spread + column][0] for column in range(spread)]
        mixes, highs, totals = merge_heads(taken, width, head_width)
        target = lax.bitwise_xor(place[2], offset)
        for head in range(count):
            out[0, target, head * head_width : (head + 1) * head_width, :] = mixes[head].astype(BF16)
        out[0, target, width:, :] = pack_stats(
            jnp.concatenate(highs, 1), jnp.concatenate(totals, 1), count, rows
        )


def merge_lots(place, parts, inner, spread, head_width):
    outer, height, rows = parts[0].shape
    spec = pl.BlockSpec((1, height, rows), lambda z, place: (z, 0, 0))
    return pl.pallas_call(
        functools.partial(gather_kernel, inner=inner, spread=spread, head_width=head_width),
        grid_spec=pltpu.PrefetchScalarGridSpec(
            num_scalar_prefetch=1,
            grid=(outer,),
            in_specs=[spec] * len(parts),
            out_specs=pl.BlockSpec((1, inner, height, rows), lambda z, place: (z, 0, 0, 0)),
        ),
        out_shape=jax.ShapeDtypeStruct((outer, inner, height, rows), BF16),
        compiler_params=grant(),
        name="merge_lots",
    )(place, *parts)


def finish_kernel(parts, out, *, head_width):
    width = parts.shape[1] - STAT_ROWS
    mixes, _, totals = merge_heads([parts[at] for at in range(parts.shape[0])], width, head_width)
    done = jnp.concatenate([mixed / total for mixed, total in zip(mixes, totals)], 0)
    out[...] = done.T.astype(BF16)


def finish(parts, head_width):
    whole = pl.BlockSpec(memory_space=pltpu.VMEM)
    return pl.pallas_call(
        functools.partial(finish_kernel, head_width=head_width),
        in_specs=[whole],
        out_specs=whole,
        out_shape=jax.ShapeDtypeStruct((parts.shape[2], parts.shape[1] - STAT_ROWS), BF16),
        compiler_params=grant(),
        name="finish",
    )(parts)


def local(
    queries,
    passages,
    noise,
    mix_weight,
    answer_queries,
    key_weight,
    value_weight,
    token_states,
    block_owner,
    listed,
):
    readers = lax.axis_size("pb")
    runners = lax.axis_size("pa")
    group = lax.axis_index("pb")
    runner = lax.axis_index("pa")
    spread = runners // PAIR
    inner = 1
    while (2 * inner) * (2 * inner) <= readers:
        inner *= 2
    outer = readers // inner
    model_width = key_weight.shape[0]
    head_width = model_width // HEADS
    slots, tokens = token_states.shape[:2]
    place = jnp.stack([runner % PAIR, runner // PAIR, group % inner, group // inner]).astype(jnp.int32)

    def swap(value, axis, bits):
        size = lax.axis_size(axis)
        return lax.ppermute(value, axis, [(at, at ^ bits) for at in range(size)])

    states = token_states.reshape(slots * tokens, model_width)
    pair_states = swap(states, "pa", 1)

    wanted = jnp.take(block_owner, listed[0], axis=0)
    wanted = jnp.concatenate([wanted, swap(wanted, "pa", 1)])
    digits = jnp.concatenate([wanted // LANES, wanted % LANES]).astype(F32)
    note = jnp.pad(digits[None], ((0, 0), (NOTE_AT, LANES - NOTE_AT - digits.shape[0])))
    keep, send = retrieve(place, queries, passages, noise, readers, spread)
    *by_column, place_own = merge_pair(place, keep, swap(send, "pa", 1), spread)
    parts = [by_column[0]] + [swap(by_column[at], "pa", at * PAIR) for at in range(1, spread)]
    own_key, own_value, own_done = project(place_own, states, key_weight, value_weight, spread)
    by_group, place_pair = merge_columns(place, note, own_done, parts)
    mine = lax.all_to_all(by_group, "pb", split_axis=0, concat_axis=0, tiled=True)
    pair_key, pair_value, pair_done = project(place_pair, pair_states, key_weight, value_weight, spread)
    keys, values = (own_key, pair_key), (own_value, pair_value)
    kept, sent = condition(place, mine, mix_weight, answer_queries, pair_done, spread)

    digits = mine[:, 0, queries.shape[1] + NOTE_AT :][:, : digits.shape[0]].astype(jnp.int32)
    slot_ids = digits[:, : wanted.shape[0]] * LANES + digits[:, wanted.shape[0] :]
    slot_ids = slot_ids.reshape(readers, PAIR, -1)
    holder = (runner ^ jnp.arange(PAIR, dtype=jnp.int32)) * readers + group
    held = slot_ids // slots == holder[None, :, None]
    inside = slot_ids % slots
    table = jnp.stack(
        [
            jnp.min(jnp.where(held, inside, slots - 1), 2),
            jnp.max(jnp.where(held, inside, 0), 2),
            jnp.any(held, 2).astype(jnp.int32),
        ],
        2,
    ).reshape(-1)

    pieces = jnp.stack([kept, swap(sent, "pa", 1)])[None]
    step = inner
    while step < readers:
        pieces = jnp.concatenate([pieces, swap(pieces, "pb", step)], 0)
        step *= 2
    own_pieces = pieces
    pieces = jnp.stack([pieces] + [swap(pieces, "pa", at * PAIR) for at in range(1, spread)])
    far = [pieces]
    for offset in range(1, inner):
        near = swap(own_pieces, "pb", offset)[None]
        far.append(jnp.concatenate([near, swap(pieces[1:], "pb", offset)], 0))
    lots = []
    for offset in range(inner):
        own = []
        for column in reversed(range(spread)):
            lot = attend(place, table, far[offset], keys, values, offset, column, inner, tokens, head_width)
            own.append(lot if column == 0 else swap(lot, "pa", column * PAIR))
        lots += own[::-1]
    merged = merge_lots(place, lots, inner, spread, head_width)
    merged = merged.reshape((readers,) + merged.shape[2:])
    return finish(lax.all_to_all(merged, "pb", split_axis=0, concat_axis=0, tiled=True), head_width)


def solution(mesh):
    return jax.shard_map(
        local,
        mesh=mesh,
        in_specs=(
            P(),
            P(("pa", "pb"), None),
            P(None, ("pa", "pb")),
            P(),
            P("pb", None),
            P(),
            P(),
            P(("pa", "pb"), None, None),
            P(),
            P("pb", "pa"),
        ),
        out_specs=P("pb", "pa"),
        check_vma=False,
    )
```

```python
import functools

import jax
import jax.numpy as jnp
from jax import lax
from jax.experimental import pallas as pl
from jax.experimental.pallas import tpu as pltpu
from jax.sharding import PartitionSpec as P

HEADS = 16
PAIR = 2
CAP = 2
TEMPER = 0.5
FLOOR = -1e30
LANES = 128
STAT_ROWS = 32
NOTE_AT = 6
STEP_GROUPS = 2
PROJECT_STEPS = 4
HEAD_BUNDLE = 2
VMEM_BYTES = 16 * 1024 * 1024
WIDE_BYTES = 60 * 1024 * 1024
F32 = jnp.float32
BF16 = jnp.bfloat16
NT = (((1,), (1,)), ((), ()))
SCALARS = pl.BlockSpec(memory_space=pltpu.SMEM)


def grant():
    return pltpu.CompilerParams(vmem_limit_bytes=VMEM_BYTES)


def thirds(value):
    first = value.astype(BF16).astype(F32)
    rest = value - first
    second = rest.astype(BF16).astype(F32)
    return first, second, rest - second


def pack_tail(shift, total):
    lane = lax.broadcasted_iota(jnp.int32, (shift.shape[0], LANES), 1)
    tail = jnp.zeros((shift.shape[0], LANES), F32)
    for at, term in enumerate(thirds(shift) + thirds(total)):
        tail = jnp.where(lane == at, term, tail)
    return tail


def unpack_tail(tail):
    term = lax.broadcasted_iota(jnp.int32, (LANES, 2 * LANES), 0)
    half = lax.broadcasted_iota(jnp.int32, (LANES, 2 * LANES), 1) // LANES
    pick = jnp.where(term // 3 == half, 1.0, 0.0).astype(BF16)
    both = jnp.dot(tail, pick, preferred_element_type=F32)
    return both[:, :LANES], both[:, LANES:]


def merge_rows(parts):
    width = parts[0].shape[1] - LANES
    stats = [unpack_tail(part[:, width:]) for part in parts]
    shift = functools.reduce(jnp.maximum, [stat[0] for stat in stats])
    factors = [jnp.exp(stat[0] - shift) for stat in stats]
    total = sum(stat[1] * factor for stat, factor in zip(stats, factors))
    tiles = [
        sum(part[:, at : at + LANES].astype(F32) * factor for part, factor in zip(parts, factors))
        for at in range(0, width, LANES)
    ]
    return tiles, shift, total


def flat(value):
    return value.reshape((-1, value.shape[-1]))


def retrieval_kernel(place, queries, passages, noise, keep, send, rows_scratch, *, spread):
    core = place[0]
    groups, part = keep.shape[1:3]
    width = queries.shape[1]
    logits = lax.dot_general(queries[...], passages[...], NT, preferred_element_type=F32)
    gumbel = -jnp.log(-jnp.log(noise[...].astype(F32)))
    scores = (logits * width ** (-0.5) + gumbel) * (1 / TEMPER)
    shift = jnp.max(scores, 1, keepdims=True)
    weight = jnp.exp(scores - shift)
    total = jnp.sum(weight, 1, keepdims=True)
    rows_scratch[:, :width] = jnp.dot(weight.astype(BF16), passages[...], preferred_element_type=F32)
    rows_scratch[:, width:] = pack_tail(shift, total)
    for at in range(groups):
        for column in range(spread):
            base = (at * spread + column) * PAIR
            mine = pl.multiple_of((base + core) * part, part)
            other = pl.multiple_of((base + 1 - core) * part, part)
            keep[column, at] = rows_scratch[pl.ds(mine, part), :].astype(BF16)
            send[column, at] = rows_scratch[pl.ds(other, part), :].astype(BF16)


def retrieve(place, queries, passages, noise, readers, spread):
    count, width = queries.shape
    group = count // readers
    part = group // (PAIR * spread)
    shape = jax.ShapeDtypeStruct((spread, readers, part, width + LANES), BF16)
    spec = pl.BlockSpec((spread, STEP_GROUPS, part, width + LANES), lambda g, place: (0, g, 0, 0))
    rows = group * STEP_GROUPS
    return pl.pallas_call(
        functools.partial(retrieval_kernel, spread=spread),
        grid_spec=pltpu.PrefetchScalarGridSpec(
            num_scalar_prefetch=1,
            grid=(readers // STEP_GROUPS,),
            in_specs=[
                pl.BlockSpec((rows, width), lambda g, place: (g, 0)),
                pl.BlockSpec(passages.shape, lambda g, place: (0, 0)),
                pl.BlockSpec((rows, noise.shape[1]), lambda g, place: (g, 0)),
            ],
            out_specs=[spec, spec],
            scratch_shapes=[pltpu.VMEM((rows, width + LANES), F32)],
        ),
        out_shape=[shape, shape],
        compiler_params=pltpu.CompilerParams(vmem_limit_bytes=WIDE_BYTES),
        cost_estimate=pl.CostEstimate(
            flops=4 * count * width * passages.shape[0],
            bytes_accessed=2 * (2 * count * width + passages.size + noise.size),
            transcendentals=3 * noise.size,
        ),
        name="retrieve",
    )(place, queries, passages, noise)


def store_rows(out, tiles, shift, total, note=None):
    for at, tile in enumerate(tiles):
        out[..., at * LANES : (at + 1) * LANES] = tile.astype(BF16).reshape(out.shape[:-1] + (LANES,))
    tail = pack_tail(shift, total)
    if note is not None:
        tail = tail + note
    out[..., len(tiles) * LANES :] = tail.astype(BF16).reshape(out.shape[:-1] + (LANES,))


def hand_on(place, out):
    for at in range(out.shape[0]):
        out[at] = place[at]


def pair_kernel(place, keep, recv, *outs):
    *outs, later = outs
    hand_on(place, later)
    for offset, out in enumerate(outs):
        column = lax.bitwise_xor(place[1], offset)
        store_rows(out, *merge_rows([flat(keep[column]), flat(recv[column])]))


def merge_pair(place, keep, recv, spread):
    readers = keep.shape[1]
    spec = pl.BlockSpec((spread, readers // 2) + keep.shape[2:], lambda g, place: (0, g, 0, 0))
    out = pl.BlockSpec((readers // 2,) + keep.shape[2:], lambda g, place: (g, 0, 0))
    return pl.pallas_call(
        pair_kernel,
        grid_spec=pltpu.PrefetchScalarGridSpec(
            num_scalar_prefetch=1, grid=(2,), in_specs=[spec, spec], out_specs=[out] * spread + [SCALARS]
        ),
        out_shape=[jax.ShapeDtypeStruct(keep.shape[1:], BF16)] * spread
        + [jax.ShapeDtypeStruct(place.shape, place.dtype)],
        compiler_params=grant(),
        name="merge_pair",
    )(place, keep, recv)


def column_kernel(place, note, done, *refs):
    *parts, out, later = refs
    hand_on(place, later)
    store_rows(out, *merge_rows([flat(part[...]) for part in parts]), note[...] + done[0:1, :])


def merge_columns(place, note, done, parts):
    readers = parts[0].shape[0]
    spec = pl.BlockSpec((readers // 2,) + parts[0].shape[1:], lambda g, place: (g, 0, 0))
    return pl.pallas_call(
        column_kernel,
        grid_spec=pltpu.PrefetchScalarGridSpec(
            num_scalar_prefetch=1,
            grid=(2,),
            in_specs=[
                pl.BlockSpec(note.shape, lambda g, place: (0, 0)),
                pl.BlockSpec(done.shape, lambda g, place: (0, 0)),
            ]
            + [spec] * len(parts),
            out_specs=[spec, SCALARS],
        ),
        out_shape=[
            jax.ShapeDtypeStruct(parts[0].shape, BF16),
            jax.ShapeDtypeStruct(place.shape, place.dtype),
        ],
        compiler_params=grant(),
        name="merge_columns",
    )(place, note, done, *parts)


def condition_kernel(place, parts, mix_weight, answers, done, keep, send, rows_scratch, *, spread):
    tiles, _, total = merge_rows([parts[at] for at in range(parts.shape[0])])
    blended_half = jnp.concatenate([(tile / total).astype(BF16) for tile in tiles], 1)
    part = blended_half.shape[0]
    start = pl.multiple_of((place[1] * PAIR + place[0]) * part, part)
    answer = answers[pl.ds(start, part), :].astype(F32)
    rows_scratch[...] = answer + jnp.dot(blended_half, mix_weight[...], preferred_element_type=F32)
    stride = keep.shape[1] // spread
    for column in range(spread):
        mine = pl.multiple_of((column * PAIR + place[0]) * stride, stride)
        other = pl.multiple_of((column * PAIR + 1 - place[0]) * stride, stride)
        keep[:, column * stride : (column + 1) * stride] = rows_scratch[:, pl.ds(mine, stride)].astype(BF16)
        send[:, column * stride : (column + 1) * stride] = rows_scratch[:, pl.ds(other, stride)].astype(BF16)


def condition(place, parts, mix_weight, answers, done, spread):
    model_width = mix_weight.shape[1]
    shape = jax.ShapeDtypeStruct((parts.shape[1], model_width // PAIR), BF16)
    whole = pl.BlockSpec(memory_space=pltpu.VMEM)
    return pl.pallas_call(
        functools.partial(condition_kernel, spread=spread),
        in_specs=[SCALARS, whole, whole, whole, whole],
        out_specs=[whole, whole],
        out_shape=[shape, shape],
        scratch_shapes=[pltpu.VMEM((parts.shape[1], model_width), F32)],
        compiler_params=grant(),
        name="condition",
    )(place, parts, mix_weight, answers, done)


def project_kernel(place, states, *refs):
    spread = (len(refs) - 3) // 2
    keys, values, done = refs[-3:]
    done[...] = jnp.zeros_like(done)
    width = keys.shape[1] // spread
    for column in range(spread):
        key = jnp.dot(states[...], refs[column][...], preferred_element_type=F32)
        keys[:, column * width : (column + 1) * width] = key.astype(BF16)
        value = jnp.dot(states[...], refs[spread + column][...], preferred_element_type=F32)
        values[column * width : (column + 1) * width, :] = value.astype(BF16).T


def project(place, states, key_weight, value_weight, spread):
    rows, model_width = states.shape
    width = model_width // (PAIR * spread)
    chunk = rows // PROJECT_STEPS

    def weight_spec(column):
        return pl.BlockSpec((model_width, width), lambda t, place: (0, column * PAIR + place[0]))

    specs = [weight_spec(column) for column in range(spread)]
    return pl.pallas_call(
        project_kernel,
        grid_spec=pltpu.PrefetchScalarGridSpec(
            num_scalar_prefetch=1,
            grid=(PROJECT_STEPS,),
            in_specs=[pl.BlockSpec((chunk, model_width), lambda t, place: (t, 0))] + specs + specs,
            out_specs=[
                pl.BlockSpec((chunk, spread * width), lambda t, place: (t, 0)),
                pl.BlockSpec((spread * width, chunk), lambda t, place: (0, t)),
                pl.BlockSpec((8, LANES), lambda t, place: (0, 0)),
            ],
        ),
        out_shape=[
            jax.ShapeDtypeStruct((rows, spread * width), BF16),
            jax.ShapeDtypeStruct((spread * width, rows), BF16),
            jax.ShapeDtypeStruct((8, LANES), F32),
        ],
        compiler_params=pltpu.CompilerParams(vmem_limit_bytes=WIDE_BYTES),
        cost_estimate=pl.CostEstimate(
            flops=4 * rows * model_width * spread * width,
            bytes_accessed=2 * (2 * model_width * spread * width + 2 * rows * model_width),
            transcendentals=0,
        ),
        name="project",
    )(place, states, *([key_weight] * spread), *([value_weight] * spread))


def attend_group(z, place, table, pieces, blocks_in, out, offset, column, inner, head_width):
    relative = lax.bitwise_xor(z, place[3])
    spread, rows = pieces.shape[0], out.shape[2]
    width = out.shape[1] - STAT_ROWS
    count = width // head_width
    left = pl.multiple_of(lax.bitwise_xor(place[1], column) * width, width)
    quarters = []
    for lane in range(spread):
        for core in range(PAIR):
            lead = (lax.bitwise_xor(place[1], lane), relative, lax.bitwise_xor(place[0], core))
            quarters.append(pieces[lead + (slice(None), pl.ds(left, width))])
    query = jnp.concatenate(quarters, 0).T
    head_at = lax.broadcasted_iota(jnp.int32, query.shape, 0) // head_width
    spaced = jnp.concatenate([jnp.where(head_at == head, query, jnp.zeros_like(query)) for head in range(count)], 1)
    entry = z * inner + lax.bitwise_xor(place[2], offset)
    bundle = min(HEAD_BUNDLE, count)
    shelves = []
    for shelf in range(PAIR):
        scores = [
            jnp.dot(blocks_in[shelf][at][0][...], spaced, preferred_element_type=F32) for at in range(CAP)
        ]
        high = functools.reduce(jnp.maximum, [jnp.max(score, 0, keepdims=True) for score in scores])
        exponents = [jnp.exp(score - high) for score in scores]
        total = sum(jnp.sum(exponent, 0, keepdims=True) for exponent in exponents)
        probs = jnp.concatenate([exponent.astype(BF16) for exponent in exponents], 0)
        there = table[entry * 6 + shelf * 3 + 2] > 0
        blocks = []
        for first in range(0, count, bundle):
            here = slice(first * head_width, (first + bundle) * head_width)
            value = jnp.concatenate([blocks_in[shelf][at][1][here, :] for at in range(CAP)], 1)
            mixed = jnp.dot(value, probs[:, first * rows : (first + bundle) * rows], preferred_element_type=F32)
            for head in range(bundle):
                blocks.append(
                    mixed[head * head_width : (head + 1) * head_width, head * rows : (head + 1) * rows]
                )
        shelves.append((jnp.where(there, high, FLOOR), jnp.where(there, total, 0.0), blocks, there))
    high = functools.reduce(jnp.maximum, [shelf[0] for shelf in shelves])
    factors = [jnp.where(there, jnp.exp(shelf_high - high), 0.0) for shelf_high, _, _, there in shelves]
    total = sum(shelf[1] * factor for shelf, factor in zip(shelves, factors))
    for head in range(count):
        here = slice(head * rows, (head + 1) * rows)
        joined = sum(shelf[2][head] * factor[:, here] for shelf, factor in zip(shelves, factors))
        out[z, head * head_width : (head + 1) * head_width, :] = joined.astype(BF16)
    out[z, width:, :] = pack_stats(high, total, count, rows)


def attend_kernel(
    place, table, pieces, key_own, key_pair, value_own, value_pair, out, held, turned, arrived, *, offset, column, inner, head_width
):
    outer = out.shape[0]
    tokens, width = held.shape[3:]
    left = pl.multiple_of(lax.bitwise_xor(place[1], column) * width, width)
    copies = []
    for z in range(outer):
        entry = z * inner + lax.bitwise_xor(place[2], offset)
        for shelf, (keys, values) in enumerate(((key_own, value_own), (key_pair, value_pair))):
            for at in range(CAP):
                start = pl.multiple_of(table[entry * 6 + shelf * 3 + at] * tokens, tokens)
                source = keys.at[pl.ds(start, tokens), pl.ds(left, width)]
                lead = (z, shelf, at)
                copies.append(pltpu.make_async_copy(source, held.at[lead], arrived.at[lead + (0,)]))
                source = values.at[pl.ds(left, width), pl.ds(start, tokens)]
                copies.append(pltpu.make_async_copy(source, turned.at[lead], arrived.at[lead + (1,)]))
    for copy in copies:
        copy.start()
    each = len(copies) // outer
    for z in range(outer):
        for copy in copies[z * each : (z + 1) * each]:
            copy.wait()
        blocks_in = [[(held.at[z, shelf, at], turned.at[z, shelf, at]) for at in range(CAP)] for shelf in range(PAIR)]
        attend_group(z, place, table, pieces, blocks_in, out, offset, column, inner, head_width)


def pack_stats(high, total, count, rows):
    places = lax.broadcasted_iota(jnp.int32, (STAT_ROWS, rows), 0)
    packed = jnp.zeros((STAT_ROWS, rows), F32)
    for head in range(count):
        here = slice(head * rows, (head + 1) * rows)
        for at, term in enumerate(thirds(high[:, here]) + thirds(total[:, here])):
            packed = jnp.where(places == head * 6 + at, term, packed)
    return packed.astype(BF16)


def attend(place, table, pieces, keys, values, offset, column, inner, tokens, head_width):
    spread, outer, pair, part, half = pieces.shape
    width = half // spread
    rows = spread * pair * part
    whole = pl.BlockSpec(memory_space=pltpu.VMEM)
    scalars = pl.BlockSpec(memory_space=pltpu.SMEM)
    apart = pl.BlockSpec(memory_space=pl.ANY)
    return pl.pallas_call(
        functools.partial(attend_kernel, offset=offset, column=column, inner=inner, head_width=head_width),
        in_specs=[scalars, scalars, whole] + [apart] * 4,
        out_specs=whole,
        scratch_shapes=[
            pltpu.VMEM((outer, PAIR, CAP, tokens, width), BF16),
            pltpu.VMEM((outer, PAIR, CAP, width, tokens), BF16),
            pltpu.SemaphoreType.DMA((outer, PAIR, CAP, 2)),
        ],
        out_shape=jax.ShapeDtypeStruct((outer, width + STAT_ROWS, rows), BF16),
        compiler_params=pltpu.CompilerParams(vmem_limit_bytes=WIDE_BYTES),
        cost_estimate=pl.CostEstimate(
            flops=outer * 4 * 4 * rows * tokens * width * (width // head_width),
            bytes_accessed=outer * 2 * (width + STAT_ROWS) * rows,
            transcendentals=outer * 4 * rows * tokens * (width // head_width),
        ),
        name="attend",
    )(place, table, pieces, *keys, *values)


def unpack_stats(packed, width, count):
    tail = packed[width:, :].astype(F32)
    highs, totals = [], []
    for head in range(count):
        base = head * 6
        highs.append(tail[base : base + 1] + tail[base + 1 : base + 2] + tail[base + 2 : base + 3])
        totals.append(tail[base + 3 : base + 4] + tail[base + 4 : base + 5] + tail[base + 5 : base + 6])
    return highs, totals


def merge_heads(parts, width, head_width):
    count = width // head_width
    stats = [unpack_stats(part, width, count) for part in parts]
    mixes, highs, totals = [], [], []
    for head in range(count):
        high = functools.reduce(jnp.maximum, [stat[0][head] for stat in stats])
        mixed, total = 0.0, 0.0
        for part, stat in zip(parts, stats):
            factor = jnp.where(stat[1][head] > 0, jnp.exp(stat[0][head] - high), 0.0)
            total = total + stat[1][head] * factor
            mixed = mixed + part[head * head_width : (head + 1) * head_width, :].astype(F32) * factor
        mixes.append(mixed)
        highs.append(high)
        totals.append(total)
    return mixes, highs, totals


def gather_kernel(place, *refs, inner, spread, head_width):
    *parts, out = refs
    width = out.shape[2] - STAT_ROWS
    rows = out.shape[3]
    count = width // head_width
    for offset in range(inner):
        taken = [parts[offset * spread + column][0] for column in range(spread)]
        mixes, highs, totals = merge_heads(taken, width, head_width)
        target = lax.bitwise_xor(place[2], offset)
        for head in range(count):
            out[0, target, head * head_width : (head + 1) * head_width, :] = mixes[head].astype(BF16)
        out[0, target, width:, :] = pack_stats(
            jnp.concatenate(highs, 1), jnp.concatenate(totals, 1), count, rows
        )


def merge_lots(place, parts, inner, spread, head_width):
    outer, height, rows = parts[0].shape
    spec = pl.BlockSpec((1, height, rows), lambda z, place: (z, 0, 0))
    return pl.pallas_call(
        functools.partial(gather_kernel, inner=inner, spread=spread, head_width=head_width),
        grid_spec=pltpu.PrefetchScalarGridSpec(
            num_scalar_prefetch=1,
            grid=(outer,),
            in_specs=[spec] * len(parts),
            out_specs=pl.BlockSpec((1, inner, height, rows), lambda z, place: (z, 0, 0, 0)),
        ),
        out_shape=jax.ShapeDtypeStruct((outer, inner, height, rows), BF16),
        compiler_params=pltpu.CompilerParams(vmem_limit_bytes=WIDE_BYTES),
        name="merge_lots",
    )(place, *parts)


def finish_kernel(parts, out, *, head_width):
    width = parts.shape[1] - STAT_ROWS
    mixes, _, totals = merge_heads([parts[at] for at in range(parts.shape[0])], width, head_width)
    done = jnp.concatenate([mixed / total for mixed, total in zip(mixes, totals)], 0)
    out[...] = done.T.astype(BF16)


def finish(parts, head_width):
    whole = pl.BlockSpec(memory_space=pltpu.VMEM)
    return pl.pallas_call(
        functools.partial(finish_kernel, head_width=head_width),
        in_specs=[whole],
        out_specs=whole,
        out_shape=jax.ShapeDtypeStruct((parts.shape[2], parts.shape[1] - STAT_ROWS), BF16),
        compiler_params=grant(),
        name="finish",
    )(parts)


def local(
    queries,
    passages,
    noise,
    mix_weight,
    answer_queries,
    key_weight,
    value_weight,
    token_states,
    block_owner,
    listed,
):
    readers = lax.axis_size("pb")
    runners = lax.axis_size("pa")
    group = lax.axis_index("pb")
    runner = lax.axis_index("pa")
    spread = runners // PAIR
    inner = 1
    while (2 * inner) * (2 * inner) <= readers:
        inner *= 2
    outer = readers // inner
    model_width = key_weight.shape[0]
    head_width = model_width // HEADS
    slots, tokens = token_states.shape[:2]
    place = jnp.stack([runner % PAIR, runner // PAIR, group % inner, group // inner]).astype(jnp.int32)

    def swap(value, axis, bits):
        size = lax.axis_size(axis)
        return lax.ppermute(value, axis, [(at, at ^ bits) for at in range(size)])

    states = token_states.reshape(slots * tokens, model_width)
    pair_states = swap(states, "pa", 1)

    wanted = jnp.take(block_owner, listed[0], axis=0)
    wanted = jnp.concatenate([wanted, swap(wanted, "pa", 1)])
    digits = jnp.concatenate([wanted // LANES, wanted % LANES]).astype(F32)
    note = jnp.pad(digits[None], ((0, 0), (NOTE_AT, LANES - NOTE_AT - digits.shape[0])))
    keep, send = retrieve(place, queries, passages, noise, readers, spread)
    *by_column, place_own = merge_pair(place, keep, swap(send, "pa", 1), spread)
    parts = [by_column[0]] + [swap(by_column[at], "pa", at * PAIR) for at in range(1, spread)]
    own_key, own_value, own_done = project(place_own, states, key_weight, value_weight, spread)
    by_group, place_pair = merge_columns(place, note, own_done, parts)
    mine = lax.all_to_all(by_group, "pb", split_axis=0, concat_axis=0, tiled=True)
    pair_key, pair_value, pair_done = project(place_pair, pair_states, key_weight, value_weight, spread)
    keys, values = (own_key, pair_key), (own_value, pair_value)
    kept, sent = condition(place, mine, mix_weight, answer_queries, pair_done, spread)

    digits = mine[:, 0, queries.shape[1] + NOTE_AT :][:, : digits.shape[0]].astype(jnp.int32)
    slot_ids = digits[:, : wanted.shape[0]] * LANES + digits[:, wanted.shape[0] :]
    slot_ids = slot_ids.reshape(readers, PAIR, -1)
    holder = (runner ^ jnp.arange(PAIR, dtype=jnp.int32)) * readers + group
    held = slot_ids // slots == holder[None, :, None]
    inside = slot_ids % slots
    table = jnp.stack(
        [
            jnp.min(jnp.where(held, inside, slots - 1), 2),
            jnp.max(jnp.where(held, inside, 0), 2),
            jnp.any(held, 2).astype(jnp.int32),
        ],
        2,
    ).reshape(-1)

    pieces = jnp.stack([kept, swap(sent, "pa", 1)])[None]
    step = inner
    while step < readers:
        pieces = jnp.concatenate([pieces, swap(pieces, "pb", step)], 0)
        step *= 2
    own_pieces = pieces
    pieces = jnp.stack([pieces] + [swap(pieces, "pa", at * PAIR) for at in range(1, spread)])
    far = [pieces]
    for offset in range(1, inner):
        near = swap(own_pieces, "pb", offset)[None]
        far.append(jnp.concatenate([near, swap(pieces[1:], "pb", offset)], 0))
    lots = []
    for offset in range(inner):
        own = []
        for column in reversed(range(spread)):
            lot = attend(place, table, far[offset], keys, values, offset, column, inner, tokens, head_width)
            own.append(lot if column == 0 else swap(lot, "pa", column * PAIR))
        lots += own[::-1]
    merged = merge_lots(place, lots, inner, spread, head_width)
    merged = merged.reshape((readers,) + merged.shape[2:])
    return finish(lax.all_to_all(merged, "pb", split_axis=0, concat_axis=0, tiled=True), head_width)


def solution(mesh):
    return jax.shard_map(
        local,
        mesh=mesh,
        in_specs=(
            P(),
            P(("pa", "pb"), None),
            P(None, ("pa", "pb")),
            P(),
            P("pb", None),
            P(),
            P(),
            P(("pa", "pb"), None, None),
            P(),
            P("pb", "pa"),
        ),
        out_specs=P("pb", "pa"),
        check_vma=False,
    )
```

```python
import functools

import jax
import jax.numpy as jnp
from jax import lax
from jax.experimental import pallas as pl
from jax.experimental.pallas import tpu as pltpu
from jax.sharding import PartitionSpec as P

HEADS = 16
PAIR = 2
CAP = 2
TEMPER = 0.5
FLOOR = -1e30
LANES = 128
STAT_ROWS = 32
NOTE_AT = 6
STEP_GROUPS = 2
PROJECT_STEPS = 4
HEAD_BUNDLE = 2
VMEM_BYTES = 16 * 1024 * 1024
WIDE_BYTES = 60 * 1024 * 1024
F32 = jnp.float32
BF16 = jnp.bfloat16
NT = (((1,), (1,)), ((), ()))
SCALARS = pl.BlockSpec(memory_space=pltpu.SMEM)


def grant():
    return pltpu.CompilerParams(vmem_limit_bytes=VMEM_BYTES)


def thirds(value):
    first = value.astype(BF16).astype(F32)
    rest = value - first
    second = rest.astype(BF16).astype(F32)
    return first, second, rest - second


def pack_tail(shift, total):
    lane = lax.broadcasted_iota(jnp.int32, (shift.shape[0], LANES), 1)
    tail = jnp.zeros((shift.shape[0], LANES), F32)
    for at, term in enumerate(thirds(shift) + thirds(total)):
        tail = jnp.where(lane == at, term, tail)
    return tail


def unpack_tail(tail):
    term = lax.broadcasted_iota(jnp.int32, (LANES, 2 * LANES), 0)
    half = lax.broadcasted_iota(jnp.int32, (LANES, 2 * LANES), 1) // LANES
    pick = jnp.where(term // 3 == half, 1.0, 0.0).astype(BF16)
    both = jnp.dot(tail, pick, preferred_element_type=F32)
    return both[:, :LANES], both[:, LANES:]


def merge_rows(parts):
    width = parts[0].shape[1] - LANES
    stats = [unpack_tail(part[:, width:]) for part in parts]
    shift = functools.reduce(jnp.maximum, [stat[0] for stat in stats])
    factors = [jnp.exp(stat[0] - shift) for stat in stats]
    total = sum(stat[1] * factor for stat, factor in zip(stats, factors))
    tiles = [
        sum(part[:, at : at + LANES].astype(F32) * factor for part, factor in zip(parts, factors))
        for at in range(0, width, LANES)
    ]
    return tiles, shift, total


def flat(value):
    return value.reshape((-1, value.shape[-1]))


def retrieval_kernel(place, queries, passages, noise, keep, send, rows_scratch, *, spread):
    core = place[0]
    groups, part = keep.shape[1:3]
    width = queries.shape[1]
    logits = lax.dot_general(queries[...], passages[...], NT, preferred_element_type=F32)
    gumbel = -jnp.log(-jnp.log(noise[...].astype(F32)))
    scores = (logits * width ** (-0.5) + gumbel) * (1 / TEMPER)
    shift = jnp.max(scores, 1, keepdims=True)
    weight = jnp.exp(scores - shift)
    total = jnp.sum(weight, 1, keepdims=True)
    rows_scratch[:, :width] = jnp.dot(weight.astype(BF16), passages[...], preferred_element_type=F32)
    rows_scratch[:, width:] = pack_tail(shift, total)
    for at in range(groups):
        for column in range(spread):
            base = (at * spread + column) * PAIR
            mine = pl.multiple_of((base + core) * part, part)
            other = pl.multiple_of((base + 1 - core) * part, part)
            keep[column, at] = rows_scratch[pl.ds(mine, part), :].astype(BF16)
            send[column, at] = rows_scratch[pl.ds(other, part), :].astype(BF16)


def retrieve(place, queries, passages, noise, readers, spread):
    count, width = queries.shape
    group = count // readers
    part = group // (PAIR * spread)
    shape = jax.ShapeDtypeStruct((spread, readers, part, width + LANES), BF16)
    spec = pl.BlockSpec((spread, STEP_GROUPS, part, width + LANES), lambda g, place: (0, g, 0, 0))
    rows = group * STEP_GROUPS
    return pl.pallas_call(
        functools.partial(retrieval_kernel, spread=spread),
        grid_spec=pltpu.PrefetchScalarGridSpec(
            num_scalar_prefetch=1,
            grid=(readers // STEP_GROUPS,),
            in_specs=[
                pl.BlockSpec((rows, width), lambda g, place: (g, 0)),
                pl.BlockSpec(passages.shape, lambda g, place: (0, 0)),
                pl.BlockSpec((rows, noise.shape[1]), lambda g, place: (g, 0)),
            ],
            out_specs=[spec, spec],
            scratch_shapes=[pltpu.VMEM((rows, width + LANES), F32)],
        ),
        out_shape=[shape, shape],
        compiler_params=pltpu.CompilerParams(vmem_limit_bytes=WIDE_BYTES),
        cost_estimate=pl.CostEstimate(
            flops=4 * count * width * passages.shape[0],
            bytes_accessed=2 * (2 * count * width + passages.size + noise.size),
            transcendentals=3 * noise.size,
        ),
        name="retrieve",
    )(place, queries, passages, noise)


def store_rows(out, tiles, shift, total, note=None):
    for at, tile in enumerate(tiles):
        out[..., at * LANES : (at + 1) * LANES] = tile.astype(BF16).reshape(out.shape[:-1] + (LANES,))
    tail = pack_tail(shift, total)
    if note is not None:
        tail = tail + note
    out[..., len(tiles) * LANES :] = tail.astype(BF16).reshape(out.shape[:-1] + (LANES,))


def hand_on(place, out):
    for at in range(out.shape[0]):
        out[at] = place[at]


def pair_kernel(place, keep, recv, *outs):
    *outs, later = outs
    hand_on(place, later)
    for offset, out in enumerate(outs):
        column = lax.bitwise_xor(place[1], offset)
        store_rows(out, *merge_rows([flat(keep[column]), flat(recv[column])]))


def merge_pair(place, keep, recv, spread):
    readers = keep.shape[1]
    spec = pl.BlockSpec((spread, readers // 2) + keep.shape[2:], lambda g, place: (0, g, 0, 0))
    out = pl.BlockSpec((readers // 2,) + keep.shape[2:], lambda g, place: (g, 0, 0))
    return pl.pallas_call(
        pair_kernel,
        grid_spec=pltpu.PrefetchScalarGridSpec(
            num_scalar_prefetch=1, grid=(2,), in_specs=[spec, spec], out_specs=[out] * spread + [SCALARS]
        ),
        out_shape=[jax.ShapeDtypeStruct(keep.shape[1:], BF16)] * spread
        + [jax.ShapeDtypeStruct(place.shape, place.dtype)],
        compiler_params=grant(),
        name="merge_pair",
    )(place, keep, recv)


def column_kernel(place, note, done, *refs):
    *parts, out, later = refs
    hand_on(place, later)
    store_rows(out, *merge_rows([flat(part[...]) for part in parts]), note[...] + done[0:1, :])


def merge_columns(place, note, done, parts):
    readers = parts[0].shape[0]
    spec = pl.BlockSpec((readers // 2,) + parts[0].shape[1:], lambda g, place: (g, 0, 0))
    return pl.pallas_call(
        column_kernel,
        grid_spec=pltpu.PrefetchScalarGridSpec(
            num_scalar_prefetch=1,
            grid=(2,),
            in_specs=[
                pl.BlockSpec(note.shape, lambda g, place: (0, 0)),
                pl.BlockSpec(done.shape, lambda g, place: (0, 0)),
            ]
            + [spec] * len(parts),
            out_specs=[spec, SCALARS],
        ),
        out_shape=[
            jax.ShapeDtypeStruct(parts[0].shape, BF16),
            jax.ShapeDtypeStruct(place.shape, place.dtype),
        ],
        compiler_params=grant(),
        name="merge_columns",
    )(place, note, done, *parts)


def condition_kernel(place, parts, mix_weight, answers, done, keep, send, rows_scratch, *, spread):
    tiles, _, total = merge_rows([parts[at] for at in range(parts.shape[0])])
    blended_half = jnp.concatenate([(tile / total).astype(BF16) for tile in tiles], 1)
    part = blended_half.shape[0]
    start = pl.multiple_of((place[1] * PAIR + place[0]) * part, part)
    answer = answers[pl.ds(start, part), :].astype(F32)
    rows_scratch[...] = answer + jnp.dot(blended_half, mix_weight[...], preferred_element_type=F32)
    stride = keep.shape[1] // spread
    for column in range(spread):
        mine = pl.multiple_of((column * PAIR + place[0]) * stride, stride)
        other = pl.multiple_of((column * PAIR + 1 - place[0]) * stride, stride)
        keep[:, column * stride : (column + 1) * stride] = rows_scratch[:, pl.ds(mine, stride)].astype(BF16)
        send[:, column * stride : (column + 1) * stride] = rows_scratch[:, pl.ds(other, stride)].astype(BF16)


def condition(place, parts, mix_weight, answers, done, spread):
    model_width = mix_weight.shape[1]
    shape = jax.ShapeDtypeStruct((parts.shape[1], model_width // PAIR), BF16)
    whole = pl.BlockSpec(memory_space=pltpu.VMEM)
    return pl.pallas_call(
        functools.partial(condition_kernel, spread=spread),
        in_specs=[SCALARS, whole, whole, whole, whole],
        out_specs=[whole, whole],
        out_shape=[shape, shape],
        scratch_shapes=[pltpu.VMEM((parts.shape[1], model_width), F32)],
        compiler_params=grant(),
        name="condition",
    )(place, parts, mix_weight, answers, done)


def project_kernel(place, states, *refs):
    spread = (len(refs) - 3) // 2
    keys, values, done = refs[-3:]
    done[...] = jnp.zeros_like(done)
    tokens = values.shape[3]
    for column in range(spread):
        keys[column] = jnp.dot(states[...], refs[column][...], preferred_element_type=F32).astype(BF16)
        value = jnp.dot(states[...], refs[spread + column][...], preferred_element_type=F32).astype(BF16)
        for block in range(values.shape[1]):
            values[column, block] = value[block * tokens : (block + 1) * tokens].T


def project(place, states, key_weight, value_weight, spread, tokens):
    rows, model_width = states.shape
    width = model_width // (PAIR * spread)
    chunk = rows // PROJECT_STEPS
    blocks = chunk // tokens

    def weight_spec(column):
        return pl.BlockSpec((model_width, width), lambda t, place: (0, column * PAIR + place[0]))

    specs = [weight_spec(column) for column in range(spread)]
    return pl.pallas_call(
        project_kernel,
        grid_spec=pltpu.PrefetchScalarGridSpec(
            num_scalar_prefetch=1,
            grid=(PROJECT_STEPS,),
            in_specs=[pl.BlockSpec((chunk, model_width), lambda t, place: (t, 0))] + specs + specs,
            out_specs=[
                pl.BlockSpec((spread, chunk, width), lambda t, place: (0, t, 0)),
                pl.BlockSpec((spread, blocks, width, tokens), lambda t, place: (0, t, 0, 0)),
                pl.BlockSpec((8, LANES), lambda t, place: (0, 0)),
            ],
        ),
        out_shape=[
            jax.ShapeDtypeStruct((spread, rows, width), BF16),
            jax.ShapeDtypeStruct((spread, rows // tokens, width, tokens), BF16),
            jax.ShapeDtypeStruct((8, LANES), F32),
        ],
        compiler_params=pltpu.CompilerParams(vmem_limit_bytes=WIDE_BYTES),
        cost_estimate=pl.CostEstimate(
            flops=4 * rows * model_width * spread * width,
            bytes_accessed=2 * (2 * model_width * spread * width + 2 * rows * model_width),
            transcendentals=0,
        ),
        name="project",
    )(place, states, *([key_weight] * spread), *([value_weight] * spread))


def attend_group(z, place, table, pieces, blocks_in, out, offset, column, inner, head_width):
    relative = lax.bitwise_xor(z, place[3])
    spread, rows = pieces.shape[0], out.shape[2]
    width = out.shape[1] - STAT_ROWS
    count = width // head_width
    left = pl.multiple_of(lax.bitwise_xor(place[1], column) * width, width)
    quarters = []
    for lane in range(spread):
        for core in range(PAIR):
            lead = (lax.bitwise_xor(place[1], lane), relative, lax.bitwise_xor(place[0], core))
            quarters.append(pieces[lead + (slice(None), pl.ds(left, width))])
    query = jnp.concatenate(quarters, 0).T
    head_at = lax.broadcasted_iota(jnp.int32, query.shape, 0) // head_width
    spaced = jnp.concatenate([jnp.where(head_at == head, query, jnp.zeros_like(query)) for head in range(count)], 1)
    entry = z * inner + lax.bitwise_xor(place[2], offset)
    bundle = min(HEAD_BUNDLE, count)
    shelves = []
    for shelf in range(PAIR):
        scores = [
            jnp.dot(blocks_in[shelf][at][0][...], spaced, preferred_element_type=F32) for at in range(CAP)
        ]
        high = functools.reduce(jnp.maximum, [jnp.max(score, 0, keepdims=True) for score in scores])
        exponents = [jnp.exp(score - high) for score in scores]
        total = sum(jnp.sum(exponent, 0, keepdims=True) for exponent in exponents)
        probs = jnp.concatenate([exponent.astype(BF16) for exponent in exponents], 0)
        there = table[entry * 6 + shelf * 3 + 2] > 0
        blocks = []
        for first in range(0, count, bundle):
            here = slice(first * head_width, (first + bundle) * head_width)
            value = jnp.concatenate([blocks_in[shelf][at][1][here, :] for at in range(CAP)], 1)
            mixed = jnp.dot(value, probs[:, first * rows : (first + bundle) * rows], preferred_element_type=F32)
            for head in range(bundle):
                blocks.append(
                    mixed[head * head_width : (head + 1) * head_width, head * rows : (head + 1) * rows]
                )
        shelves.append((jnp.where(there, high, FLOOR), jnp.where(there, total, 0.0), blocks, there))
    high = functools.reduce(jnp.maximum, [shelf[0] for shelf in shelves])
    factors = [jnp.where(there, jnp.exp(shelf_high - high), 0.0) for shelf_high, _, _, there in shelves]
    total = sum(shelf[1] * factor for shelf, factor in zip(shelves, factors))
    for head in range(count):
        here = slice(head * rows, (head + 1) * rows)
        joined = sum(shelf[2][head] * factor[:, here] for shelf, factor in zip(shelves, factors))
        out[z, head * head_width : (head + 1) * head_width, :] = joined.astype(BF16)
    out[z, width:, :] = pack_stats(high, total, count, rows)


def attend_kernel(
    place, table, pieces, key_own, key_pair, value_own, value_pair, out, held, turned, arrived, *, offset, column, inner, head_width
):
    outer = out.shape[0]
    tokens, width = held.shape[3:]
    side = lax.bitwise_xor(place[1], column)
    copies = []
    for z in range(outer):
        entry = z * inner + lax.bitwise_xor(place[2], offset)
        for shelf, (keys, values) in enumerate(((key_own, value_own), (key_pair, value_pair))):
            for at in range(CAP):
                slot = table[entry * 6 + shelf * 3 + at]
                lead = (z, shelf, at)
                source = keys.at[side, pl.ds(pl.multiple_of(slot * tokens, tokens), tokens), :]
                copies.append(pltpu.make_async_copy(source, held.at[lead], arrived.at[lead + (0,)]))
                copies.append(pltpu.make_async_copy(values.at[side, slot], turned.at[lead], arrived.at[lead + (1,)]))
    for copy in copies:
        copy.start()
    each = len(copies) // outer
    for z in range(outer):
        for copy in copies[z * each : (z + 1) * each]:
            copy.wait()
        blocks_in = [[(held.at[z, shelf, at], turned.at[z, shelf, at]) for at in range(CAP)] for shelf in range(PAIR)]
        attend_group(z, place, table, pieces, blocks_in, out, offset, column, inner, head_width)


def pack_stats(high, total, count, rows):
    places = lax.broadcasted_iota(jnp.int32, (STAT_ROWS, rows), 0)
    packed = jnp.zeros((STAT_ROWS, rows), F32)
    for head in range(count):
        here = slice(head * rows, (head + 1) * rows)
        for at, term in enumerate(thirds(high[:, here]) + thirds(total[:, here])):
            packed = jnp.where(places == head * 6 + at, term, packed)
    return packed.astype(BF16)


def attend(place, table, pieces, keys, values, offset, column, inner, tokens, head_width):
    spread, outer, pair, part, half = pieces.shape
    width = half // spread
    rows = spread * pair * part
    whole = pl.BlockSpec(memory_space=pltpu.VMEM)
    scalars = pl.BlockSpec(memory_space=pltpu.SMEM)
    apart = pl.BlockSpec(memory_space=pl.ANY)
    return pl.pallas_call(
        functools.partial(attend_kernel, offset=offset, column=column, inner=inner, head_width=head_width),
        in_specs=[scalars, scalars, whole] + [apart] * 4,
        out_specs=whole,
        scratch_shapes=[
            pltpu.VMEM((outer, PAIR, CAP, tokens, width), BF16),
            pltpu.VMEM((outer, PAIR, CAP, width, tokens), BF16),
            pltpu.SemaphoreType.DMA((outer, PAIR, CAP, 2)),
        ],
        out_shape=jax.ShapeDtypeStruct((outer, width + STAT_ROWS, rows), BF16),
        compiler_params=pltpu.CompilerParams(vmem_limit_bytes=WIDE_BYTES),
        cost_estimate=pl.CostEstimate(
            flops=outer * 4 * 4 * rows * tokens * width * (width // head_width),
            bytes_accessed=outer * 2 * (width + STAT_ROWS) * rows,
            transcendentals=outer * 4 * rows * tokens * (width // head_width),
        ),
        name="attend",
    )(place, table, pieces, *keys, *values)


def unpack_stats(packed, width, count):
    tail = packed[width:, :].astype(F32)
    highs, totals = [], []
    for head in range(count):
        base = head * 6
        highs.append(tail[base : base + 1] + tail[base + 1 : base + 2] + tail[base + 2 : base + 3])
        totals.append(tail[base + 3 : base + 4] + tail[base + 4 : base + 5] + tail[base + 5 : base + 6])
    return highs, totals


def merge_heads(parts, width, head_width):
    count = width // head_width
    stats = [unpack_stats(part, width, count) for part in parts]
    mixes, highs, totals = [], [], []
    for head in range(count):
        high = functools.reduce(jnp.maximum, [stat[0][head] for stat in stats])
        mixed, total = 0.0, 0.0
        for part, stat in zip(parts, stats):
            factor = jnp.where(stat[1][head] > 0, jnp.exp(stat[0][head] - high), 0.0)
            total = total + stat[1][head] * factor
            mixed = mixed + part[head * head_width : (head + 1) * head_width, :].astype(F32) * factor
        mixes.append(mixed)
        highs.append(high)
        totals.append(total)
    return mixes, highs, totals


def gather_kernel(place, *refs, outer, head_width):
    parts, outs = refs[:-outer], refs[-outer:]
    rows = outs[0].shape[1]
    width = outs[0].shape[0] - STAT_ROWS
    count = width // head_width
    for step, out in enumerate(outs):
        z = lax.bitwise_xor(place[3], step)
        mixes, highs, totals = merge_heads([part[z] for part in parts], width, head_width)
        for head in range(count):
            out[head * head_width : (head + 1) * head_width, :] = mixes[head].astype(BF16)
        out[width:, :] = pack_stats(jnp.concatenate(highs, 1), jnp.concatenate(totals, 1), count, rows)


def merge_lots(place, parts, head_width):
    outer, height, rows = parts[0].shape
    whole = pl.BlockSpec(memory_space=pltpu.VMEM)
    return pl.pallas_call(
        functools.partial(gather_kernel, outer=outer, head_width=head_width),
        in_specs=[SCALARS] + [whole] * len(parts),
        out_specs=[whole] * outer,
        out_shape=[jax.ShapeDtypeStruct((height, rows), BF16)] * outer,
        compiler_params=grant(),
        name="merge_lots",
    )(place, *parts)


def finish_kernel(*refs, head_width):
    *parts, out = refs
    width = out.shape[1]
    mixes, _, totals = merge_heads([part[...] for part in parts], width, head_width)
    done = jnp.concatenate([mixed / total for mixed, total in zip(mixes, totals)], 0)
    out[...] = done.T.astype(BF16)


def finish(parts, head_width):
    whole = pl.BlockSpec(memory_space=pltpu.VMEM)
    return pl.pallas_call(
        functools.partial(finish_kernel, head_width=head_width),
        in_specs=[whole] * len(parts),
        out_specs=whole,
        out_shape=jax.ShapeDtypeStruct((parts[0].shape[1], parts[0].shape[0] - STAT_ROWS), BF16),
        compiler_params=grant(),
        name="finish",
    )(*parts)


def local(
    queries,
    passages,
    noise,
    mix_weight,
    answer_queries,
    key_weight,
    value_weight,
    token_states,
    block_owner,
    listed,
):
    readers = lax.axis_size("pb")
    runners = lax.axis_size("pa")
    group = lax.axis_index("pb")
    runner = lax.axis_index("pa")
    spread = runners // PAIR
    inner = 1
    while (2 * inner) * (2 * inner) <= readers:
        inner *= 2
    outer = readers // inner
    model_width = key_weight.shape[0]
    head_width = model_width // HEADS
    slots, tokens = token_states.shape[:2]
    place = jnp.stack([runner % PAIR, runner // PAIR, group % inner, group // inner]).astype(jnp.int32)

    def swap(value, axis, bits):
        size = lax.axis_size(axis)
        return lax.ppermute(value, axis, [(at, at ^ bits) for at in range(size)])

    states = token_states.reshape(slots * tokens, model_width)
    pair_states = swap(states, "pa", 1)

    wanted = jnp.take(block_owner, listed[0], axis=0)
    wanted = jnp.concatenate([wanted, swap(wanted, "pa", 1)])
    digits = jnp.concatenate([wanted // LANES, wanted % LANES]).astype(F32)
    note = jnp.pad(digits[None], ((0, 0), (NOTE_AT, LANES - NOTE_AT - digits.shape[0])))
    keep, send = retrieve(place, queries, passages, noise, readers, spread)
    *by_column, place_own = merge_pair(place, keep, swap(send, "pa", 1), spread)
    parts = [by_column[0]] + [swap(by_column[at], "pa", at * PAIR) for at in range(1, spread)]
    own_key, own_value, own_done = project(place_own, states, key_weight, value_weight, spread, tokens)
    by_group, place_pair = merge_columns(place, note, own_done, parts)
    mine = lax.all_to_all(by_group, "pb", split_axis=0, concat_axis=0, tiled=True)
    pair_key, pair_value, pair_done = project(place_pair, pair_states, key_weight, value_weight, spread, tokens)
    keys, values = (own_key, pair_key), (own_value, pair_value)
    kept, sent = condition(place, mine, mix_weight, answer_queries, pair_done, spread)

    digits = mine[:, 0, queries.shape[1] + NOTE_AT :][:, : digits.shape[0]].astype(jnp.int32)
    slot_ids = digits[:, : wanted.shape[0]] * LANES + digits[:, wanted.shape[0] :]
    slot_ids = slot_ids.reshape(readers, PAIR, -1)
    holder = (runner ^ jnp.arange(PAIR, dtype=jnp.int32)) * readers + group
    held = slot_ids // slots == holder[None, :, None]
    inside = slot_ids % slots
    table = jnp.stack(
        [
            jnp.min(jnp.where(held, inside, slots - 1), 2),
            jnp.max(jnp.where(held, inside, 0), 2),
            jnp.any(held, 2).astype(jnp.int32),
        ],
        2,
    ).reshape(-1)

    pieces = jnp.stack([kept, swap(sent, "pa", 1)])[None]
    step = inner
    while step < readers:
        pieces = jnp.concatenate([pieces, swap(pieces, "pb", step)], 0)
        step *= 2
    own_pieces = pieces
    pieces = jnp.stack([pieces] + [swap(pieces, "pa", at * PAIR) for at in range(1, spread)])
    far = [pieces]
    for offset in range(1, inner):
        near = swap(own_pieces, "pb", offset)[None]
        far.append(jnp.concatenate([near, swap(pieces[1:], "pb", offset)], 0))
    lots = []
    for offset, column in [(o, c) for o in range(inner) for c in range(spread)][1:] + [(0, 0)]:
        lot = attend(place, table, far[offset], keys, values, offset, column, inner, tokens, head_width)
        bits = column * PAIR * readers + offset
        if bits:
            lot = lax.ppermute(lot, ("pa", "pb"), [(at, at ^ bits) for at in range(runners * readers)])
        lots.append(lot)
    kept, *away = merge_lots(place, lots, head_width)
    back = [swap(part, "pb", (step + 1) * inner) for step, part in enumerate(away)]
    return finish([kept] + back, head_width)


def solution(mesh):
    return jax.shard_map(
        local,
        mesh=mesh,
        in_specs=(
            P(),
            P(("pa", "pb"), None),
            P(None, ("pa", "pb")),
            P(),
            P("pb", None),
            P(),
            P(),
            P(("pa", "pb"), None, None),
            P(),
            P("pb", "pa"),
        ),
        out_specs=P("pb", "pa"),
        check_vma=False,
    )
```

```python
import functools

import jax
import jax.numpy as jnp
from jax import lax
from jax.experimental import pallas as pl
from jax.experimental.pallas import tpu as pltpu
from jax.sharding import PartitionSpec as P

HEADS = 16
PAIR = 2
CAP = 2
TEMPER = 0.5
FLOOR = -1e30
LANES = 128
STAT_ROWS = 32
NOTE_AT = 6
STEP_GROUPS = 2
PROJECT_STEPS = 4
HEAD_BUNDLE = 2
VMEM_BYTES = 16 * 1024 * 1024
WIDE_BYTES = 60 * 1024 * 1024
F32 = jnp.float32
BF16 = jnp.bfloat16
NT = (((1,), (1,)), ((), ()))
SCALARS = pl.BlockSpec(memory_space=pltpu.SMEM)


def grant():
    return pltpu.CompilerParams(vmem_limit_bytes=VMEM_BYTES)


def thirds(value):
    first = value.astype(BF16).astype(F32)
    rest = value - first
    second = rest.astype(BF16).astype(F32)
    return first, second, rest - second


def pack_tail(shift, total):
    lane = lax.broadcasted_iota(jnp.int32, (shift.shape[0], LANES), 1)
    tail = jnp.zeros((shift.shape[0], LANES), F32)
    for at, term in enumerate(thirds(shift) + thirds(total)):
        tail = jnp.where(lane == at, term, tail)
    return tail


def unpack_tail(tail):
    term = lax.broadcasted_iota(jnp.int32, (LANES, 2 * LANES), 0)
    half = lax.broadcasted_iota(jnp.int32, (LANES, 2 * LANES), 1) // LANES
    pick = jnp.where(term // 3 == half, 1.0, 0.0).astype(BF16)
    both = jnp.dot(tail, pick, preferred_element_type=F32)
    return both[:, :LANES], both[:, LANES:]


def merge_rows(parts):
    width = parts[0].shape[1] - LANES
    stats = [unpack_tail(part[:, width:]) for part in parts]
    shift = functools.reduce(jnp.maximum, [stat[0] for stat in stats])
    factors = [jnp.exp(stat[0] - shift) for stat in stats]
    total = sum(stat[1] * factor for stat, factor in zip(stats, factors))
    tiles = [
        sum(part[:, at : at + LANES].astype(F32) * factor for part, factor in zip(parts, factors))
        for at in range(0, width, LANES)
    ]
    return tiles, shift, total


def flat(value):
    return value.reshape((-1, value.shape[-1]))


def retrieval_kernel(place, queries, passages, noise, keep, send, rows_scratch, *, spread):
    core = place[0]
    groups, part = keep.shape[1:3]
    width = queries.shape[1]
    logits = lax.dot_general(queries[...], passages[...], NT, preferred_element_type=F32)
    gumbel = -jnp.log(-jnp.log(noise[...].astype(F32)))
    scores = (logits * width ** (-0.5) + gumbel) * (1 / TEMPER)
    shift = jnp.max(scores, 1, keepdims=True)
    weight = jnp.exp(scores - shift)
    total = jnp.sum(weight, 1, keepdims=True)
    rows_scratch[:, :width] = jnp.dot(weight.astype(BF16), passages[...], preferred_element_type=F32)
    rows_scratch[:, width:] = pack_tail(shift, total)
    for at in range(groups):
        for column in range(spread):
            base = (at * spread + column) * PAIR
            mine = pl.multiple_of((base + core) * part, part)
            other = pl.multiple_of((base + 1 - core) * part, part)
            keep[column, at] = rows_scratch[pl.ds(mine, part), :].astype(BF16)
            send[column, at] = rows_scratch[pl.ds(other, part), :].astype(BF16)


def retrieve(place, queries, passages, noise, readers, spread):
    count, width = queries.shape
    group = count // readers
    part = group // (PAIR * spread)
    shape = jax.ShapeDtypeStruct((spread, readers, part, width + LANES), BF16)
    spec = pl.BlockSpec((spread, STEP_GROUPS, part, width + LANES), lambda g, place: (0, g, 0, 0))
    rows = group * STEP_GROUPS
    return pl.pallas_call(
        functools.partial(retrieval_kernel, spread=spread),
        grid_spec=pltpu.PrefetchScalarGridSpec(
            num_scalar_prefetch=1,
            grid=(readers // STEP_GROUPS,),
            in_specs=[
                pl.BlockSpec((rows, width), lambda g, place: (g, 0)),
                pl.BlockSpec(passages.shape, lambda g, place: (0, 0)),
                pl.BlockSpec((rows, noise.shape[1]), lambda g, place: (g, 0)),
            ],
            out_specs=[spec, spec],
            scratch_shapes=[pltpu.VMEM((rows, width + LANES), F32)],
        ),
        out_shape=[shape, shape],
        compiler_params=pltpu.CompilerParams(vmem_limit_bytes=WIDE_BYTES),
        cost_estimate=pl.CostEstimate(
            flops=4 * count * width * passages.shape[0],
            bytes_accessed=2 * (2 * count * width + passages.size + noise.size),
            transcendentals=3 * noise.size,
        ),
        name="retrieve",
    )(place, queries, passages, noise)


def store_rows(out, tiles, shift, total, note=None):
    for at, tile in enumerate(tiles):
        out[..., at * LANES : (at + 1) * LANES] = tile.astype(BF16).reshape(out.shape[:-1] + (LANES,))
    tail = pack_tail(shift, total)
    if note is not None:
        tail = tail + note
    out[..., len(tiles) * LANES :] = tail.astype(BF16).reshape(out.shape[:-1] + (LANES,))


def hand_on(place, out):
    for at in range(out.shape[0]):
        out[at] = place[at]


def pair_kernel(place, keep, recv, *outs):
    *outs, later = outs
    hand_on(place, later)
    for offset, out in enumerate(outs):
        column = lax.bitwise_xor(place[1], offset)
        store_rows(out, *merge_rows([flat(keep[column]), flat(recv[column])]))


def merge_pair(place, keep, recv, spread):
    readers = keep.shape[1]
    spec = pl.BlockSpec((spread, readers // 2) + keep.shape[2:], lambda g, place: (0, g, 0, 0))
    out = pl.BlockSpec((readers // 2,) + keep.shape[2:], lambda g, place: (g, 0, 0))
    return pl.pallas_call(
        pair_kernel,
        grid_spec=pltpu.PrefetchScalarGridSpec(
            num_scalar_prefetch=1, grid=(2,), in_specs=[spec, spec], out_specs=[out] * spread + [SCALARS]
        ),
        out_shape=[jax.ShapeDtypeStruct(keep.shape[1:], BF16)] * spread
        + [jax.ShapeDtypeStruct(place.shape, place.dtype)],
        compiler_params=grant(),
        name="merge_pair",
    )(place, keep, recv)


def column_kernel(place, note, done, *refs):
    *parts, out, later = refs
    hand_on(place, later)
    store_rows(out, *merge_rows([flat(part[...]) for part in parts]), note[...] + done[0:1, :])


def merge_columns(place, note, done, parts):
    readers = parts[0].shape[0]
    spec = pl.BlockSpec((readers // 2,) + parts[0].shape[1:], lambda g, place: (g, 0, 0))
    return pl.pallas_call(
        column_kernel,
        grid_spec=pltpu.PrefetchScalarGridSpec(
            num_scalar_prefetch=1,
            grid=(2,),
            in_specs=[
                pl.BlockSpec(note.shape, lambda g, place: (0, 0)),
                pl.BlockSpec(done.shape, lambda g, place: (0, 0)),
            ]
            + [spec] * len(parts),
            out_specs=[spec, SCALARS],
        ),
        out_shape=[
            jax.ShapeDtypeStruct(parts[0].shape, BF16),
            jax.ShapeDtypeStruct(place.shape, place.dtype),
        ],
        compiler_params=grant(),
        name="merge_columns",
    )(place, note, done, *parts)


def condition_kernel(place, parts, mix_weight, answers, done, keep, send, rows_scratch, *, spread):
    tiles, _, total = merge_rows([parts[at] for at in range(parts.shape[0])])
    blended_half = jnp.concatenate([(tile / total).astype(BF16) for tile in tiles], 1)
    part = blended_half.shape[0]
    start = pl.multiple_of((place[1] * PAIR + place[0]) * part, part)
    answer = answers[pl.ds(start, part), :].astype(F32)
    rows_scratch[...] = answer + jnp.dot(blended_half, mix_weight[...], preferred_element_type=F32)
    stride = keep.shape[1] // spread
    for column in range(spread):
        mine = pl.multiple_of((column * PAIR + place[0]) * stride, stride)
        other = pl.multiple_of((column * PAIR + 1 - place[0]) * stride, stride)
        keep[:, column * stride : (column + 1) * stride] = rows_scratch[:, pl.ds(mine, stride)].astype(BF16)
        send[:, column * stride : (column + 1) * stride] = rows_scratch[:, pl.ds(other, stride)].astype(BF16)


def condition(place, parts, mix_weight, answers, done, spread):
    model_width = mix_weight.shape[1]
    shape = jax.ShapeDtypeStruct((parts.shape[1], model_width // PAIR), BF16)
    whole = pl.BlockSpec(memory_space=pltpu.VMEM)
    return pl.pallas_call(
        functools.partial(condition_kernel, spread=spread),
        in_specs=[SCALARS, whole, whole, whole, whole],
        out_specs=[whole, whole],
        out_shape=[shape, shape],
        scratch_shapes=[pltpu.VMEM((parts.shape[1], model_width), F32)],
        compiler_params=grant(),
        name="condition",
    )(place, parts, mix_weight, answers, done)


def project_kernel(place, states, *refs):
    spread = (len(refs) - 3) // 2
    keys, values, done = refs[-3:]
    done[...] = jnp.zeros_like(done)
    tokens = values.shape[3]
    for column in range(spread):
        keys[column] = jnp.dot(states[...], refs[column][...], preferred_element_type=F32).astype(BF16)
        value = jnp.dot(states[...], refs[spread + column][...], preferred_element_type=F32).astype(BF16)
        for block in range(values.shape[1]):
            values[column, block] = value[block * tokens : (block + 1) * tokens].T


def project(place, states, key_weight, value_weight, spread, tokens):
    rows, model_width = states.shape
    width = model_width // (PAIR * spread)
    chunk = rows // PROJECT_STEPS
    blocks = chunk // tokens

    def weight_spec(column):
        return pl.BlockSpec((model_width, width), lambda t, place: (0, column * PAIR + place[0]))

    specs = [weight_spec(column) for column in range(spread)]
    return pl.pallas_call(
        project_kernel,
        grid_spec=pltpu.PrefetchScalarGridSpec(
            num_scalar_prefetch=1,
            grid=(PROJECT_STEPS,),
            in_specs=[pl.BlockSpec((chunk, model_width), lambda t, place: (t, 0))] + specs + specs,
            out_specs=[
                pl.BlockSpec((spread, chunk, width), lambda t, place: (0, t, 0)),
                pl.BlockSpec((spread, blocks, width, tokens), lambda t, place: (0, t, 0, 0)),
                pl.BlockSpec((8, LANES), lambda t, place: (0, 0)),
            ],
        ),
        out_shape=[
            jax.ShapeDtypeStruct((spread, rows, width), BF16),
            jax.ShapeDtypeStruct((spread, rows // tokens, width, tokens), BF16),
            jax.ShapeDtypeStruct((8, LANES), F32),
        ],
        compiler_params=pltpu.CompilerParams(vmem_limit_bytes=WIDE_BYTES),
        cost_estimate=pl.CostEstimate(
            flops=4 * rows * model_width * spread * width,
            bytes_accessed=2 * (2 * model_width * spread * width + 2 * rows * model_width),
            transcendentals=0,
        ),
        name="project",
    )(place, states, *([key_weight] * spread), *([value_weight] * spread))


def attend_group(z, place, table, pieces, keys, values, out, rows_scratch, offset, column, inner, head_width):
    relative = lax.bitwise_xor(z, place[3])
    part, rows = pieces[0].shape[2], out.shape[2]
    width = out.shape[1] - STAT_ROWS
    count = width // head_width
    side = lax.bitwise_xor(place[1], column)
    left = pl.multiple_of(side * width, width)
    for step, piece in enumerate(pieces):
        for core in range(PAIR):
            top = lax.bitwise_xor(place[1], step) * PAIR + lax.bitwise_xor(place[0], core)
            top = pl.multiple_of(top * part, part)
            rows_scratch[z, pl.ds(top, part), :] = piece[relative, core, :, pl.ds(left, width)]
    query = rows_scratch[z].T
    tokens = values[0].shape[3]
    head_at = lax.broadcasted_iota(jnp.int32, query.shape, 0) // head_width
    spaced = jnp.concatenate([jnp.where(head_at == head, query, jnp.zeros_like(query)) for head in range(count)], 1)
    entry = z * inner + lax.bitwise_xor(place[2], offset)
    bundle = min(HEAD_BUNDLE, count)
    shelves = []
    for shelf in range(PAIR):
        chosen = [table[entry * 6 + shelf * 3 + at] for at in range(CAP)]
        scores = [
            jnp.dot(
                keys[shelf][side, pl.ds(pl.multiple_of(slot * tokens, tokens), tokens), :],
                spaced,
                preferred_element_type=F32,
            )
            for slot in chosen
        ]
        high = functools.reduce(jnp.maximum, [jnp.max(score, 0, keepdims=True) for score in scores])
        exponents = [jnp.exp(score - high) for score in scores]
        total = sum(jnp.sum(exponent, 0, keepdims=True) for exponent in exponents)
        probs = jnp.concatenate([exponent.astype(BF16) for exponent in exponents], 0)
        there = table[entry * 6 + shelf * 3 + 2] > 0
        blocks = []
        for first in range(0, count, bundle):
            here = slice(first * head_width, (first + bundle) * head_width)
            value = jnp.concatenate([values[shelf][side, slot, here, :] for slot in chosen], 1)
            mixed = jnp.dot(value, probs[:, first * rows : (first + bundle) * rows], preferred_element_type=F32)
            for head in range(bundle):
                blocks.append(
                    mixed[head * head_width : (head + 1) * head_width, head * rows : (head + 1) * rows]
                )
        shelves.append((jnp.where(there, high, FLOOR), jnp.where(there, total, 0.0), blocks, there))
    high = functools.reduce(jnp.maximum, [shelf[0] for shelf in shelves])
    factors = [jnp.where(there, jnp.exp(shelf_high - high), 0.0) for shelf_high, _, _, there in shelves]
    total = sum(shelf[1] * factor for shelf, factor in zip(shelves, factors))
    for head in range(count):
        here = slice(head * rows, (head + 1) * rows)
        joined = sum(shelf[2][head] * factor[:, here] for shelf, factor in zip(shelves, factors))
        out[z, head * head_width : (head + 1) * head_width, :] = joined.astype(BF16)
    out[z, width:, :] = pack_stats(high, total, count, rows)


def attend_kernel(place, table, key_own, key_pair, value_own, value_pair, *refs, **fixed):
    *pieces, out, rows_scratch = refs
    for z in range(out.shape[0]):
        keys, values = (key_own, key_pair), (value_own, value_pair)
        attend_group(z, place, table, pieces, keys, values, out, rows_scratch, **fixed)


def pack_stats(high, total, count, rows):
    places = lax.broadcasted_iota(jnp.int32, (STAT_ROWS, rows), 0)
    packed = jnp.zeros((STAT_ROWS, rows), F32)
    for head in range(count):
        here = slice(head * rows, (head + 1) * rows)
        for at, term in enumerate(thirds(high[:, here]) + thirds(total[:, here])):
            packed = jnp.where(places == head * 6 + at, term, packed)
    return packed.astype(BF16)


def attend(place, table, pieces, keys, values, offset, column, inner, head_width):
    outer, pair, part, half = pieces[0].shape
    width = half // len(pieces)
    rows = len(pieces) * pair * part
    tokens = values[0].shape[3]
    whole = pl.BlockSpec(memory_space=pltpu.VMEM)
    return pl.pallas_call(
        functools.partial(attend_kernel, offset=offset, column=column, inner=inner, head_width=head_width),
        in_specs=[SCALARS, SCALARS] + [whole] * (4 + len(pieces)),
        out_specs=whole,
        scratch_shapes=[pltpu.VMEM((outer, rows, width), BF16)],
        out_shape=jax.ShapeDtypeStruct((outer, width + STAT_ROWS, rows), BF16),
        compiler_params=grant(),
        cost_estimate=pl.CostEstimate(
            flops=outer * 4 * 4 * rows * tokens * width * (width // head_width),
            bytes_accessed=outer * 2 * (width + STAT_ROWS) * rows,
            transcendentals=outer * 4 * rows * tokens * (width // head_width),
        ),
        name="attend",
    )(place, table, *keys, *values, *pieces)


def stage_kernel(table, key_own, key_pair, value_own, value_pair, queries, out):
    hand_on(table, out)


def stage(table, keys, values, queries):
    whole = pl.BlockSpec(memory_space=pltpu.VMEM)
    return pl.pallas_call(
        stage_kernel,
        in_specs=[SCALARS] + [whole] * 4 + [pl.BlockSpec(memory_space=pl.ANY)],
        out_specs=SCALARS,
        out_shape=jax.ShapeDtypeStruct(table.shape, table.dtype),
        compiler_params=grant(),
        cost_estimate=pl.CostEstimate(flops=0, bytes_accessed=8 * 1024 * 1024, transcendentals=0),
        name="stage",
    )(table, *keys, *values, queries)


def join_kernel(ready, first, second, out):
    half = first.shape[0]
    out[:half] = first[...]
    out[half:] = second[...]


def join(ready, first, second):
    whole = pl.BlockSpec(memory_space=pltpu.VMEM)
    return pl.pallas_call(
        join_kernel,
        in_specs=[SCALARS, whole, whole],
        out_specs=whole,
        out_shape=jax.ShapeDtypeStruct((2 * first.shape[0],) + first.shape[1:], first.dtype),
        compiler_params=grant(),
        name="join",
    )(ready, first, second)


def unpack_stats(packed, width, count):
    tail = packed[width:, :].astype(F32)
    highs, totals = [], []
    for head in range(count):
        base = head * 6
        highs.append(tail[base : base + 1] + tail[base + 1 : base + 2] + tail[base + 2 : base + 3])
        totals.append(tail[base + 3 : base + 4] + tail[base + 4 : base + 5] + tail[base + 5 : base + 6])
    return highs, totals


def merge_heads(parts, width, head_width):
    count = width // head_width
    stats = [unpack_stats(part, width, count) for part in parts]
    mixes, highs, totals = [], [], []
    for head in range(count):
        high = functools.reduce(jnp.maximum, [stat[0][head] for stat in stats])
        mixed, total = 0.0, 0.0
        for part, stat in zip(parts, stats):
            factor = jnp.where(stat[1][head] > 0, jnp.exp(stat[0][head] - high), 0.0)
            total = total + stat[1][head] * factor
            mixed = mixed + part[head * head_width : (head + 1) * head_width, :].astype(F32) * factor
        mixes.append(mixed)
        highs.append(high)
        totals.append(total)
    return mixes, highs, totals


def gather_kernel(place, *refs, outer, head_width):
    parts, outs = refs[:-outer], refs[-outer:]
    rows = outs[0].shape[1]
    width = outs[0].shape[0] - STAT_ROWS
    count = width // head_width
    for step, out in enumerate(outs):
        z = lax.bitwise_xor(place[3], step)
        mixes, highs, totals = merge_heads([part[z] for part in parts], width, head_width)
        for head in range(count):
            out[head * head_width : (head + 1) * head_width, :] = mixes[head].astype(BF16)
        out[width:, :] = pack_stats(jnp.concatenate(highs, 1), jnp.concatenate(totals, 1), count, rows)


def merge_lots(place, parts, head_width):
    outer, height, rows = parts[0].shape
    whole = pl.BlockSpec(memory_space=pltpu.VMEM)
    return pl.pallas_call(
        functools.partial(gather_kernel, outer=outer, head_width=head_width),
        in_specs=[SCALARS] + [whole] * len(parts),
        out_specs=[whole] * outer,
        out_shape=[jax.ShapeDtypeStruct((height, rows), BF16)] * outer,
        compiler_params=grant(),
        name="merge_lots",
    )(place, *parts)


def finish_kernel(*refs, head_width):
    *parts, out = refs
    width = out.shape[1]
    mixes, _, totals = merge_heads([part[...] for part in parts], width, head_width)
    done = jnp.concatenate([mixed / total for mixed, total in zip(mixes, totals)], 0)
    out[...] = done.T.astype(BF16)


def finish(parts, head_width):
    whole = pl.BlockSpec(memory_space=pltpu.VMEM)
    return pl.pallas_call(
        functools.partial(finish_kernel, head_width=head_width),
        in_specs=[whole] * len(parts),
        out_specs=whole,
        out_shape=jax.ShapeDtypeStruct((parts[0].shape[1], parts[0].shape[0] - STAT_ROWS), BF16),
        compiler_params=grant(),
        name="finish",
    )(*parts)


def local(
    queries,
    passages,
    noise,
    mix_weight,
    answer_queries,
    key_weight,
    value_weight,
    token_states,
    block_owner,
    listed,
):
    readers = lax.axis_size("pb")
    runners = lax.axis_size("pa")
    group = lax.axis_index("pb")
    runner = lax.axis_index("pa")
    spread = runners // PAIR
    inner = 1
    while (2 * inner) * (2 * inner) <= readers:
        inner *= 2
    outer = readers // inner
    model_width = key_weight.shape[0]
    head_width = model_width // HEADS
    slots, tokens = token_states.shape[:2]
    place = jnp.stack([runner % PAIR, runner // PAIR, group % inner, group // inner]).astype(jnp.int32)

    def swap(value, axis, bits):
        size = lax.axis_size(axis)
        return lax.ppermute(value, axis, [(at, at ^ bits) for at in range(size)])

    states = token_states.reshape(slots * tokens, model_width)
    pair_states = swap(states, "pa", 1)

    wanted = jnp.take(block_owner, listed[0], axis=0)
    wanted = jnp.concatenate([wanted, swap(wanted, "pa", 1)])
    digits = jnp.concatenate([wanted // LANES, wanted % LANES]).astype(F32)
    note = jnp.pad(digits[None], ((0, 0), (NOTE_AT, LANES - NOTE_AT - digits.shape[0])))
    keep, send = retrieve(place, queries, passages, noise, readers, spread)
    *by_column, place_own = merge_pair(place, keep, swap(send, "pa", 1), spread)
    parts = [by_column[0]] + [swap(by_column[at], "pa", at * PAIR) for at in range(1, spread)]
    own_key, own_value, own_done = project(place_own, states, key_weight, value_weight, spread, tokens)
    by_group, place_pair = merge_columns(place, note, own_done, parts)
    mine = lax.all_to_all(by_group, "pb", split_axis=0, concat_axis=0, tiled=True)
    pair_key, pair_value, pair_done = project(place_pair, pair_states, key_weight, value_weight, spread, tokens)
    keys, values = (own_key, pair_key), (own_value, pair_value)
    kept, sent = condition(place, mine, mix_weight, answer_queries, pair_done, spread)

    digits = mine[:, 0, queries.shape[1] + NOTE_AT :][:, : digits.shape[0]].astype(jnp.int32)
    slot_ids = digits[:, : wanted.shape[0]] * LANES + digits[:, wanted.shape[0] :]
    slot_ids = slot_ids.reshape(readers, PAIR, -1)
    holder = (runner ^ jnp.arange(PAIR, dtype=jnp.int32)) * readers + group
    held = slot_ids // slots == holder[None, :, None]
    inside = slot_ids % slots
    table = jnp.stack(
        [
            jnp.min(jnp.where(held, inside, slots - 1), 2),
            jnp.max(jnp.where(held, inside, 0), 2),
            jnp.any(held, 2).astype(jnp.int32),
        ],
        2,
    ).reshape(-1)

    pieces = jnp.stack([kept, swap(sent, "pa", 1)])[None]
    step = inner
    while 2 * step < readers:
        pieces = jnp.concatenate([pieces, swap(pieces, "pb", step)], 0)
        step *= 2
    ready = stage(table, keys, values, pieces)
    pieces = join(ready, pieces, swap(pieces, "pb", step))
    near = [pieces] + [swap(pieces, "pa", at * PAIR) for at in range(1, spread)]
    far = [near]
    for offset in range(1, inner):
        far.append([swap(piece, "pb", offset) for piece in near])
    lots = []
    for offset, column in [(o, c) for o in range(inner) for c in range(spread)][1:] + [(0, 0)]:
        lot = attend(place, ready, far[offset], keys, values, offset, column, inner, head_width)
        bits = column * PAIR * readers + offset
        if bits:
            lot = lax.ppermute(lot, ("pa", "pb"), [(at, at ^ bits) for at in range(runners * readers)])
        lots.append(lot)
    kept, *away = merge_lots(place, lots, head_width)
    back = [swap(part, "pb", (step + 1) * inner) for step, part in enumerate(away)]
    return finish([kept] + back, head_width)


def solution(mesh):
    return jax.shard_map(
        local,
        mesh=mesh,
        in_specs=(
            P(),
            P(("pa", "pb"), None),
            P(None, ("pa", "pb")),
            P(),
            P("pb", None),
            P(),
            P(),
            P(("pa", "pb"), None, None),
            P(),
            P("pb", "pa"),
        ),
        out_specs=P("pb", "pa"),
        check_vma=False,
    )
```

```python
import functools

import jax
import jax.numpy as jnp
from jax import lax
from jax.experimental import pallas as pl
from jax.experimental.pallas import tpu as pltpu
from jax.sharding import PartitionSpec as P

HEADS = 16
PAIR = 2
CAP = 2
TEMPER = 0.5
FLOOR = -1e30
LANES = 128
STAT_ROWS = 32
NOTE_AT = 6
STEP_GROUPS = 2
PROJECT_STEPS = 4
HINT = 16
HEAD_BUNDLE = 2
VMEM_BYTES = 16 * 1024 * 1024
WIDE_BYTES = 62 * 1024 * 1024
F32 = jnp.float32
BF16 = jnp.bfloat16
NT = (((1,), (1,)), ((), ()))
SCALARS = pl.BlockSpec(memory_space=pltpu.SMEM)


def grant():
    return pltpu.CompilerParams(vmem_limit_bytes=VMEM_BYTES)


def thirds(value):
    first = value.astype(BF16).astype(F32)
    rest = value - first
    second = rest.astype(BF16).astype(F32)
    return first, second, rest - second


def pack_tail(shift, total):
    lane = lax.broadcasted_iota(jnp.int32, (shift.shape[0], LANES), 1)
    tail = jnp.zeros((shift.shape[0], LANES), F32)
    for at, term in enumerate(thirds(shift) + thirds(total)):
        tail = jnp.where(lane == at, term, tail)
    return tail


def unpack_tail(tail):
    term = lax.broadcasted_iota(jnp.int32, (LANES, 2 * LANES), 0)
    half = lax.broadcasted_iota(jnp.int32, (LANES, 2 * LANES), 1) // LANES
    pick = jnp.where(term // 3 == half, 1.0, 0.0).astype(BF16)
    both = jnp.dot(tail, pick, preferred_element_type=F32)
    return both[:, :LANES], both[:, LANES:]


def merge_rows(parts):
    width = parts[0].shape[1] - LANES
    stats = [unpack_tail(part[:, width:]) for part in parts]
    shift = functools.reduce(jnp.maximum, [stat[0] for stat in stats])
    factors = [jnp.exp(stat[0] - shift) for stat in stats]
    total = sum(stat[1] * factor for stat, factor in zip(stats, factors))
    tiles = [
        sum(part[:, at : at + LANES].astype(F32) * factor for part, factor in zip(parts, factors))
        for at in range(0, width, LANES)
    ]
    return tiles, shift, total


def flat(value):
    return value.reshape((-1, value.shape[-1]))


def retrieval_kernel(place, queries, passages, noise, keep, send, rows_scratch, *, spread):
    core = place[0]
    groups, part = keep.shape[1:3]
    width = queries.shape[1]
    logits = lax.dot_general(queries[...], passages[...], NT, preferred_element_type=F32)
    gumbel = -jnp.log(-jnp.log(noise[...].astype(F32)))
    scores = (logits * width ** (-0.5) + gumbel) * (1 / TEMPER)
    shift = jnp.max(scores, 1, keepdims=True)
    weight = jnp.exp(scores - shift)
    total = jnp.sum(weight, 1, keepdims=True)
    rows_scratch[:, :width] = jnp.dot(weight.astype(BF16), passages[...], preferred_element_type=F32)
    rows_scratch[:, width:] = pack_tail(shift, total)
    for at in range(groups):
        for column in range(spread):
            base = (at * spread + column) * PAIR
            mine = pl.multiple_of((base + core) * part, part)
            other = pl.multiple_of((base + 1 - core) * part, part)
            keep[column, at] = rows_scratch[pl.ds(mine, part), :].astype(BF16)
            send[column, at] = rows_scratch[pl.ds(other, part), :].astype(BF16)


def retrieve(place, queries, passages, noise, readers, spread):
    count, width = queries.shape
    group = count // readers
    part = group // (PAIR * spread)
    shape = jax.ShapeDtypeStruct((spread, readers, part, width + LANES), BF16)
    spec = pl.BlockSpec((spread, STEP_GROUPS, part, width + LANES), lambda g, place: (0, g, 0, 0))
    rows = group * STEP_GROUPS
    return pl.pallas_call(
        functools.partial(retrieval_kernel, spread=spread),
        grid_spec=pltpu.PrefetchScalarGridSpec(
            num_scalar_prefetch=1,
            grid=(readers // STEP_GROUPS,),
            in_specs=[
                pl.BlockSpec((rows, width), lambda g, place: (g, 0)),
                pl.BlockSpec(passages.shape, lambda g, place: (0, 0)),
                pl.BlockSpec((rows, noise.shape[1]), lambda g, place: (g, 0)),
            ],
            out_specs=[spec, spec],
            scratch_shapes=[pltpu.VMEM((rows, width + LANES), F32)],
        ),
        out_shape=[shape, shape],
        compiler_params=pltpu.CompilerParams(vmem_limit_bytes=WIDE_BYTES),
        cost_estimate=pl.CostEstimate(
            flops=4 * count * width * passages.shape[0],
            bytes_accessed=2 * (2 * count * width + passages.size + noise.size),
            transcendentals=3 * noise.size,
        ),
        name="retrieve",
    )(place, queries, passages, noise)


def store_rows(out, tiles, shift, total, note=None):
    for at, tile in enumerate(tiles):
        out[..., at * LANES : (at + 1) * LANES] = tile.astype(BF16).reshape(out.shape[:-1] + (LANES,))
    tail = pack_tail(shift, total)
    if note is not None:
        tail = tail + note
    out[..., len(tiles) * LANES :] = tail.astype(BF16).reshape(out.shape[:-1] + (LANES,))


def hand_on(place, out):
    for at in range(out.shape[0]):
        out[at] = place[at]


def pair_kernel(place, keep, recv, *outs):
    *outs, later = outs
    hand_on(place, later)
    for offset, out in enumerate(outs):
        column = lax.bitwise_xor(place[1], offset)
        store_rows(out, *merge_rows([flat(keep[column]), flat(recv[column])]))


def merge_pair(place, keep, recv, spread):
    readers = keep.shape[1]
    spec = pl.BlockSpec((spread, readers // 2) + keep.shape[2:], lambda g, place: (0, g, 0, 0))
    out = pl.BlockSpec((readers // 2,) + keep.shape[2:], lambda g, place: (g, 0, 0))
    return pl.pallas_call(
        pair_kernel,
        grid_spec=pltpu.PrefetchScalarGridSpec(
            num_scalar_prefetch=1, grid=(2,), in_specs=[spec, spec], out_specs=[out] * spread + [SCALARS]
        ),
        out_shape=[jax.ShapeDtypeStruct(keep.shape[1:], BF16)] * spread
        + [jax.ShapeDtypeStruct(place.shape, place.dtype)],
        compiler_params=grant(),
        name="merge_pair",
    )(place, keep, recv)


def column_kernel(place, note, done, *refs):
    *parts, out, later = refs
    hand_on(place, later)
    store_rows(out, *merge_rows([flat(part[...]) for part in parts]), note[...] + done[0:1, :])


def merge_columns(place, note, done, parts):
    readers = parts[0].shape[0]
    spec = pl.BlockSpec((readers // 2,) + parts[0].shape[1:], lambda g, place: (g, 0, 0))
    return pl.pallas_call(
        column_kernel,
        grid_spec=pltpu.PrefetchScalarGridSpec(
            num_scalar_prefetch=1,
            grid=(2,),
            in_specs=[
                pl.BlockSpec(note.shape, lambda g, place: (0, 0)),
                pl.BlockSpec(done.shape, lambda g, place: (0, 0)),
            ]
            + [spec] * len(parts),
            out_specs=[spec, SCALARS],
        ),
        out_shape=[
            jax.ShapeDtypeStruct(parts[0].shape, BF16),
            jax.ShapeDtypeStruct(place.shape, place.dtype),
        ],
        compiler_params=grant(),
        name="merge_columns",
    )(place, note, done, *parts)


def condition_kernel(place, parts, mix_weight, answers, done, keep, send, rows_scratch, *, spread):
    tiles, _, total = merge_rows([parts[at] for at in range(parts.shape[0])])
    blended_half = jnp.concatenate([(tile / total).astype(BF16) for tile in tiles], 1)
    part = blended_half.shape[0]
    start = pl.multiple_of((place[1] * PAIR + place[0]) * part, part)
    answer = answers[pl.ds(start, part), :].astype(F32)
    rows_scratch[...] = answer + jnp.dot(blended_half, mix_weight[...], preferred_element_type=F32)
    stride = keep.shape[1] // spread
    for column in range(spread):
        mine = pl.multiple_of((column * PAIR + place[0]) * stride, stride)
        other = pl.multiple_of((column * PAIR + 1 - place[0]) * stride, stride)
        keep[:, column * stride : (column + 1) * stride] = rows_scratch[:, pl.ds(mine, stride)].astype(BF16)
        send[:, column * stride : (column + 1) * stride] = rows_scratch[:, pl.ds(other, stride)].astype(BF16)


def condition(place, parts, mix_weight, answers, done, spread):
    model_width = mix_weight.shape[1]
    shape = jax.ShapeDtypeStruct((parts.shape[1], model_width // PAIR), BF16)
    whole = pl.BlockSpec(memory_space=pltpu.VMEM)
    return pl.pallas_call(
        functools.partial(condition_kernel, spread=spread),
        in_specs=[SCALARS, whole, whole, whole, whole],
        out_specs=[whole, whole],
        out_shape=[shape, shape],
        scratch_shapes=[pltpu.VMEM((parts.shape[1], model_width), F32)],
        compiler_params=grant(),
        name="condition",
    )(place, parts, mix_weight, answers, done)


def project_kernel(place, states, *refs):
    spread = (len(refs) - 3) // 2
    keys, values, done = refs[-3:]
    done[...] = jnp.zeros_like(done)
    tokens = values.shape[3]
    for column in range(spread):
        keys[column] = jnp.dot(states[...], refs[column][...], preferred_element_type=F32).astype(BF16)
        value = jnp.dot(states[...], refs[spread + column][...], preferred_element_type=F32).astype(BF16)
        for block in range(values.shape[1]):
            values[column, block] = value[block * tokens : (block + 1) * tokens].T


def project(place, states, key_weight, value_weight, spread, tokens):
    rows, model_width = states.shape
    width = model_width // (PAIR * spread)
    chunk = rows // PROJECT_STEPS
    blocks = chunk // tokens

    def weight_spec(column):
        return pl.BlockSpec((model_width, width), lambda t, place: (0, column * PAIR + place[0]))

    specs = [weight_spec(column) for column in range(spread)]
    return pl.pallas_call(
        project_kernel,
        grid_spec=pltpu.PrefetchScalarGridSpec(
            num_scalar_prefetch=1,
            grid=(PROJECT_STEPS,),
            in_specs=[pl.BlockSpec((chunk, model_width), lambda t, place: (t, 0))] + specs + specs,
            out_specs=[
                pl.BlockSpec((spread, chunk, width), lambda t, place: (0, t, 0)),
                pl.BlockSpec((spread, blocks, width, tokens), lambda t, place: (0, t, 0, 0)),
                pl.BlockSpec((8, LANES), lambda t, place: (0, 0)),
            ],
        ),
        out_shape=[
            jax.ShapeDtypeStruct((spread, rows, width), BF16),
            jax.ShapeDtypeStruct((spread, rows // tokens, width, tokens), BF16),
            jax.ShapeDtypeStruct((8, LANES), F32),
        ],
        compiler_params=pltpu.CompilerParams(vmem_limit_bytes=WIDE_BYTES),
        cost_estimate=pl.CostEstimate(
            flops=4 * rows * model_width * spread * width // HINT,
            bytes_accessed=2 * (2 * model_width * spread * width + 2 * rows * model_width) // HINT,
            transcendentals=0,
        ),
        name="project",
    )(place, states, *([key_weight] * spread), *([value_weight] * spread))


def attend_group(z, place, table, pieces, keys, values, out, rows_scratch, offset, column, inner, head_width):
    relative = lax.bitwise_xor(z, place[3])
    part, rows = pieces[0].shape[2], out.shape[2]
    width = out.shape[1] - STAT_ROWS
    count = width // head_width
    side = lax.bitwise_xor(place[1], column)
    left = pl.multiple_of(side * width, width)
    for step, piece in enumerate(pieces):
        for core in range(PAIR):
            top = lax.bitwise_xor(place[1], step) * PAIR + lax.bitwise_xor(place[0], core)
            top = pl.multiple_of(top * part, part)
            rows_scratch[z, pl.ds(top, part), :] = piece[relative, core, :, pl.ds(left, width)]
    query = rows_scratch[z].T
    tokens = values[0].shape[3]
    head_at = lax.broadcasted_iota(jnp.int32, query.shape, 0) // head_width
    spaced = jnp.concatenate([jnp.where(head_at == head, query, jnp.zeros_like(query)) for head in range(count)], 1)
    entry = z * inner + lax.bitwise_xor(place[2], offset)
    bundle = min(HEAD_BUNDLE, count)
    shelves = []
    for shelf in range(PAIR):
        chosen = [table[entry * 6 + shelf * 3 + at] for at in range(CAP)]
        scores = [
            jnp.dot(
                keys[shelf][side, pl.ds(pl.multiple_of(slot * tokens, tokens), tokens), :],
                spaced,
                preferred_element_type=F32,
            )
            for slot in chosen
        ]
        high = functools.reduce(jnp.maximum, [jnp.max(score, 0, keepdims=True) for score in scores])
        exponents = [jnp.exp(score - high) for score in scores]
        total = sum(jnp.sum(exponent, 0, keepdims=True) for exponent in exponents)
        probs = jnp.concatenate([exponent.astype(BF16) for exponent in exponents], 0)
        there = table[entry * 6 + shelf * 3 + 2] > 0
        blocks = []
        for first in range(0, count, bundle):
            here = slice(first * head_width, (first + bundle) * head_width)
            value = jnp.concatenate([values[shelf][side, slot, here, :] for slot in chosen], 1)
            mixed = jnp.dot(value, probs[:, first * rows : (first + bundle) * rows], preferred_element_type=F32)
            for head in range(bundle):
                blocks.append(
                    mixed[head * head_width : (head + 1) * head_width, head * rows : (head + 1) * rows]
                )
        shelves.append((jnp.where(there, high, FLOOR), jnp.where(there, total, 0.0), blocks, there))
    high = functools.reduce(jnp.maximum, [shelf[0] for shelf in shelves])
    factors = [jnp.where(there, jnp.exp(shelf_high - high), 0.0) for shelf_high, _, _, there in shelves]
    total = sum(shelf[1] * factor for shelf, factor in zip(shelves, factors))
    for head in range(count):
        here = slice(head * rows, (head + 1) * rows)
        joined = sum(shelf[2][head] * factor[:, here] for shelf, factor in zip(shelves, factors))
        out[z, head * head_width : (head + 1) * head_width, :] = joined.astype(BF16)
    out[z, width:, :] = pack_stats(high, total, count, rows)


def attend_kernel(place, table, key_own, key_pair, value_own, value_pair, *refs, **fixed):
    *pieces, out, rows_scratch = refs
    for z in range(out.shape[0]):
        keys, values = (key_own, key_pair), (value_own, value_pair)
        attend_group(z, place, table, pieces, keys, values, out, rows_scratch, **fixed)


def pack_stats(high, total, count, rows):
    places = lax.broadcasted_iota(jnp.int32, (STAT_ROWS, rows), 0)
    packed = jnp.zeros((STAT_ROWS, rows), F32)
    for head in range(count):
        here = slice(head * rows, (head + 1) * rows)
        for at, term in enumerate(thirds(high[:, here]) + thirds(total[:, here])):
            packed = jnp.where(places == head * 6 + at, term, packed)
    return packed.astype(BF16)


def attend(place, table, pieces, keys, values, offset, column, inner, head_width):
    outer, pair, part, half = pieces[0].shape
    width = half // len(pieces)
    rows = len(pieces) * pair * part
    tokens = values[0].shape[3]
    whole = pl.BlockSpec(memory_space=pltpu.VMEM)
    return pl.pallas_call(
        functools.partial(attend_kernel, offset=offset, column=column, inner=inner, head_width=head_width),
        in_specs=[SCALARS, SCALARS] + [whole] * (4 + len(pieces)),
        out_specs=whole,
        scratch_shapes=[pltpu.VMEM((outer, rows, width), BF16)],
        out_shape=jax.ShapeDtypeStruct((outer, width + STAT_ROWS, rows), BF16),
        compiler_params=grant(),
        cost_estimate=pl.CostEstimate(
            flops=outer * 4 * 4 * rows * tokens * width * (width // head_width),
            bytes_accessed=outer * 2 * (width + STAT_ROWS) * rows,
            transcendentals=outer * 4 * rows * tokens * (width // head_width),
        ),
        name="attend",
    )(place, table, *keys, *values, *pieces)


def stage_kernel(table, key_own, key_pair, value_own, value_pair, queries, out):
    hand_on(table, out)


def stage(table, keys, values, queries):
    whole = pl.BlockSpec(memory_space=pltpu.VMEM)
    return pl.pallas_call(
        stage_kernel,
        in_specs=[SCALARS] + [whole] * 4 + [pl.BlockSpec(memory_space=pl.ANY)],
        out_specs=SCALARS,
        out_shape=jax.ShapeDtypeStruct(table.shape, table.dtype),
        compiler_params=grant(),
        cost_estimate=pl.CostEstimate(flops=0, bytes_accessed=8 * 1024 * 1024, transcendentals=0),
        name="stage",
    )(table, *keys, *values, queries)


def join_kernel(ready, first, second, out):
    half = first.shape[0]
    out[:half] = first[...]
    out[half:] = second[...]


def join(ready, first, second):
    whole = pl.BlockSpec(memory_space=pltpu.VMEM)
    return pl.pallas_call(
        join_kernel,
        in_specs=[SCALARS, whole, whole],
        out_specs=whole,
        out_shape=jax.ShapeDtypeStruct((2 * first.shape[0],) + first.shape[1:], first.dtype),
        compiler_params=grant(),
        name="join",
    )(ready, first, second)


def unpack_stats(packed, width, count):
    tail = packed[width:, :].astype(F32)
    highs, totals = [], []
    for head in range(count):
        base = head * 6
        highs.append(tail[base : base + 1] + tail[base + 1 : base + 2] + tail[base + 2 : base + 3])
        totals.append(tail[base + 3 : base + 4] + tail[base + 4 : base + 5] + tail[base + 5 : base + 6])
    return highs, totals


def merge_heads(parts, width, head_width):
    count = width // head_width
    stats = [unpack_stats(part, width, count) for part in parts]
    mixes, highs, totals = [], [], []
    for head in range(count):
        high = functools.reduce(jnp.maximum, [stat[0][head] for stat in stats])
        mixed, total = 0.0, 0.0
        for part, stat in zip(parts, stats):
            factor = jnp.where(stat[1][head] > 0, jnp.exp(stat[0][head] - high), 0.0)
            total = total + stat[1][head] * factor
            mixed = mixed + part[head * head_width : (head + 1) * head_width, :].astype(F32) * factor
        mixes.append(mixed)
        highs.append(high)
        totals.append(total)
    return mixes, highs, totals


def gather_kernel(place, *refs, outer, head_width):
    parts, outs = refs[:-outer], refs[-outer:]
    rows = outs[0].shape[1]
    width = outs[0].shape[0] - STAT_ROWS
    count = width // head_width
    for step, out in enumerate(outs):
        z = lax.bitwise_xor(place[3], step)
        mixes, highs, totals = merge_heads([part[z] for part in parts], width, head_width)
        for head in range(count):
            out[head * head_width : (head + 1) * head_width, :] = mixes[head].astype(BF16)
        out[width:, :] = pack_stats(jnp.concatenate(highs, 1), jnp.concatenate(totals, 1), count, rows)


def merge_lots(place, parts, head_width):
    outer, height, rows = parts[0].shape
    whole = pl.BlockSpec(memory_space=pltpu.VMEM)
    return pl.pallas_call(
        functools.partial(gather_kernel, outer=outer, head_width=head_width),
        in_specs=[SCALARS] + [whole] * len(parts),
        out_specs=[whole] * outer,
        out_shape=[jax.ShapeDtypeStruct((height, rows), BF16)] * outer,
        compiler_params=grant(),
        name="merge_lots",
    )(place, *parts)


def finish_kernel(*refs, head_width):
    *parts, out = refs
    width = out.shape[1]
    mixes, _, totals = merge_heads([part[...] for part in parts], width, head_width)
    done = jnp.concatenate([mixed / total for mixed, total in zip(mixes, totals)], 0)
    out[...] = done.T.astype(BF16)


def finish(parts, head_width):
    whole = pl.BlockSpec(memory_space=pltpu.VMEM)
    return pl.pallas_call(
        functools.partial(finish_kernel, head_width=head_width),
        in_specs=[whole] * len(parts),
        out_specs=whole,
        out_shape=jax.ShapeDtypeStruct((parts[0].shape[1], parts[0].shape[0] - STAT_ROWS), BF16),
        compiler_params=grant(),
        name="finish",
    )(*parts)


def local(
    queries,
    passages,
    noise,
    mix_weight,
    answer_queries,
    key_weight,
    value_weight,
    token_states,
    block_owner,
    listed,
):
    readers = lax.axis_size("pb")
    runners = lax.axis_size("pa")
    group = lax.axis_index("pb")
    runner = lax.axis_index("pa")
    spread = runners // PAIR
    inner = 1
    while (2 * inner) * (2 * inner) <= readers:
        inner *= 2
    outer = readers // inner
    model_width = key_weight.shape[0]
    head_width = model_width // HEADS
    slots, tokens = token_states.shape[:2]
    place = jnp.stack([runner % PAIR, runner // PAIR, group % inner, group // inner]).astype(jnp.int32)

    def swap(value, axis, bits):
        size = lax.axis_size(axis)
        return lax.ppermute(value, axis, [(at, at ^ bits) for at in range(size)])

    states = token_states.reshape(slots * tokens, model_width)
    pair_states = swap(states, "pa", 1)

    wanted = jnp.take(block_owner, listed[0], axis=0)
    wanted = jnp.concatenate([wanted, swap(wanted, "pa", 1)])
    digits = jnp.concatenate([wanted // LANES, wanted % LANES]).astype(F32)
    note = jnp.pad(digits[None], ((0, 0), (NOTE_AT, LANES - NOTE_AT - digits.shape[0])))
    keep, send = retrieve(place, queries, passages, noise, readers, spread)
    *by_column, place_own = merge_pair(place, keep, swap(send, "pa", 1), spread)
    parts = [by_column[0]] + [swap(by_column[at], "pa", at * PAIR) for at in range(1, spread)]
    own_key, own_value, own_done = project(place_own, states, key_weight, value_weight, spread, tokens)
    by_group, place_pair = merge_columns(place, note, own_done, parts)
    mine = lax.all_to_all(by_group, "pb", split_axis=0, concat_axis=0, tiled=True)
    pair_key, pair_value, pair_done = project(place_pair, pair_states, key_weight, value_weight, spread, tokens)
    keys, values = (own_key, pair_key), (own_value, pair_value)
    kept, sent = condition(place, mine, mix_weight, answer_queries, pair_done, spread)

    digits = mine[:, 0, queries.shape[1] + NOTE_AT :][:, : digits.shape[0]].astype(jnp.int32)
    slot_ids = digits[:, : wanted.shape[0]] * LANES + digits[:, wanted.shape[0] :]
    slot_ids = slot_ids.reshape(readers, PAIR, -1)
    holder = (runner ^ jnp.arange(PAIR, dtype=jnp.int32)) * readers + group
    held = slot_ids // slots == holder[None, :, None]
    inside = slot_ids % slots
    table = jnp.stack(
        [
            jnp.min(jnp.where(held, inside, slots - 1), 2),
            jnp.max(jnp.where(held, inside, 0), 2),
            jnp.any(held, 2).astype(jnp.int32),
        ],
        2,
    ).reshape(-1)

    pieces = jnp.stack([kept, swap(sent, "pa", 1)])[None]
    step = inner
    while 2 * step < readers:
        pieces = jnp.concatenate([pieces, swap(pieces, "pb", step)], 0)
        step *= 2
    ready = stage(table, keys, values, pieces)
    pieces = join(ready, pieces, swap(pieces, "pb", step))
    near = [pieces] + [swap(pieces, "pa", at * PAIR) for at in range(1, spread)]
    far = [near]
    for offset in range(1, inner):
        far.append([swap(piece, "pb", offset) for piece in near])
    lots = []
    for offset, column in [(o, c) for o in range(inner) for c in range(spread)][1:] + [(0, 0)]:
        lot = attend(place, ready, far[offset], keys, values, offset, column, inner, head_width)
        bits = column * PAIR * readers + offset
        if bits:
            lot = lax.ppermute(lot, ("pa", "pb"), [(at, at ^ bits) for at in range(runners * readers)])
        lots.append(lot)
    kept, *away = merge_lots(place, lots, head_width)
    back = [swap(part, "pb", (step + 1) * inner) for step, part in enumerate(away)]
    return finish([kept] + back, head_width)


def solution(mesh):
    return jax.shard_map(
        local,
        mesh=mesh,
        in_specs=(
            P(),
            P(("pa", "pb"), None),
            P(None, ("pa", "pb")),
            P(),
            P("pb", None),
            P(),
            P(),
            P(("pa", "pb"), None, None),
            P(),
            P("pb", "pa"),
        ),
        out_specs=P("pb", "pa"),
        check_vma=False,
    )
```

```python
import functools

import jax
import jax.numpy as jnp
from jax import lax
from jax.experimental import pallas as pl
from jax.experimental.pallas import tpu as pltpu
from jax.sharding import PartitionSpec as P

HEADS = 16
PAIR = 2
CAP = 2
TEMPER = 0.5
FLOOR = -1e30
LANES = 128
STAT_ROWS = 32
NOTE_AT = 6
STEP_GROUPS = 2
PROJECT_STEPS = 4
HINT = 16
HEAD_BUNDLE = 2
VMEM_BYTES = 16 * 1024 * 1024
WIDE_BYTES = 62 * 1024 * 1024
F32 = jnp.float32
BF16 = jnp.bfloat16
NT = (((1,), (1,)), ((), ()))
SCALARS = pl.BlockSpec(memory_space=pltpu.SMEM)


def grant():
    return pltpu.CompilerParams(vmem_limit_bytes=VMEM_BYTES)


def thirds(value):
    first = value.astype(BF16).astype(F32)
    rest = value - first
    second = rest.astype(BF16).astype(F32)
    return first, second, rest - second


def pack_tail(shift, total):
    lane = lax.broadcasted_iota(jnp.int32, (shift.shape[0], LANES), 1)
    tail = jnp.zeros((shift.shape[0], LANES), F32)
    for at, term in enumerate(thirds(shift) + thirds(total)):
        tail = jnp.where(lane == at, term, tail)
    return tail


def unpack_tail(tail):
    term = lax.broadcasted_iota(jnp.int32, (LANES, 2 * LANES), 0)
    half = lax.broadcasted_iota(jnp.int32, (LANES, 2 * LANES), 1) // LANES
    pick = jnp.where(term // 3 == half, 1.0, 0.0).astype(BF16)
    both = jnp.dot(tail, pick, preferred_element_type=F32)
    return both[:, :LANES], both[:, LANES:]


def merge_rows(parts):
    width = parts[0].shape[1] - LANES
    stats = [unpack_tail(part[:, width:]) for part in parts]
    shift = functools.reduce(jnp.maximum, [stat[0] for stat in stats])
    factors = [jnp.exp(stat[0] - shift) for stat in stats]
    total = sum(stat[1] * factor for stat, factor in zip(stats, factors))
    tiles = [
        sum(part[:, at : at + LANES].astype(F32) * factor for part, factor in zip(parts, factors))
        for at in range(0, width, LANES)
    ]
    return tiles, shift, total


def flat(value):
    return value.reshape((-1, value.shape[-1]))


def retrieval_kernel(place, queries, passages, noise, keep, send, rows_scratch, *, spread):
    core = place[0]
    groups, part = keep.shape[1:3]
    width = queries.shape[1]
    logits = lax.dot_general(queries[...], passages[...], NT, preferred_element_type=F32)
    gumbel = -jnp.log(-jnp.log(noise[...].astype(F32)))
    scores = (logits * width ** (-0.5) + gumbel) * (1 / TEMPER)
    shift = jnp.max(scores, 1, keepdims=True)
    weight = jnp.exp(scores - shift)
    total = jnp.sum(weight, 1, keepdims=True)
    rows_scratch[:, :width] = jnp.dot(weight.astype(BF16), passages[...], preferred_element_type=F32)
    rows_scratch[:, width:] = pack_tail(shift, total)
    for at in range(groups):
        for column in range(spread):
            base = (at * spread + column) * PAIR
            mine = pl.multiple_of((base + core) * part, part)
            other = pl.multiple_of((base + 1 - core) * part, part)
            keep[column, at] = rows_scratch[pl.ds(mine, part), :].astype(BF16)
            send[column, at] = rows_scratch[pl.ds(other, part), :].astype(BF16)


def retrieve(place, queries, passages, noise, readers, spread):
    count, width = queries.shape
    group = count // readers
    part = group // (PAIR * spread)
    shape = jax.ShapeDtypeStruct((spread, readers, part, width + LANES), BF16)
    spec = pl.BlockSpec((spread, STEP_GROUPS, part, width + LANES), lambda g, place: (0, g, 0, 0))
    rows = group * STEP_GROUPS
    return pl.pallas_call(
        functools.partial(retrieval_kernel, spread=spread),
        grid_spec=pltpu.PrefetchScalarGridSpec(
            num_scalar_prefetch=1,
            grid=(readers // STEP_GROUPS,),
            in_specs=[
                pl.BlockSpec((rows, width), lambda g, place: (g, 0)),
                pl.BlockSpec(passages.shape, lambda g, place: (0, 0)),
                pl.BlockSpec((rows, noise.shape[1]), lambda g, place: (g, 0)),
            ],
            out_specs=[spec, spec],
            scratch_shapes=[pltpu.VMEM((rows, width + LANES), F32)],
        ),
        out_shape=[shape, shape],
        compiler_params=pltpu.CompilerParams(vmem_limit_bytes=WIDE_BYTES),
        cost_estimate=pl.CostEstimate(
            flops=4 * count * width * passages.shape[0],
            bytes_accessed=2 * (2 * count * width + passages.size + noise.size),
            transcendentals=3 * noise.size,
        ),
        name="retrieve",
    )(place, queries, passages, noise)


def store_rows(out, tiles, shift, total, note=None):
    for at, tile in enumerate(tiles):
        out[..., at * LANES : (at + 1) * LANES] = tile.astype(BF16).reshape(out.shape[:-1] + (LANES,))
    tail = pack_tail(shift, total)
    if note is not None:
        tail = tail + note
    out[..., len(tiles) * LANES :] = tail.astype(BF16).reshape(out.shape[:-1] + (LANES,))


def hand_on(place, out):
    for at in range(out.shape[0]):
        out[at] = place[at]


def pair_kernel(place, keep, recv, *outs):
    *outs, later = outs
    hand_on(place, later)
    for offset, out in enumerate(outs):
        column = lax.bitwise_xor(place[1], offset)
        store_rows(out, *merge_rows([flat(keep[column]), flat(recv[column])]))


def merge_pair(place, keep, recv, spread):
    readers = keep.shape[1]
    spec = pl.BlockSpec((spread, readers // 2) + keep.shape[2:], lambda g, place: (0, g, 0, 0))
    out = pl.BlockSpec((readers // 2,) + keep.shape[2:], lambda g, place: (g, 0, 0))
    return pl.pallas_call(
        pair_kernel,
        grid_spec=pltpu.PrefetchScalarGridSpec(
            num_scalar_prefetch=1, grid=(2,), in_specs=[spec, spec], out_specs=[out] * spread + [SCALARS]
        ),
        out_shape=[jax.ShapeDtypeStruct(keep.shape[1:], BF16)] * spread
        + [jax.ShapeDtypeStruct(place.shape, place.dtype)],
        compiler_params=grant(),
        name="merge_pair",
    )(place, keep, recv)


def column_kernel(place, note, done, *refs, inner):
    *refs, later = refs
    parts, outs = refs[:-inner], refs[-inner:]
    hand_on(place, later)
    row = lax.broadcasted_iota(jnp.int32, (outs[0].shape[1], LANES), 0)
    first = jnp.where(row == 0, note[...] + done[0:1, :], 0.0)
    for offset, out in enumerate(outs):
        for z in range(out.shape[0]):
            at = z * inner + lax.bitwise_xor(place[2], offset)
            store_rows(out.at[z], *merge_rows([part[at] for part in parts]), first)


def merge_columns(place, note, done, parts, inner):
    readers, part, width = parts[0].shape
    whole = pl.BlockSpec(memory_space=pltpu.VMEM)
    return pl.pallas_call(
        functools.partial(column_kernel, inner=inner),
        in_specs=[SCALARS] + [whole] * (2 + len(parts)),
        out_specs=[whole] * inner + [SCALARS],
        out_shape=[jax.ShapeDtypeStruct((readers // inner, part, width), BF16)] * inner
        + [jax.ShapeDtypeStruct(place.shape, place.dtype)],
        compiler_params=grant(),
        name="merge_columns",
    )(place, note, done, *parts)


def near_kernel(place, done, *refs, outer):
    parts, outs = refs[:-outer], refs[-outer:]
    shape = (outs[0].shape[0], LANES)
    row, lane = (lax.broadcasted_iota(jnp.int32, shape, at) for at in range(2))
    for step, out in enumerate(outs):
        taken = [part[lax.bitwise_xor(place[3], step)] for part in parts]
        notes = jnp.zeros(shape, F32) + done[0:1, :]
        for offset, part in enumerate(taken):
            carried = part[0:1, part.shape[1] - LANES :].astype(F32)
            notes = jnp.where((row == offset) & (lane >= NOTE_AT), carried, notes)
        store_rows(out, *merge_rows(taken), notes)


def merge_near(place, done, parts):
    outer, part, width = parts[0].shape
    whole = pl.BlockSpec(memory_space=pltpu.VMEM)
    return pl.pallas_call(
        functools.partial(near_kernel, outer=outer),
        in_specs=[SCALARS] + [whole] * (1 + len(parts)),
        out_specs=[whole] * outer,
        out_shape=[jax.ShapeDtypeStruct((part, width), BF16)] * outer,
        compiler_params=grant(),
        name="merge_near",
    )(place, done, *parts)


def condition_kernel(place, mix_weight, answers, *refs, spread):
    *parts, keep, send, rows_scratch = refs
    tiles, _, total = merge_rows([part[...] for part in parts])
    blended_half = jnp.concatenate([(tile / total).astype(BF16) for tile in tiles], 1)
    part = blended_half.shape[0]
    start = pl.multiple_of((place[1] * PAIR + place[0]) * part, part)
    answer = answers[pl.ds(start, part), :].astype(F32)
    rows_scratch[...] = answer + jnp.dot(blended_half, mix_weight[...], preferred_element_type=F32)
    stride = keep.shape[1] // spread
    for column in range(spread):
        mine = pl.multiple_of((column * PAIR + place[0]) * stride, stride)
        other = pl.multiple_of((column * PAIR + 1 - place[0]) * stride, stride)
        keep[:, column * stride : (column + 1) * stride] = rows_scratch[:, pl.ds(mine, stride)].astype(BF16)
        send[:, column * stride : (column + 1) * stride] = rows_scratch[:, pl.ds(other, stride)].astype(BF16)


def condition(place, parts, mix_weight, answers, spread):
    model_width = mix_weight.shape[1]
    shape = jax.ShapeDtypeStruct((parts[0].shape[0], model_width // PAIR), BF16)
    whole = pl.BlockSpec(memory_space=pltpu.VMEM)
    return pl.pallas_call(
        functools.partial(condition_kernel, spread=spread),
        in_specs=[SCALARS] + [whole] * (2 + len(parts)),
        out_specs=[whole, whole],
        out_shape=[shape, shape],
        scratch_shapes=[pltpu.VMEM((parts[0].shape[0], model_width), F32)],
        compiler_params=grant(),
        name="condition",
    )(place, mix_weight, answers, *parts)


def project_kernel(place, states, *refs):
    spread = (len(refs) - 3) // 2
    keys, values, done = refs[-3:]
    done[...] = jnp.zeros_like(done)
    tokens = values.shape[3]
    for column in range(spread):
        keys[column] = jnp.dot(states[...], refs[column][...], preferred_element_type=F32).astype(BF16)
        value = jnp.dot(states[...], refs[spread + column][...], preferred_element_type=F32).astype(BF16)
        for block in range(values.shape[1]):
            values[column, block] = value[block * tokens : (block + 1) * tokens].T


def project(place, states, key_weight, value_weight, spread, tokens):
    rows, model_width = states.shape
    width = model_width // (PAIR * spread)
    chunk = rows // PROJECT_STEPS
    blocks = chunk // tokens

    def weight_spec(column):
        return pl.BlockSpec((model_width, width), lambda t, place: (0, column * PAIR + place[0]))

    specs = [weight_spec(column) for column in range(spread)]
    return pl.pallas_call(
        project_kernel,
        grid_spec=pltpu.PrefetchScalarGridSpec(
            num_scalar_prefetch=1,
            grid=(PROJECT_STEPS,),
            in_specs=[pl.BlockSpec((chunk, model_width), lambda t, place: (t, 0))] + specs + specs,
            out_specs=[
                pl.BlockSpec((spread, chunk, width), lambda t, place: (0, t, 0)),
                pl.BlockSpec((spread, blocks, width, tokens), lambda t, place: (0, t, 0, 0)),
                pl.BlockSpec((8, LANES), lambda t, place: (0, 0)),
            ],
        ),
        out_shape=[
            jax.ShapeDtypeStruct((spread, rows, width), BF16),
            jax.ShapeDtypeStruct((spread, rows // tokens, width, tokens), BF16),
            jax.ShapeDtypeStruct((8, LANES), F32),
        ],
        compiler_params=pltpu.CompilerParams(vmem_limit_bytes=WIDE_BYTES),
        cost_estimate=pl.CostEstimate(
            flops=4 * rows * model_width * spread * width // HINT,
            bytes_accessed=2 * (2 * model_width * spread * width + 2 * rows * model_width) // HINT,
            transcendentals=0,
        ),
        name="project",
    )(place, states, *([key_weight] * spread), *([value_weight] * spread))


def attend_group(z, place, table, pieces, keys, values, out, rows_scratch, offset, column, inner, head_width):
    relative = lax.bitwise_xor(z, place[3])
    part, rows = pieces[0].shape[2], out.shape[2]
    width = out.shape[1] - STAT_ROWS
    count = width // head_width
    side = lax.bitwise_xor(place[1], column)
    left = pl.multiple_of(side * width, width)
    for step, piece in enumerate(pieces):
        for core in range(PAIR):
            top = lax.bitwise_xor(place[1], step) * PAIR + lax.bitwise_xor(place[0], core)
            top = pl.multiple_of(top * part, part)
            rows_scratch[z, pl.ds(top, part), :] = piece[relative, core, :, pl.ds(left, width)]
    query = rows_scratch[z].T
    tokens = values[0].shape[3]
    head_at = lax.broadcasted_iota(jnp.int32, query.shape, 0) // head_width
    spaced = jnp.concatenate([jnp.where(head_at == head, query, jnp.zeros_like(query)) for head in range(count)], 1)
    entry = relative * inner + offset
    bundle = min(HEAD_BUNDLE, count)
    shelves = []
    for shelf in range(PAIR):
        chosen = [table[entry * 6 + shelf * 3 + at] for at in range(CAP)]
        scores = [
            jnp.dot(
                keys[shelf][side, pl.ds(pl.multiple_of(slot * tokens, tokens), tokens), :],
                spaced,
                preferred_element_type=F32,
            )
            for slot in chosen
        ]
        high = functools.reduce(jnp.maximum, [jnp.max(score, 0, keepdims=True) for score in scores])
        exponents = [jnp.exp(score - high) for score in scores]
        total = sum(jnp.sum(exponent, 0, keepdims=True) for exponent in exponents)
        probs = jnp.concatenate([exponent.astype(BF16) for exponent in exponents], 0)
        there = table[entry * 6 + shelf * 3 + 2] > 0
        blocks = []
        for first in range(0, count, bundle):
            here = slice(first * head_width, (first + bundle) * head_width)
            value = jnp.concatenate([values[shelf][side, slot, here, :] for slot in chosen], 1)
            mixed = jnp.dot(value, probs[:, first * rows : (first + bundle) * rows], preferred_element_type=F32)
            for head in range(bundle):
                blocks.append(
                    mixed[head * head_width : (head + 1) * head_width, head * rows : (head + 1) * rows]
                )
        shelves.append((jnp.where(there, high, FLOOR), jnp.where(there, total, 0.0), blocks, there))
    high = functools.reduce(jnp.maximum, [shelf[0] for shelf in shelves])
    factors = [jnp.where(there, jnp.exp(shelf_high - high), 0.0) for shelf_high, _, _, there in shelves]
    total = sum(shelf[1] * factor for shelf, factor in zip(shelves, factors))
    for head in range(count):
        here = slice(head * rows, (head + 1) * rows)
        joined = sum(shelf[2][head] * factor[:, here] for shelf, factor in zip(shelves, factors))
        out[z, head * head_width : (head + 1) * head_width, :] = joined.astype(BF16)
    out[z, width:, :] = pack_stats(high, total, count, rows)


def attend_kernel(place, table, key_own, key_pair, value_own, value_pair, *refs, **fixed):
    *pieces, out, rows_scratch = refs
    for z in range(out.shape[0]):
        keys, values = (key_own, key_pair), (value_own, value_pair)
        attend_group(z, place, table, pieces, keys, values, out, rows_scratch, **fixed)


def pack_stats(high, total, count, rows):
    places = lax.broadcasted_iota(jnp.int32, (STAT_ROWS, rows), 0)
    packed = jnp.zeros((STAT_ROWS, rows), F32)
    for head in range(count):
        here = slice(head * rows, (head + 1) * rows)
        for at, term in enumerate(thirds(high[:, here]) + thirds(total[:, here])):
            packed = jnp.where(places == head * 6 + at, term, packed)
    return packed.astype(BF16)


def attend(place, table, pieces, keys, values, offset, column, inner, head_width):
    outer, pair, part, half = pieces[0].shape
    width = half // len(pieces)
    rows = len(pieces) * pair * part
    tokens = values[0].shape[3]
    whole = pl.BlockSpec(memory_space=pltpu.VMEM)
    return pl.pallas_call(
        functools.partial(attend_kernel, offset=offset, column=column, inner=inner, head_width=head_width),
        in_specs=[SCALARS, SCALARS] + [whole] * (4 + len(pieces)),
        out_specs=whole,
        scratch_shapes=[pltpu.VMEM((outer, rows, width), BF16)],
        out_shape=jax.ShapeDtypeStruct((outer, width + STAT_ROWS, rows), BF16),
        compiler_params=grant(),
        cost_estimate=pl.CostEstimate(
            flops=outer * 4 * 4 * rows * tokens * width * (width // head_width),
            bytes_accessed=outer * 2 * (width + STAT_ROWS) * rows,
            transcendentals=outer * 4 * rows * tokens * (width // head_width),
        ),
        name="attend",
    )(place, table, *keys, *values, *pieces)


def stage_kernel(table, key_own, key_pair, value_own, value_pair, queries, out):
    hand_on(table, out)


def stage(table, keys, values, queries):
    whole = pl.BlockSpec(memory_space=pltpu.VMEM)
    return pl.pallas_call(
        stage_kernel,
        in_specs=[SCALARS] + [whole] * 4 + [pl.BlockSpec(memory_space=pl.ANY)],
        out_specs=SCALARS,
        out_shape=jax.ShapeDtypeStruct(table.shape, table.dtype),
        compiler_params=grant(),
        cost_estimate=pl.CostEstimate(flops=0, bytes_accessed=8 * 1024 * 1024, transcendentals=0),
        name="stage",
    )(table, *keys, *values, queries)


def join_kernel(ready, first, second, out):
    half = first.shape[0]
    out[:half] = first[...]
    out[half:] = second[...]


def join(ready, first, second):
    whole = pl.BlockSpec(memory_space=pltpu.VMEM)
    return pl.pallas_call(
        join_kernel,
        in_specs=[SCALARS, whole, whole],
        out_specs=whole,
        out_shape=jax.ShapeDtypeStruct((2 * first.shape[0],) + first.shape[1:], first.dtype),
        compiler_params=grant(),
        name="join",
    )(ready, first, second)


def unpack_stats(packed, width, count):
    tail = packed[width:, :].astype(F32)
    highs, totals = [], []
    for head in range(count):
        base = head * 6
        highs.append(tail[base : base + 1] + tail[base + 1 : base + 2] + tail[base + 2 : base + 3])
        totals.append(tail[base + 3 : base + 4] + tail[base + 4 : base + 5] + tail[base + 5 : base + 6])
    return highs, totals


def merge_heads(parts, width, head_width):
    count = width // head_width
    stats = [unpack_stats(part, width, count) for part in parts]
    mixes, highs, totals = [], [], []
    for head in range(count):
        high = functools.reduce(jnp.maximum, [stat[0][head] for stat in stats])
        mixed, total = 0.0, 0.0
        for part, stat in zip(parts, stats):
            factor = jnp.where(stat[1][head] > 0, jnp.exp(stat[0][head] - high), 0.0)
            total = total + stat[1][head] * factor
            mixed = mixed + part[head * head_width : (head + 1) * head_width, :].astype(F32) * factor
        mixes.append(mixed)
        highs.append(high)
        totals.append(total)
    return mixes, highs, totals


def gather_kernel(place, *refs, outer, head_width):
    parts, outs = refs[:-outer], refs[-outer:]
    rows = outs[0].shape[1]
    width = outs[0].shape[0] - STAT_ROWS
    count = width // head_width
    for step, out in enumerate(outs):
        z = lax.bitwise_xor(place[3], step)
        mixes, highs, totals = merge_heads([part[z] for part in parts], width, head_width)
        for head in range(count):
            out[head * head_width : (head + 1) * head_width, :] = mixes[head].astype(BF16)
        out[width:, :] = pack_stats(jnp.concatenate(highs, 1), jnp.concatenate(totals, 1), count, rows)


def merge_lots(place, parts, head_width):
    outer, height, rows = parts[0].shape
    whole = pl.BlockSpec(memory_space=pltpu.VMEM)
    return pl.pallas_call(
        functools.partial(gather_kernel, outer=outer, head_width=head_width),
        in_specs=[SCALARS] + [whole] * len(parts),
        out_specs=[whole] * outer,
        out_shape=[jax.ShapeDtypeStruct((height, rows), BF16)] * outer,
        compiler_params=grant(),
        name="merge_lots",
    )(place, *parts)


def finish_kernel(*refs, head_width):
    *parts, out = refs
    width = out.shape[1]
    mixes, _, totals = merge_heads([part[...] for part in parts], width, head_width)
    done = jnp.concatenate([mixed / total for mixed, total in zip(mixes, totals)], 0)
    out[...] = done.T.astype(BF16)


def finish(parts, head_width):
    whole = pl.BlockSpec(memory_space=pltpu.VMEM)
    return pl.pallas_call(
        functools.partial(finish_kernel, head_width=head_width),
        in_specs=[whole] * len(parts),
        out_specs=whole,
        out_shape=jax.ShapeDtypeStruct((parts[0].shape[1], parts[0].shape[0] - STAT_ROWS), BF16),
        compiler_params=grant(),
        name="finish",
    )(*parts)


def local(
    queries,
    passages,
    noise,
    mix_weight,
    answer_queries,
    key_weight,
    value_weight,
    token_states,
    block_owner,
    listed,
):
    readers = lax.axis_size("pb")
    runners = lax.axis_size("pa")
    group = lax.axis_index("pb")
    runner = lax.axis_index("pa")
    spread = runners // PAIR
    inner = 1
    while (2 * inner) * (2 * inner) <= readers:
        inner *= 2
    outer = readers // inner
    model_width = key_weight.shape[0]
    head_width = model_width // HEADS
    slots, tokens = token_states.shape[:2]
    place = jnp.stack([runner % PAIR, runner // PAIR, group % inner, group // inner]).astype(jnp.int32)

    def swap(value, axis, bits):
        size = lax.axis_size(axis)
        return lax.ppermute(value, axis, [(at, at ^ bits) for at in range(size)])

    states = token_states.reshape(slots * tokens, model_width)
    pair_states = swap(states, "pa", 1)

    wanted = jnp.take(block_owner, listed[0], axis=0)
    wanted = jnp.concatenate([wanted, swap(wanted, "pa", 1)])
    digits = jnp.concatenate([wanted // LANES, wanted % LANES]).astype(F32)
    note = jnp.pad(digits[None], ((0, 0), (NOTE_AT, LANES - NOTE_AT - digits.shape[0])))
    keep, send = retrieve(place, queries, passages, noise, readers, spread)
    *by_column, place_own = merge_pair(place, keep, swap(send, "pa", 1), spread)
    parts = [by_column[0]] + [swap(by_column[at], "pa", at * PAIR) for at in range(1, spread)]
    own_key, own_value, own_done = project(place_own, states, key_weight, value_weight, spread, tokens)
    *by_group, place_pair = merge_columns(place, note, own_done, parts, inner)
    parts = [by_group[0]] + [swap(by_group[at], "pb", at) for at in range(1, inner)]
    pair_key, pair_value, pair_done = project(place_pair, pair_states, key_weight, value_weight, spread, tokens)
    own_part, *by_reader = merge_near(place, pair_done, parts)
    mine = [own_part] + [swap(part, "pb", (at + 1) * inner) for at, part in enumerate(by_reader)]
    keys, values = (own_key, pair_key), (own_value, pair_value)
    kept, sent = condition(place, mine, mix_weight, answer_queries, spread)

    first = queries.shape[1] + NOTE_AT
    digits = jnp.concatenate([part[:inner, first : first + digits.shape[0]] for part in mine]).astype(jnp.int32)
    slot_ids = digits[:, : wanted.shape[0]] * LANES + digits[:, wanted.shape[0] :]
    slot_ids = slot_ids.reshape(readers, PAIR, -1)
    holder = (runner ^ jnp.arange(PAIR, dtype=jnp.int32)) * readers + group
    held = slot_ids // slots == holder[None, :, None]
    inside = slot_ids % slots
    table = jnp.stack(
        [
            jnp.min(jnp.where(held, inside, slots - 1), 2),
            jnp.max(jnp.where(held, inside, 0), 2),
            jnp.any(held, 2).astype(jnp.int32),
        ],
        2,
    ).reshape(-1)

    pieces = jnp.stack([kept, swap(sent, "pa", 1)])[None]
    step = inner
    while 2 * step < readers:
        pieces = jnp.concatenate([pieces, swap(pieces, "pb", step)], 0)
        step *= 2
    ready = stage(table, keys, values, pieces)
    pieces = join(ready, pieces, swap(pieces, "pb", step))
    near = [pieces] + [swap(pieces, "pa", at * PAIR) for at in range(1, spread)]
    far = [near]
    for offset in range(1, inner):
        far.append([swap(piece, "pb", offset) for piece in near])
    lots = []
    for offset, column in [(o, c) for o in range(inner) for c in range(spread)][1:] + [(0, 0)]:
        lot = attend(place, ready, far[offset], keys, values, offset, column, inner, head_width)
        bits = column * PAIR * readers + offset
        if bits:
            lot = lax.ppermute(lot, ("pa", "pb"), [(at, at ^ bits) for at in range(runners * readers)])
        lots.append(lot)
    kept, *away = merge_lots(place, lots, head_width)
    back = [swap(part, "pb", (step + 1) * inner) for step, part in enumerate(away)]
    return finish([kept] + back, head_width)


def solution(mesh):
    return jax.shard_map(
        local,
        mesh=mesh,
        in_specs=(
            P(),
            P(("pa", "pb"), None),
            P(None, ("pa", "pb")),
            P(),
            P("pb", None),
            P(),
            P(),
            P(("pa", "pb"), None, None),
            P(),
            P("pb", "pa"),
        ),
        out_specs=P("pb", "pa"),
        check_vma=False,
    )
```

```python
import functools

import jax
import jax.numpy as jnp
from jax import lax
from jax.experimental import pallas as pl
from jax.experimental.pallas import tpu as pltpu
from jax.sharding import PartitionSpec as P

HEADS = 16
PAIR = 2
CAP = 2
TEMPER = 0.5
FLOOR = -1e30
LANES = 128
STAT_ROWS = 32
NOTE_AT = 6
STEP_GROUPS = 2
PROJECT_STEPS = 4
HINT = 16
HEAD_BUNDLE = 2
VMEM_BYTES = 16 * 1024 * 1024
WIDE_BYTES = 62 * 1024 * 1024
F32 = jnp.float32
BF16 = jnp.bfloat16
NT = (((1,), (1,)), ((), ()))
SCALARS = pl.BlockSpec(memory_space=pltpu.SMEM)
UNREAD = pl.BlockSpec(memory_space=pl.ANY)


def grant():
    return pltpu.CompilerParams(vmem_limit_bytes=VMEM_BYTES)


def thirds(value):
    first = value.astype(BF16).astype(F32)
    rest = value - first
    second = rest.astype(BF16).astype(F32)
    return first, second, rest - second


def pack_tail(shift, total):
    lane = lax.broadcasted_iota(jnp.int32, (shift.shape[0], LANES), 1)
    tail = jnp.zeros((shift.shape[0], LANES), F32)
    for at, term in enumerate(thirds(shift) + thirds(total)):
        tail = jnp.where(lane == at, term, tail)
    return tail


def unpack_tail(tail):
    term = lax.broadcasted_iota(jnp.int32, (LANES, 2 * LANES), 0)
    half = lax.broadcasted_iota(jnp.int32, (LANES, 2 * LANES), 1) // LANES
    pick = jnp.where(term // 3 == half, 1.0, 0.0).astype(BF16)
    both = jnp.dot(tail, pick, preferred_element_type=F32)
    return both[:, :LANES], both[:, LANES:]


def merge_rows(parts):
    width = parts[0].shape[1] - LANES
    stats = [unpack_tail(part[:, width:]) for part in parts]
    shift = functools.reduce(jnp.maximum, [stat[0] for stat in stats])
    factors = [jnp.exp(stat[0] - shift) for stat in stats]
    total = sum(stat[1] * factor for stat, factor in zip(stats, factors))
    tiles = [
        sum(part[:, at : at + LANES].astype(F32) * factor for part, factor in zip(parts, factors))
        for at in range(0, width, LANES)
    ]
    return tiles, shift, total


def flat(value):
    return value.reshape((-1, value.shape[-1]))


def retrieval_kernel(place, queries, passages, noise, keep, send, rows_scratch, *, spread):
    core = place[0]
    groups, part = keep.shape[1:3]
    width = queries.shape[1]
    logits = lax.dot_general(queries[...], passages[...], NT, preferred_element_type=F32)
    gumbel = -jnp.log(-jnp.log(noise[...].astype(F32)))
    scores = (logits * width ** (-0.5) + gumbel) * (1 / TEMPER)
    shift = jnp.max(scores, 1, keepdims=True)
    weight = jnp.exp(scores - shift)
    total = jnp.sum(weight, 1, keepdims=True)
    rows_scratch[:, :width] = jnp.dot(weight.astype(BF16), passages[...], preferred_element_type=F32)
    rows_scratch[:, width:] = pack_tail(shift, total)
    for at in range(groups):
        for column in range(spread):
            base = (at * spread + column) * PAIR
            mine = pl.multiple_of((base + core) * part, part)
            other = pl.multiple_of((base + 1 - core) * part, part)
            keep[column, at] = rows_scratch[pl.ds(mine, part), :].astype(BF16)
            send[column, at] = rows_scratch[pl.ds(other, part), :].astype(BF16)


def retrieve(place, queries, passages, noise, readers, spread):
    count, width = queries.shape
    group = count // readers
    part = group // (PAIR * spread)
    shape = jax.ShapeDtypeStruct((spread, readers, part, width + LANES), BF16)
    spec = pl.BlockSpec((spread, STEP_GROUPS, part, width + LANES), lambda g, place: (0, g, 0, 0))
    rows = group * STEP_GROUPS
    return pl.pallas_call(
        functools.partial(retrieval_kernel, spread=spread),
        grid_spec=pltpu.PrefetchScalarGridSpec(
            num_scalar_prefetch=1,
            grid=(readers // STEP_GROUPS,),
            in_specs=[
                pl.BlockSpec((rows, width), lambda g, place: (g, 0)),
                pl.BlockSpec(passages.shape, lambda g, place: (0, 0)),
                pl.BlockSpec((rows, noise.shape[1]), lambda g, place: (g, 0)),
            ],
            out_specs=[spec, spec],
            scratch_shapes=[pltpu.VMEM((rows, width + LANES), F32)],
        ),
        out_shape=[shape, shape],
        compiler_params=pltpu.CompilerParams(vmem_limit_bytes=WIDE_BYTES),
        cost_estimate=pl.CostEstimate(
            flops=4 * count * width * passages.shape[0],
            bytes_accessed=2 * (2 * count * width + passages.size + noise.size),
            transcendentals=3 * noise.size,
        ),
        name="retrieve",
    )(place, queries, passages, noise)


def store_rows(out, tiles, shift, total, note=None):
    for at, tile in enumerate(tiles):
        out[..., at * LANES : (at + 1) * LANES] = tile.astype(BF16).reshape(out.shape[:-1] + (LANES,))
    tail = pack_tail(shift, total)
    if note is not None:
        tail = tail + note
    out[..., len(tiles) * LANES :] = tail.astype(BF16).reshape(out.shape[:-1] + (LANES,))


def hand_on(place, out):
    for at in range(out.shape[0]):
        out[at] = place[at]


def pair_kernel(place, keep, recv, *outs):
    for offset, out in enumerate(outs):
        column = lax.bitwise_xor(place[1], offset)
        store_rows(out, *merge_rows([flat(keep[column]), flat(recv[column])]))


def merge_pair(place, keep, recv, spread):
    readers = keep.shape[1]
    spec = pl.BlockSpec((spread, readers // 2) + keep.shape[2:], lambda g, place: (0, g, 0, 0))
    out = pl.BlockSpec((readers // 2,) + keep.shape[2:], lambda g, place: (g, 0, 0))
    return pl.pallas_call(
        pair_kernel,
        grid_spec=pltpu.PrefetchScalarGridSpec(
            num_scalar_prefetch=1, grid=(2,), in_specs=[spec, spec], out_specs=[out] * spread
        ),
        out_shape=[jax.ShapeDtypeStruct(keep.shape[1:], BF16)] * spread,
        compiler_params=grant(),
        name="merge_pair",
    )(place, keep, recv)


def column_kernel(place, note, done, *refs, inner):
    parts, outs = refs[:-inner], refs[-inner:]
    row = lax.broadcasted_iota(jnp.int32, (outs[0].shape[1], LANES), 0)
    first = jnp.where(row == 0, note[...], 0.0)
    for offset, out in enumerate(outs):
        for z in range(out.shape[0]):
            at = z * inner + lax.bitwise_xor(place[2], offset)
            store_rows(out.at[z], *merge_rows([part[at] for part in parts]), first)


def merge_columns(place, note, done, parts, inner):
    readers, part, width = parts[0].shape
    whole = pl.BlockSpec(memory_space=pltpu.VMEM)
    return pl.pallas_call(
        functools.partial(column_kernel, inner=inner),
        in_specs=[SCALARS, whole, UNREAD] + [whole] * len(parts),
        out_specs=[whole] * inner,
        out_shape=[jax.ShapeDtypeStruct((readers // inner, part, width), BF16)] * inner,
        compiler_params=grant(),
        name="merge_columns",
    )(place, note, done, *parts)


def near_kernel(place, done, *refs, outer):
    parts, outs = refs[:-outer], refs[-outer:]
    shape = (outs[0].shape[0], LANES)
    row, lane = (lax.broadcasted_iota(jnp.int32, shape, at) for at in range(2))
    for step, out in enumerate(outs):
        taken = [part[lax.bitwise_xor(place[3], step)] for part in parts]
        notes = jnp.zeros(shape, F32)
        for offset, part in enumerate(taken):
            carried = part[0:1, part.shape[1] - LANES :].astype(F32)
            notes = jnp.where((row == offset) & (lane >= NOTE_AT), carried, notes)
        store_rows(out, *merge_rows(taken), notes)


def merge_near(place, done, parts):
    outer, part, width = parts[0].shape
    whole = pl.BlockSpec(memory_space=pltpu.VMEM)
    return pl.pallas_call(
        functools.partial(near_kernel, outer=outer),
        in_specs=[SCALARS, UNREAD] + [whole] * len(parts),
        out_specs=[whole] * outer,
        out_shape=[jax.ShapeDtypeStruct((part, width), BF16)] * outer,
        compiler_params=grant(),
        name="merge_near",
    )(place, done, *parts)


def condition_kernel(place, mix_weight, answers, *refs, spread):
    *parts, keep, send, rows_scratch = refs
    tiles, _, total = merge_rows([part[...] for part in parts])
    blended_half = jnp.concatenate([(tile / total).astype(BF16) for tile in tiles], 1)
    part = blended_half.shape[0]
    start = pl.multiple_of((place[1] * PAIR + place[0]) * part, part)
    answer = answers[pl.ds(start, part), :].astype(F32)
    rows_scratch[...] = answer + jnp.dot(blended_half, mix_weight[...], preferred_element_type=F32)
    stride = keep.shape[1] // spread
    for column in range(spread):
        mine = pl.multiple_of((column * PAIR + place[0]) * stride, stride)
        other = pl.multiple_of((column * PAIR + 1 - place[0]) * stride, stride)
        keep[:, column * stride : (column + 1) * stride] = rows_scratch[:, pl.ds(mine, stride)].astype(BF16)
        send[:, column * stride : (column + 1) * stride] = rows_scratch[:, pl.ds(other, stride)].astype(BF16)


def condition(place, parts, mix_weight, answers, spread):
    model_width = mix_weight.shape[1]
    shape = jax.ShapeDtypeStruct((parts[0].shape[0], model_width // PAIR), BF16)
    whole = pl.BlockSpec(memory_space=pltpu.VMEM)
    return pl.pallas_call(
        functools.partial(condition_kernel, spread=spread),
        in_specs=[SCALARS] + [whole] * (2 + len(parts)),
        out_specs=[whole, whole],
        out_shape=[shape, shape],
        scratch_shapes=[pltpu.VMEM((parts[0].shape[0], model_width), F32)],
        compiler_params=grant(),
        name="condition",
    )(place, mix_weight, answers, *parts)


def project_kernel(place, states, *refs):
    spread = (len(refs) - 4) // 2
    keys, values, done = refs[-3:]
    done[...] = jnp.zeros_like(done)
    tokens = values.shape[3]
    for column in range(spread):
        keys[column] = jnp.dot(states[...], refs[column][...], preferred_element_type=F32).astype(BF16)
        value = jnp.dot(states[...], refs[spread + column][...], preferred_element_type=F32).astype(BF16)
        for block in range(values.shape[1]):
            values[column, block] = value[block * tokens : (block + 1) * tokens].T


def project(place, states, key_weight, value_weight, after, spread, tokens):
    rows, model_width = states.shape
    width = model_width // (PAIR * spread)
    chunk = rows // PROJECT_STEPS
    blocks = chunk // tokens

    def weight_spec(column):
        return pl.BlockSpec((model_width, width), lambda t, place: (0, column * PAIR + place[0]))

    specs = [weight_spec(column) for column in range(spread)]
    return pl.pallas_call(
        project_kernel,
        grid_spec=pltpu.PrefetchScalarGridSpec(
            num_scalar_prefetch=1,
            grid=(PROJECT_STEPS,),
            in_specs=[pl.BlockSpec((chunk, model_width), lambda t, place: (t, 0))] + specs + specs + [UNREAD],
            out_specs=[
                pl.BlockSpec((spread, chunk, width), lambda t, place: (0, t, 0)),
                pl.BlockSpec((spread, blocks, width, tokens), lambda t, place: (0, t, 0, 0)),
                pl.BlockSpec((8, LANES), lambda t, place: (0, 0)),
            ],
        ),
        out_shape=[
            jax.ShapeDtypeStruct((spread, rows, width), BF16),
            jax.ShapeDtypeStruct((spread, rows // tokens, width, tokens), BF16),
            jax.ShapeDtypeStruct((8, LANES), F32),
        ],
        compiler_params=pltpu.CompilerParams(vmem_limit_bytes=WIDE_BYTES),
        cost_estimate=pl.CostEstimate(
            flops=4 * rows * model_width * spread * width // HINT,
            bytes_accessed=2 * (2 * model_width * spread * width + 2 * rows * model_width) // HINT,
            transcendentals=0,
        ),
        name="project",
    )(place, states, *([key_weight] * spread), *([value_weight] * spread), after)


def attend_group(z, place, table, pieces, keys, values, out, rows_scratch, offset, column, inner, head_width):
    relative = lax.bitwise_xor(z, place[3])
    part, rows = pieces[0].shape[2], out.shape[2]
    width = out.shape[1] - STAT_ROWS
    count = width // head_width
    side = lax.bitwise_xor(place[1], column)
    left = pl.multiple_of(side * width, width)
    for step, piece in enumerate(pieces):
        for core in range(PAIR):
            top = lax.bitwise_xor(place[1], step) * PAIR + lax.bitwise_xor(place[0], core)
            top = pl.multiple_of(top * part, part)
            rows_scratch[z, pl.ds(top, part), :] = piece[relative, core, :, pl.ds(left, width)]
    query = rows_scratch[z].T
    tokens = values[0].shape[3]
    head_at = lax.broadcasted_iota(jnp.int32, query.shape, 0) // head_width
    spaced = jnp.concatenate([jnp.where(head_at == head, query, jnp.zeros_like(query)) for head in range(count)], 1)
    entry = relative * inner + offset
    bundle = min(HEAD_BUNDLE, count)
    shelves = []
    for shelf in range(PAIR):
        chosen = [table[entry * 6 + shelf * 3 + at] for at in range(CAP)]
        scores = [
            jnp.dot(
                keys[shelf][side, pl.ds(pl.multiple_of(slot * tokens, tokens), tokens), :],
                spaced,
                preferred_element_type=F32,
            )
            for slot in chosen
        ]
        high = functools.reduce(jnp.maximum, [jnp.max(score, 0, keepdims=True) for score in scores])
        exponents = [jnp.exp(score - high) for score in scores]
        total = sum(jnp.sum(exponent, 0, keepdims=True) for exponent in exponents)
        probs = jnp.concatenate([exponent.astype(BF16) for exponent in exponents], 0)
        there = table[entry * 6 + shelf * 3 + 2] > 0
        blocks = []
        for first in range(0, count, bundle):
            here = slice(first * head_width, (first + bundle) * head_width)
            value = jnp.concatenate([values[shelf][side, slot, here, :] for slot in chosen], 1)
            mixed = jnp.dot(value, probs[:, first * rows : (first + bundle) * rows], preferred_element_type=F32)
            for head in range(bundle):
                blocks.append(
                    mixed[head * head_width : (head + 1) * head_width, head * rows : (head + 1) * rows]
                )
        shelves.append((jnp.where(there, high, FLOOR), jnp.where(there, total, 0.0), blocks, there))
    high = functools.reduce(jnp.maximum, [shelf[0] for shelf in shelves])
    factors = [jnp.where(there, jnp.exp(shelf_high - high), 0.0) for shelf_high, _, _, there in shelves]
    total = sum(shelf[1] * factor for shelf, factor in zip(shelves, factors))
    for head in range(count):
        here = slice(head * rows, (head + 1) * rows)
        joined = sum(shelf[2][head] * factor[:, here] for shelf, factor in zip(shelves, factors))
        out[z, head * head_width : (head + 1) * head_width, :] = joined.astype(BF16)
    out[z, width:, :] = pack_stats(high, total, count, rows)


def attend_kernel(place, table, key_own, key_pair, value_own, value_pair, *refs, **fixed):
    *pieces, out, rows_scratch = refs
    for z in range(out.shape[0]):
        keys, values = (key_own, key_pair), (value_own, value_pair)
        attend_group(z, place, table, pieces, keys, values, out, rows_scratch, **fixed)


def pack_stats(high, total, count, rows):
    places = lax.broadcasted_iota(jnp.int32, (STAT_ROWS, rows), 0)
    packed = jnp.zeros((STAT_ROWS, rows), F32)
    for head in range(count):
        here = slice(head * rows, (head + 1) * rows)
        for at, term in enumerate(thirds(high[:, here]) + thirds(total[:, here])):
            packed = jnp.where(places == head * 6 + at, term, packed)
    return packed.astype(BF16)


def attend(place, table, pieces, keys, values, offset, column, inner, head_width):
    outer, pair, part, half = pieces[0].shape
    width = half // len(pieces)
    rows = len(pieces) * pair * part
    tokens = values[0].shape[3]
    whole = pl.BlockSpec(memory_space=pltpu.VMEM)
    return pl.pallas_call(
        functools.partial(attend_kernel, offset=offset, column=column, inner=inner, head_width=head_width),
        in_specs=[SCALARS, SCALARS] + [whole] * (4 + len(pieces)),
        out_specs=whole,
        scratch_shapes=[pltpu.VMEM((outer, rows, width), BF16)],
        out_shape=jax.ShapeDtypeStruct((outer, width + STAT_ROWS, rows), BF16),
        compiler_params=grant(),
        cost_estimate=pl.CostEstimate(
            flops=outer * 4 * 4 * rows * tokens * width * (width // head_width),
            bytes_accessed=outer * 2 * (width + STAT_ROWS) * rows,
            transcendentals=outer * 4 * rows * tokens * (width // head_width),
        ),
        name="attend",
    )(place, table, *keys, *values, *pieces)


def stage_kernel(table, key_own, key_pair, value_own, value_pair, queries, out):
    hand_on(table, out)


def stage(table, keys, values, queries):
    whole = pl.BlockSpec(memory_space=pltpu.VMEM)
    return pl.pallas_call(
        stage_kernel,
        in_specs=[SCALARS] + [whole] * 4 + [pl.BlockSpec(memory_space=pl.ANY)],
        out_specs=SCALARS,
        out_shape=jax.ShapeDtypeStruct(table.shape, table.dtype),
        compiler_params=grant(),
        cost_estimate=pl.CostEstimate(flops=0, bytes_accessed=8 * 1024 * 1024, transcendentals=0),
        name="stage",
    )(table, *keys, *values, queries)


def join_kernel(ready, first, second, out):
    half = first.shape[0]
    out[:half] = first[...]
    out[half:] = second[...]


def join(ready, first, second):
    whole = pl.BlockSpec(memory_space=pltpu.VMEM)
    return pl.pallas_call(
        join_kernel,
        in_specs=[SCALARS, whole, whole],
        out_specs=whole,
        out_shape=jax.ShapeDtypeStruct((2 * first.shape[0],) + first.shape[1:], first.dtype),
        compiler_params=grant(),
        name="join",
    )(ready, first, second)


def unpack_stats(packed, width, count):
    tail = packed[width:, :].astype(F32)
    highs, totals = [], []
    for head in range(count):
        base = head * 6
        highs.append(tail[base : base + 1] + tail[base + 1 : base + 2] + tail[base + 2 : base + 3])
        totals.append(tail[base + 3 : base + 4] + tail[base + 4 : base + 5] + tail[base + 5 : base + 6])
    return highs, totals


def merge_heads(parts, width, head_width):
    count = width // head_width
    stats = [unpack_stats(part, width, count) for part in parts]
    mixes, highs, totals = [], [], []
    for head in range(count):
        high = functools.reduce(jnp.maximum, [stat[0][head] for stat in stats])
        mixed, total = 0.0, 0.0
        for part, stat in zip(parts, stats):
            factor = jnp.where(stat[1][head] > 0, jnp.exp(stat[0][head] - high), 0.0)
            total = total + stat[1][head] * factor
            mixed = mixed + part[head * head_width : (head + 1) * head_width, :].astype(F32) * factor
        mixes.append(mixed)
        highs.append(high)
        totals.append(total)
    return mixes, highs, totals


def gather_kernel(place, *refs, outer, head_width):
    parts, outs = refs[:-outer], refs[-outer:]
    rows = outs[0].shape[1]
    width = outs[0].shape[0] - STAT_ROWS
    count = width // head_width
    for step, out in enumerate(outs):
        z = lax.bitwise_xor(place[3], step)
        mixes, highs, totals = merge_heads([part[z] for part in parts], width, head_width)
        for head in range(count):
            out[head * head_width : (head + 1) * head_width, :] = mixes[head].astype(BF16)
        out[width:, :] = pack_stats(jnp.concatenate(highs, 1), jnp.concatenate(totals, 1), count, rows)


def merge_lots(place, parts, head_width):
    outer, height, rows = parts[0].shape
    whole = pl.BlockSpec(memory_space=pltpu.VMEM)
    return pl.pallas_call(
        functools.partial(gather_kernel, outer=outer, head_width=head_width),
        in_specs=[SCALARS] + [whole] * len(parts),
        out_specs=[whole] * outer,
        out_shape=[jax.ShapeDtypeStruct((height, rows), BF16)] * outer,
        compiler_params=grant(),
        name="merge_lots",
    )(place, *parts)


def finish_kernel(*refs, head_width):
    *parts, out = refs
    width = out.shape[1]
    mixes, _, totals = merge_heads([part[...] for part in parts], width, head_width)
    done = jnp.concatenate([mixed / total for mixed, total in zip(mixes, totals)], 0)
    out[...] = done.T.astype(BF16)


def finish(parts, head_width):
    whole = pl.BlockSpec(memory_space=pltpu.VMEM)
    return pl.pallas_call(
        functools.partial(finish_kernel, head_width=head_width),
        in_specs=[whole] * len(parts),
        out_specs=whole,
        out_shape=jax.ShapeDtypeStruct((parts[0].shape[1], parts[0].shape[0] - STAT_ROWS), BF16),
        compiler_params=grant(),
        name="finish",
    )(*parts)


def local(
    queries,
    passages,
    noise,
    mix_weight,
    answer_queries,
    key_weight,
    value_weight,
    token_states,
    block_owner,
    listed,
):
    readers = lax.axis_size("pb")
    runners = lax.axis_size("pa")
    group = lax.axis_index("pb")
    runner = lax.axis_index("pa")
    spread = runners // PAIR
    inner = 1
    while (2 * inner) * (2 * inner) <= readers:
        inner *= 2
    outer = readers // inner
    model_width = key_weight.shape[0]
    head_width = model_width // HEADS
    slots, tokens = token_states.shape[:2]
    place = jnp.stack([runner % PAIR, runner // PAIR, group % inner, group // inner]).astype(jnp.int32)

    def swap(value, axis, bits):
        size = lax.axis_size(axis)
        return lax.ppermute(value, axis, [(at, at ^ bits) for at in range(size)])

    states = token_states.reshape(slots * tokens, model_width)
    pair_states = swap(states, "pa", 1)

    wanted = jnp.take(block_owner, listed[0], axis=0)
    wanted = jnp.concatenate([wanted, swap(wanted, "pa", 1)])
    digits = jnp.concatenate([wanted // LANES, wanted % LANES]).astype(F32)
    note = jnp.pad(digits[None], ((0, 0), (NOTE_AT, LANES - NOTE_AT - digits.shape[0])))
    keep, send = retrieve(place, queries, passages, noise, readers, spread)
    by_column = merge_pair(place, keep, swap(send, "pa", 1), spread)
    parts = [by_column[0]] + [swap(by_column[at], "pa", at * PAIR) for at in range(1, spread)]
    own_key, own_value, own_done = project(place, states, key_weight, value_weight, by_column[0], spread, tokens)
    by_group = merge_columns(place, note, own_done, parts, inner)
    parts = [by_group[0]] + [swap(by_group[at], "pb", at) for at in range(1, inner)]
    pair_key, pair_value, pair_done = project(
        place, pair_states, key_weight, value_weight, by_group[0], spread, tokens
    )
    own_part, *by_reader = merge_near(place, pair_done, parts)
    mine = [own_part] + [swap(part, "pb", (at + 1) * inner) for at, part in enumerate(by_reader)]
    keys, values = (own_key, pair_key), (own_value, pair_value)
    kept, sent = condition(place, mine, mix_weight, answer_queries, spread)

    first = queries.shape[1] + NOTE_AT
    digits = jnp.concatenate([part[:inner, first : first + digits.shape[0]] for part in mine]).astype(jnp.int32)
    slot_ids = digits[:, : wanted.shape[0]] * LANES + digits[:, wanted.shape[0] :]
    slot_ids = slot_ids.reshape(readers, PAIR, -1)
    holder = (runner ^ jnp.arange(PAIR, dtype=jnp.int32)) * readers + group
    held = slot_ids // slots == holder[None, :, None]
    inside = slot_ids % slots
    table = jnp.stack(
        [
            jnp.min(jnp.where(held, inside, slots - 1), 2),
            jnp.max(jnp.where(held, inside, 0), 2),
            jnp.any(held, 2).astype(jnp.int32),
        ],
        2,
    ).reshape(-1)

    pieces = jnp.stack([kept, swap(sent, "pa", 1)])[None]
    step = inner
    while 2 * step < readers:
        pieces = jnp.concatenate([pieces, swap(pieces, "pb", step)], 0)
        step *= 2
    ready = stage(table, keys, values, pieces)
    pieces = join(ready, pieces, swap(pieces, "pb", step))
    near = [pieces] + [swap(pieces, "pa", at * PAIR) for at in range(1, spread)]
    far = [near]
    for offset in range(1, inner):
        far.append([swap(piece, "pb", offset) for piece in near])
    lots = []
    for offset, column in [(o, c) for o in range(inner) for c in range(spread)][1:] + [(0, 0)]:
        lot = attend(place, ready, far[offset], keys, values, offset, column, inner, head_width)
        bits = column * PAIR * readers + offset
        if bits:
            lot = lax.ppermute(lot, ("pa", "pb"), [(at, at ^ bits) for at in range(runners * readers)])
        lots.append(lot)
    kept, *away = merge_lots(place, lots, head_width)
    back = [swap(part, "pb", (step + 1) * inner) for step, part in enumerate(away)]
    return finish([kept] + back, head_width)


def solution(mesh):
    return jax.shard_map(
        local,
        mesh=mesh,
        in_specs=(
            P(),
            P(("pa", "pb"), None),
            P(None, ("pa", "pb")),
            P(),
            P("pb", None),
            P(),
            P(),
            P(("pa", "pb"), None, None),
            P(),
            P("pb", "pa"),
        ),
        out_specs=P("pb", "pa"),
        check_vma=False,
    )
```
